32 devices in a mesh: ctx: 8 (over y, x, core), pair: 4 (over z).
Axes of the slice: x: 2, y: 2, z: 4, core: 2. Of those that a mesh axis runs over, the one named last changes fastest.
Arguments:
- prompt_x: bfloat16 [2, 2048, 16384], P(None, 'ctx', 'pair'), may hold values from -6 to 6
- prompt_bc: bfloat16 [2, 2, 16, 2048], P(None, None, None, 'ctx'), may hold values from -3 to 3
- prompt_logdec: float32 [2, 256, 2048], P(None, 'pair', 'ctx'), may hold values from -2.5 to 0, as said below
- branch_x: bfloat16 [8, 512, 16384], P('pair', None, 'ctx'), may hold values from -6 to 6
- branch_bc: bfloat16 [2, 8, 16, 512], P(None, 'pair'), may hold values from -3 to 3
- branch_logdec: float32 [8, 256, 512], P('pair', 'ctx'), may hold values from -2.5 to 0, as said below
- branch_prompt: int32 [4], P('pair'), may hold values from 0 to 1
- branch_len: int32 [8], P('pair'), may hold values from 128 to 512, as said below
Outputs:
- prompt_y: bfloat16 [2, 2048, 16384], P(None, 'ctx', 'pair')
- branch_y: bfloat16 [8, 512, 16384], P('pair', None, 'ctx')
The draws below stay inside these ranges and needn't reach their ends.
Inputs may be any that keep to these rules, and one draw needn't show every extreme that they name: `prompt_logdec`: the logarithm of a position's decay for each head. `branch_logdec`: the logarithm of a position's decay for each head. `branch_len`: positions of a branch at or after its length are masked; some branch has all 512 positions live.
All inputs are finite; a program needn't handle non-finite values.
Results may differ from the reference program's by a relative error of at most 0.0049.
Values sent between devices are 32-bit elements; how exact they have to be, the bound alone decides.
No kernel may reach another device: no remote copies, remote signals or barrier semaphores. Data moves between devices by JAX's collectives and lax.ppermute only.
A program may use at most 128 MiB of HBM per device.

```python
import math
import jax
import jax.numpy as jnp
from jax import lax

H = 256
P_SIZE = 64
N = 16
W = 16384
NPROMPT = 2
TP_DEV = 256
LB = 512
LP = 2048
NPAIR = 4
BR = 8
BLOCK = 256


def head_rates(key):
    key_kind, key_slow, key_fast = jax.random.split(jax.random.fold_in(key, 4242), 3)
    chain_len = LP + LB
    slow_share = 0.5
    coin = jax.random.uniform(key_kind, (H,))
    slow_rate = jnp.exp(jax.random.uniform(key_slow, (H,), minval=math.log(0.05 / chain_len), maxval=math.log(0.8 / chain_len)))
    fast_rate = jnp.exp(jax.random.uniform(key_fast, (H,), minval=math.log(1.0 / 400.0), maxval=math.log(1.0 / 8.0)))
    return jnp.where(coin < slow_share, slow_rate, fast_rate)


def decay_rule(key, label_marker, count_of_rows, sequence_length, section_piece, spike_amounts):
    head_decay_speed = head_rates(key)
    key_jit, key_seg, key_position_draw, key_split_point = jax.random.split(jax.random.fold_in(key, label_marker), 4)
    small_noise = jnp.exp(jax.random.uniform(key_jit, (count_of_rows, H, sequence_length), minval=math.log(0.5), maxval=math.log(2.0)))
    multiplier = jnp.exp(jax.random.uniform(key_seg, (count_of_rows, H, sequence_length // section_piece), minval=math.log(0.5), maxval=math.log(2.0)))
    multiplier = jnp.repeat(multiplier, section_piece, axis=2, total_repeat_length=sequence_length)
    token_positions = jax.random.randint(key_position_draw, (count_of_rows, spike_amounts), 0, sequence_length)
    split_points = jnp.log(jax.random.uniform(key_split_point, (count_of_rows, spike_amounts), minval=0.5, maxval=0.8))
    spots_list = jnp.arange(sequence_length, dtype=jnp.int32)
    spike_amount = jnp.sum(jnp.where(spots_list[None, None, :] == token_positions[:, :, None], split_points[:, :, None], 0.0), axis=1)
    return -(head_decay_speed[None, :, None] * small_noise * multiplier) + spike_amount[:, None, :]


def draw_prompt_logdec(key, part):
    return decay_rule(key, 17, NPROMPT, LP, TP_DEV, 2).astype(jnp.float32)


def draw_branch_logdec(key, part):
    return decay_rule(key, 23, BR, LB, LB, 1).astype(jnp.float32)


def draw_branch_len(key, part):
    key_len, key_perm = jax.random.split(jax.random.fold_in(key, 31), 2)
    values = jax.random.randint(key_len, (BR,), LB // 4, LB + 1)
    order = jax.random.permutation(key_perm, BR)
    values = values.at[order[0]].set(LB)
    values = values.at[order[1]].set(LB // 4)
    return values.astype(jnp.int32)


def touch_ends(array, own_key, least, largest):
    extent = array.shape
    place = [jax.random.randint(jax.random.fold_in(own_key, axis), (), 0, extent[axis]) for axis in range(len(extent))]
    array = array.at[tuple(place)].set(least)
    longest = extent.index(max(extent))
    place[longest] = (place[longest] + 1) % extent[longest]
    return array.at[tuple(place)].set(largest)


def level_of(stream_key, extent, cuts, smallest, largest):
    gain = 1.0
    for dim, blocks in cuts:
        draws = jax.random.uniform(jax.random.fold_in(jax.random.fold_in(stream_key, 6), dim), (blocks,), jnp.float32, smallest / len(cuts), largest / len(cuts))
        gain = gain * jnp.repeat(jnp.exp(draws), extent[dim] // blocks).reshape((-1,) + (1,) * (len(extent) - 1 - dim))
    return gain


def noise(key, shape, width, limit, cuts=(), kind=jnp.bfloat16):
    level = level_of(key, shape, cuts, -0.22, 0.18) if cuts else 1.0
    values = jax.random.normal(key, shape, jnp.float32) * width * level
    return jnp.minimum(jnp.maximum(values, -limit), limit).astype(kind)


def setup_inputs(seed: int = 0) -> dict:
    keys = jax.random.split(jax.random.key(seed), 9)
    return {
        "prompt_x": noise(keys[0], (NPROMPT, LP, W), 1.0, 6.0, ((1, 8), (2, 4))),
        "prompt_bc": noise(keys[1], (2, NPROMPT, N, LP), 0.5, 3.0, ((3, 8),)),
        "prompt_logdec": draw_prompt_logdec(jax.random.fold_in(keys[8], 71), 0),
        "branch_x": noise(keys[3], (BR, LB, W), 1.0, 6.0, ((0, 4), (2, 8))),
        "branch_bc": noise(keys[4], (2, BR, N, LB), 0.5, 3.0, ((1, 4),)),
        "branch_logdec": draw_branch_logdec(jax.random.fold_in(keys[8], 71), 0),
        "branch_prompt": touch_ends(jax.random.randint(keys[6], (NPAIR,), 0, NPROMPT), jax.random.fold_in(keys[6], 1), 0, NPROMPT - 1).astype(jnp.int32),
        "branch_len": draw_branch_len(jax.random.fold_in(keys[8], 71), 0),
    }


def block_pass(inputs, log_decay, b_rows, c_rows, start_state):
    block_rows, channels = inputs.shape
    head_count = log_decay.shape[0]
    head_width = channels // head_count
    running = jnp.cumsum(log_decay, axis=1)
    in_gain = jnp.sqrt(-jnp.expm1(2.0 * log_decay))
    scores = jnp.dot(c_rows.T, b_rows, preferred_element_type=jnp.float32)
    row_ids = lax.broadcasted_iota(jnp.int32, (block_rows, block_rows), 0)
    col_ids = lax.broadcasted_iota(jnp.int32, (block_rows, block_rows), 1)
    causal = col_ids <= row_ids
    to_end = jnp.exp(running[:, -1:] - running) * in_gain
    inject = (b_rows.astype(jnp.float32)[None, :, :] * to_end[:, None, :]).astype(jnp.bfloat16)

    def head_pass(head_id):
        running_h = running[head_id]
        columns = lax.dynamic_slice_in_dim(inputs, head_id * head_width, head_width, 1)
        differ = jnp.where(causal, running_h[:, None] - running_h[None, :], 0.0)
        weights = jnp.where(causal, jnp.exp(differ), 0.0)
        weights = (scores * weights * in_gain[head_id][None, :]).astype(jnp.bfloat16)
        inner_out = jnp.dot(weights, columns, preferred_element_type=jnp.float32)
        states = jnp.dot(inject[head_id], columns, preferred_element_type=jnp.float32)
        return (inner_out, states)
    inner_out, states = lax.map(head_pass, jnp.arange(head_count, dtype=jnp.int32))
    inner_out = jnp.transpose(inner_out, (1, 0, 2)).reshape(block_rows, channels)
    projected = jnp.einsum('nt,hnp->thp', c_rows.astype(jnp.float32), start_state, precision=lax.Precision.HIGHEST)
    carried = (projected * jnp.exp(running).T[:, :, None]).reshape(block_rows, channels)
    end_state = jnp.exp(running[:, -1])[:, None, None] * start_state + states
    return (inner_out + carried, end_state)

def run_blocks(inputs, log_decay, b_and_c, start_state):
    sequence_length, channels = inputs.shape
    head_count = log_decay.shape[0]
    state_size = b_and_c.shape[1]
    block_count = sequence_length // BLOCK
    input_blocks = inputs.reshape(block_count, BLOCK, channels)
    decay_blocks = jnp.transpose(log_decay.reshape(head_count, block_count, BLOCK), (1, 0, 2))
    proj_blocks = jnp.transpose(b_and_c.reshape(2, state_size, block_count, BLOCK), (2, 0, 1, 3))

    def advance(carry_state, pieces):
        block_in, block_decay, block_proj = pieces
        block_out, end_state = block_pass(block_in, block_decay, block_proj[0], block_proj[1], carry_state)
        return (end_state, block_out.astype(jnp.bfloat16))
    end_state, outputs = lax.scan(advance, start_state, (input_blocks, decay_blocks, proj_blocks))
    return (outputs.reshape(sequence_length, channels), end_state)

def reference(prompt_x, prompt_bc, prompt_logdec, branch_x, branch_bc, branch_logdec, branch_prompt, branch_len):
    zero_state = jnp.zeros((H, N, P_SIZE), jnp.float32)
    prompt_out = []
    finals = []
    for prompt_id in range(NPROMPT):
        result, end_state = run_blocks(prompt_x[prompt_id], prompt_logdec[prompt_id], prompt_bc[:, prompt_id], zero_state)
        prompt_out.append(result)
        finals.append(end_state)
    finals = jnp.stack(finals)

    def branch_pass(branch_id):
        source = branch_prompt[branch_id // 2]
        start_state = jnp.take(finals, source, axis=0)
        result, end_state = run_blocks(branch_x[branch_id], branch_logdec[branch_id], branch_bc[:, branch_id], start_state)
        live_rows = jnp.arange(LB, dtype=jnp.int32) < branch_len[branch_id]
        return jnp.where(live_rows[:, None], result, jnp.zeros_like(result))
    branch_out = lax.map(branch_pass, jnp.arange(BR, dtype=jnp.int32))
    return (jnp.stack(prompt_out), branch_out)
```

```python
import functools
import jax
import jax.numpy as jnp
from jax import lax
from jax.experimental import pallas as pl
from jax.experimental.pallas import tpu as pltpu
from jax.sharding import PartitionSpec as P

BLOCK = 256
CHUNK = 32
F32 = jnp.float32
BF16 = jnp.bfloat16
VMEM_LIMIT = 40 * 1024 * 1024


def iota(shape, dim):
    return lax.broadcasted_iota(jnp.int32, shape, dim)


def exact_dot(a, b):
    return jnp.dot(a, b, preferred_element_type=F32, precision=lax.Precision.HIGHEST)


def gain_of(log_decay):
    z = 2.0 * log_decay
    series = 1.0 + z * (1.0 / 9.0)
    for k in (8, 7, 6, 5, 4, 3, 2):
        series = 1.0 + z * (1.0 / k) * series
    small = -z * series
    large = 1.0 - jnp.exp(z)
    return jnp.sqrt(jnp.maximum(jnp.where(z > -0.5, small, large), 0.0))


def hi_lo(value):
    high = value.astype(BF16).astype(F32)
    return jnp.concatenate([high, value - high], axis=0)


def spread(heads, width, lanes, first_head):
    rows = lax.rem(iota((2 * heads, lanes), 0), heads)
    cols = iota((2 * heads, lanes), 1) // width
    return jnp.where(rows - cols == first_head, 1.0, 0.0).astype(BF16)


def ends_kernel(x_ref, ld_ref, b_ref, end_ref, log_ref, push_ref, *, heads, width, state):
    tile = pl.program_id(0)
    positions = ld_ref.shape[2]
    lanes = x_ref.shape[2]

    @pl.when(tile == 0)
    def _():
        logs = ld_ref[0]
        after = jnp.where(iota((positions, positions), 0) > iota((positions, positions), 1), 1.0, 0.0)
        to_end = jnp.exp(exact_dot(logs, after)) * gain_of(logs)
        b_rows = b_ref[0, 0].astype(F32)
        push = b_rows[None, :, :] * to_end[:, None, :]
        push_ref[...] = push.reshape(heads * state, positions).astype(BF16)

    group = 256 // width
    tile_heads = lanes // width
    for g in range(tile_heads // group):
        first = tile * tile_heads + g * group
        rows = pl.ds(pl.multiple_of(first * state, group * state), group * state)
        cols = pl.ds(g * 256, 256)
        both = jnp.dot(push_ref[rows, :], x_ref[0, :, cols], preferred_element_type=F32)
        both = both.reshape(group, state, 256)
        own = iota(both.shape, 0) == iota(both.shape, 2) // width
        end_ref[:, cols] = jnp.sum(jnp.where(own, both, 0.0), axis=0)
    totals = lax.dot_general(
        jnp.ones((8, positions), F32), ld_ref[0], (((1,), (1,)), ((), ())),
        preferred_element_type=F32, precision=lax.Precision.HIGHEST)
    pick = iota((heads, lanes), 0) == iota((heads, lanes), 1) // width + tile * tile_heads
    log_ref[...] = exact_dot(totals, jnp.where(pick, 1.0, 0.0))


def local_ends(x, logdec, bc, which):
    _, positions, channels = x.shape
    heads, state = logdec.shape[1], bc.shape[2]
    width = channels // heads
    lanes = min(1024, channels)
    kernel = functools.partial(ends_kernel, heads=heads, width=width, state=state)
    return pl.pallas_call(
        kernel,
        grid=(channels // lanes,),
        in_specs=[
            pl.BlockSpec((1, positions, lanes), lambda j: (which, 0, j)),
            pl.BlockSpec((1, heads, positions), lambda j: (which, 0, 0)),
            pl.BlockSpec((1, 1, state, positions), lambda j: (0, which, 0, 0)),
        ],
        out_specs=[
            pl.BlockSpec((state, lanes), lambda j: (0, j)),
            pl.BlockSpec((8, lanes), lambda j: (0, j)),
        ],
        out_shape=[
            jax.ShapeDtypeStruct((state, channels), F32),
            jax.ShapeDtypeStruct((8, channels), F32),
        ],
        scratch_shapes=[pltpu.VMEM((heads * state, positions), BF16)],
        compiler_params=pltpu.CompilerParams(vmem_limit_bytes=VMEM_LIMIT),
        cost_estimate=pl.CostEstimate(
            flops=2 * 64 * positions * channels, bytes_accessed=2 * positions * channels, transcendentals=0),
        name="local_ends",
    )(x, logdec, bc)


def prepare(logs, b_rows, c_rows, w_ref, l_ref, c_ref, state):
    size = logs.shape[1]
    chunks = size // CHUNK
    half = CHUNK // 2
    src, dst = iota((size, size), 0), iota((size, size), 1)
    middle = dst // CHUNK * CHUNK + half - 1
    plus = (src > middle) & (src <= dst)
    minus = (src > dst) & (src <= middle)
    offset = exact_dot(logs, jnp.where(plus, 1.0, jnp.where(minus, -1.0, 0.0)))
    row_scale = hi_lo(jnp.exp(offset))
    in_scale = hi_lo(jnp.exp(-offset) * gain_of(logs))
    span = iota((size, 128), 1) == (iota((size, 128), 0) + half) // CHUNK
    steps = hi_lo(jnp.exp(exact_dot(logs, jnp.where(span, 1.0, 0.0))))
    w_ref[pl.ds(0, size), :] = in_scale.T.astype(BF16)
    w_ref[pl.ds(size, size), :] = row_scale.T.astype(BF16)
    w_ref[pl.ds(2 * size, 16), :] = steps.T[:16].astype(BF16)

    scores = lax.dot_general(c_rows, b_rows, (((0,), (0,)), ((), ())), preferred_element_type=F32)
    keep = (dst <= src) & (dst // CHUNK == src // CHUNK)
    l_ref[pl.ds(0, size), :] = jnp.where(keep, scores, 0.0).astype(BF16)
    rows = state * chunks
    mine = iota((rows, size), 0) // state == iota((rows, size), 1) // CHUNK
    b_all = jnp.concatenate([b_rows.astype(F32)] * chunks, axis=0)
    l_ref[pl.ds(size, rows), :] = jnp.where(mine, b_all, 0.0).astype(BF16)
    c_all = jnp.concatenate([c_rows.astype(F32)] * chunks, axis=0)
    c_ref[...] = jnp.where(mine, c_all, 0.0).T.astype(BF16)


def layer_kernel(*refs, heads, width, state, has_start, with_reach):
    x_ref, ld_ref, bc_ref = refs[:3]
    refs = refs[3:]
    if has_start:
        start_ref, refs = refs[0], refs[1:]
    y_ref, refs = refs[0], refs[1:]
    if with_reach:
        reach_ref, refs = refs[0], refs[1:]
        before_ref, refs = refs[-1], refs[:-1]
    w_ref, l_ref, c_ref, s_ref = refs
    block, tile = pl.program_id(1), pl.program_id(2)
    size, lanes = x_ref.shape[1], x_ref.shape[2]
    chunks = size // CHUNK
    tile_heads = lanes // width

    @pl.when(tile == 0)
    def _():
        logs = ld_ref[0]
        c_rows = bc_ref[1, 0]
        prepare(logs, bc_ref[0, 0], c_rows, w_ref, l_ref, c_ref, state)
        if with_reach:
            upto = jnp.where(iota((size, size), 0) <= iota((size, size), 1), 1.0, 0.0)
            run = exact_dot(logs, upto)
            entered = jnp.where(block == 0, 0.0, before_ref[:, 0:1])
            run = run + entered
            before_ref[...] = jnp.broadcast_to(run[:, size - 1:size], before_ref.shape)
            reach = c_rows.astype(F32)[None, :, :] * jnp.exp(run)[:, None, :]
            reach_ref[0] = reach.reshape(heads * state, size).T.astype(BF16)

    for g in range(lanes // 256):
        cols = pl.ds(g * 256, 256)
        here = pl.ds(pl.multiple_of(tile * lanes + g * 256, 256), 256)
        one_hot = spread(heads, width, 256, tile * tile_heads + g * (256 // width))
        scales = jnp.dot(w_ref[...], one_hot, preferred_element_type=F32)
        scaled = (x_ref[0, :, cols].astype(F32) * scales[:size]).astype(BF16)
        both = jnp.dot(l_ref[...], scaled, preferred_element_type=F32)
        if has_start:
            first = start_ref[0, :, cols]
        else:
            first = jnp.zeros((state, 256), F32)
        entering = jnp.where(block == 0, first, s_ref[:, here])
        carry = scales[2 * size:2 * size + 1] * entering
        carries = []
        for c in range(chunks):
            carries.append(carry.astype(BF16))
            local = both[size + c * state:size + (c + 1) * state]
            carry = scales[2 * size + c + 1:2 * size + c + 2] * (carry + local)
        s_ref[:, here] = carry
        carried = jnp.dot(c_ref[...], jnp.concatenate(carries, axis=0), preferred_element_type=F32)
        out = (both[:size] + carried) * scales[size:2 * size]
        y_ref[0, :, cols] = out.astype(y_ref.dtype)


def layer(x, logdec, bc, start, out_type, with_reach, name):
    count, positions, channels = x.shape
    heads, state = logdec.shape[1], bc.shape[2]
    width = channels // heads
    lanes = min(1024, channels)
    blocks = positions // BLOCK
    chunks = BLOCK // CHUNK
    kernel = functools.partial(
        layer_kernel, heads=heads, width=width, state=state,
        has_start=start is not None, with_reach=with_reach)
    in_specs = [
        pl.BlockSpec((1, BLOCK, lanes), lambda i, b, j: (i, b, j)),
        pl.BlockSpec((1, heads, BLOCK), lambda i, b, j: (i, 0, b)),
        pl.BlockSpec((2, 1, state, BLOCK), lambda i, b, j: (0, i, 0, b)),
    ]
    args = [x, logdec, bc]
    if start is not None:
        in_specs.append(pl.BlockSpec((1, state, lanes), lambda i, b, j: (i, 0, j)))
        args.append(start)
    out_specs = [pl.BlockSpec((1, BLOCK, lanes), lambda i, b, j: (i, b, j))]
    out_shape = [jax.ShapeDtypeStruct(x.shape, out_type)]
    scratch = [
        pltpu.VMEM((2 * BLOCK + 16, 2 * heads), BF16),
        pltpu.VMEM((BLOCK + chunks * state, BLOCK), BF16),
        pltpu.VMEM((BLOCK, chunks * state), BF16),
        pltpu.VMEM((state, channels), F32),
    ]
    if with_reach:
        out_specs.append(pl.BlockSpec((1, BLOCK, heads * state), lambda i, b, j: (i, b, 0)))
        out_shape.append(jax.ShapeDtypeStruct((count, positions, heads * state), BF16))
        scratch.append(pltpu.VMEM((heads, 128), F32))
    return pl.pallas_call(
        kernel,
        grid=(count, blocks, channels // lanes),
        in_specs=in_specs,
        out_specs=out_specs,
        out_shape=out_shape,
        scratch_shapes=scratch,
        compiler_params=pltpu.CompilerParams(vmem_limit_bytes=VMEM_LIMIT),
        cost_estimate=pl.CostEstimate(
            flops=2 * 1152 * x.size, bytes_accessed=4 * x.size, transcendentals=0),
        name=name,
    )(*args)


def finish_kernel(len_ref, own_ref, reach_ref, start_ref, y_ref, *, width, state):
    branch = pl.program_id(0)
    tile = pl.program_id(1)
    positions, lanes = own_ref.shape[1], own_ref.shape[2]
    group = 128 // state
    span = group * width
    live = iota((positions, 1), 0) < len_ref[branch]
    own_head = iota((group * state, span), 0) // state == iota((group * state, span), 1) // width
    for g in range(lanes // span):
        cols = pl.ds(g * span, span)
        first = (tile * (lanes // span) + g) * 128
        start = jnp.concatenate([start_ref[:, cols]] * group, axis=0)
        start = jnp.where(own_head, start, 0.0).astype(BF16)
        term = jnp.dot(reach_ref[0, :, pl.ds(pl.multiple_of(first, 128), 128)], start, preferred_element_type=F32)
        out = own_ref[0, :, cols].astype(F32) + term
        y_ref[0, :, cols] = jnp.where(live, out, 0.0).astype(BF16)


def finish(lengths, own, reach, start):
    count, positions, channels = own.shape
    state = start.shape[0]
    width = channels * state // reach.shape[2]
    lanes = min(1024, channels)
    return pl.pallas_call(
        functools.partial(finish_kernel, width=width, state=state),
        grid=(count, channels // lanes),
        in_specs=[
            pl.BlockSpec(memory_space=pltpu.SMEM),
            pl.BlockSpec((1, positions, lanes), lambda i, j: (i, 0, j)),
            pl.BlockSpec((1, positions, reach.shape[2]), lambda i, j: (i, 0, 0)),
            pl.BlockSpec((state, lanes), lambda i, j: (0, j)),
        ],
        out_specs=pl.BlockSpec((1, positions, lanes), lambda i, j: (i, 0, j)),
        out_shape=jax.ShapeDtypeStruct(own.shape, BF16),
        compiler_params=pltpu.CompilerParams(vmem_limit_bytes=VMEM_LIMIT),
        cost_estimate=pl.CostEstimate(
            flops=2 * 128 * own.size, bytes_accessed=6 * own.size, transcendentals=0),
        name="branch_finish",
    )(lengths, own, reach, start)


def swap_bit(value, bit, size):
    return lax.ppermute(value, "ctx", [(k, k ^ bit) for k in range(size)])


def prefix_and_total(end, log, size):
    mine = lax.axis_index("ctx")
    odd = (mine & 1) == 1
    width = end.shape[1] // 2
    log = log[:1]

    def halves(a):
        return a[:, :width], a[:, width:]

    low, high = halves(end)
    log_low, log_high = halves(log)
    got = swap_bit(jnp.where(odd, low, high), 1, size)
    got_log = swap_bit(jnp.where(odd, log_low, log_high), 1, size)
    keep, keep_log = jnp.where(odd, high, low), jnp.where(odd, log_high, log_low)
    first = jnp.where(odd, got, keep)
    first_log = jnp.where(odd, got_log, keep_log)
    second = jnp.where(odd, keep, got)
    second_log = jnp.where(odd, keep_log, got_log)
    total = jnp.exp(second_log) * first + second
    total_log = first_log + second_log
    before = jnp.zeros_like(total)
    before_log = jnp.zeros_like(total_log)
    bit = 2
    while bit < size:
        upper = (mine & bit) != 0
        other = swap_bit(total, bit, size)
        other_log = swap_bit(total_log, bit, size)
        before = jnp.where(upper, jnp.exp(before_log) * other + before, before)
        before_log = jnp.where(upper, before_log + other_log, before_log)
        total = jnp.where(
            upper, jnp.exp(total_log) * other + total, jnp.exp(other_log) * total + other)
        total_log = total_log + other_log
        bit *= 2
    next_before = jnp.exp(first_log) * before + first
    got = swap_bit(jnp.where(odd, before, next_before), 1, size)
    keep = jnp.where(odd, next_before, before)
    entering = jnp.concatenate([jnp.where(odd, got, keep), jnp.where(odd, keep, got)], axis=1)
    return entering, total


def branch_start(totals, chosen, ctx_size, pair_size):
    ctx, pair = lax.axis_index("ctx"), lax.axis_index("pair")
    owner = ctx * pair_size // ctx_size

    def shift(value, hop, back):
        links = []
        for k in range(ctx_size):
            z = k * pair_size // ctx_size
            ends = (k * pair_size + z, k * pair_size + (z + hop) % pair_size)
            links.append(ends[::-1] if back else ends)
        return lax.ppermute(value, ("ctx", "pair"), links)

    def pick(which):
        out = totals[0]
        for i in range(1, len(totals)):
            out = jnp.where(which == i, totals[i], out)
        return out

    start = jnp.where(pair == owner, pick(chosen[0]), 0.0)
    for hop in range(1, pair_size):
        wanted = shift(chosen, hop, True)[0]
        start = start + shift(pick(wanted), hop, False)
    return start


def body(
    prompt_x,
    prompt_bc,
    prompt_logdec,
    branch_x,
    branch_bc,
    branch_logdec,
    branch_prompt,
    branch_len,
):
    ctx_size, pair_size = lax.axis_size("ctx"), lax.axis_size("pair")
    entering, totals = [], []
    for which in range(prompt_x.shape[0]):
        end, log = local_ends(prompt_x, prompt_logdec, prompt_bc, which)
        before, total = prefix_and_total(end, log, ctx_size)
        entering.append(before)
        totals.append(total)
    own, reach = layer(branch_x, branch_logdec, branch_bc, None, F32, True, "branch_own")
    (prompt_y,) = layer(prompt_x, prompt_logdec, prompt_bc, jnp.stack(entering), BF16, False, "prompt_layer")
    start = branch_start(totals, branch_prompt, ctx_size, pair_size)
    branch_y = finish(branch_len, own, reach, start)
    return prompt_y, branch_y


def solution(mesh):
    return jax.shard_map(
        body,
        mesh=mesh,
        in_specs=(
            P(None, "ctx", "pair"),
            P(None, None, None, "ctx"),
            P(None, "pair", "ctx"),
            P("pair", None, "ctx"),
            P(None, "pair", None, None),
            P("pair", "ctx", None),
            P("pair"),
            P("pair"),
        ),
        out_specs=(P(None, "ctx", "pair"), P("pair", None, "ctx")),
        check_vma=False,
    )
```

```python
import functools
import jax
import jax.numpy as jnp
from jax import lax
from jax.experimental import pallas as pl
from jax.experimental.pallas import tpu as pltpu
from jax.sharding import PartitionSpec as P

BLOCK = 256
CHUNK = 32
F32 = jnp.float32
BF16 = jnp.bfloat16
VMEM_LIMIT = 40 * 1024 * 1024


def iota(shape, dim):
    return lax.broadcasted_iota(jnp.int32, shape, dim)


def quotient(index, divisor):
    if divisor & (divisor - 1) == 0:
        return lax.shift_right_logical(index, divisor.bit_length() - 1)
    return lax.div(index, divisor)


def remainder(index, divisor):
    if divisor & (divisor - 1) == 0:
        return index & (divisor - 1)
    return lax.rem(index, divisor)


def exact_dot(a, b):
    return jnp.dot(a, b, preferred_element_type=F32, precision=lax.Precision.HIGHEST)


def gain_of(log_decay):
    z = 2.0 * log_decay
    series = 1.0 + z * (1.0 / 9.0)
    for k in (8, 7, 6, 5, 4, 3, 2):
        series = 1.0 + z * (1.0 / k) * series
    small = -z * series
    large = 1.0 - jnp.exp(z)
    return jnp.sqrt(jnp.maximum(jnp.where(z > -0.5, small, large), 0.0))


def hi_lo(value):
    high = value.astype(BF16).astype(F32)
    return jnp.concatenate([high, value - high], axis=0)


def head_distance(heads, width, lanes):
    return remainder(iota((2 * heads, 1), 0), heads) - quotient(iota((1, lanes), 1), width)


def ends_kernel(x_ref, ld_ref, b_ref, end_ref, log_ref, push_ref, *, heads, width, state):
    tile = pl.program_id(1)
    positions = ld_ref.shape[2]
    lanes = x_ref.shape[2]

    @pl.when(tile == 0)
    def _():
        logs = ld_ref[0]
        after = jnp.where(iota((positions, 1), 0) > iota((1, positions), 1), 1.0, 0.0)
        to_end = jnp.exp(exact_dot(logs, after)) * gain_of(logs)
        b_rows = b_ref[0, 0].astype(F32)
        push = b_rows[None, :, :] * to_end[:, None, :]
        push_ref[...] = push.reshape(heads * state, positions).astype(BF16)

    group = 256 // width
    tile_heads = lanes // width
    lane_head = quotient(iota((1, 256), 1), width)
    for g in range(tile_heads // group):
        first = tile * tile_heads + g * group
        rows = pl.ds(pl.multiple_of(first * state, group * state), group * state)
        cols = pl.ds(g * 256, 256)
        both = jnp.dot(push_ref[rows, :], x_ref[0, :, cols], preferred_element_type=F32)
        end = jnp.where(lane_head == 0, both[:state], 0.0)
        for i in range(1, group):
            end = jnp.where(lane_head == i, both[i * state:(i + 1) * state], end)
        end_ref[0, :, cols] = end
    totals = lax.dot_general(
        jnp.ones((8, positions), F32), ld_ref[0], (((1,), (1,)), ((), ())),
        preferred_element_type=F32, precision=lax.Precision.HIGHEST)
    pick = iota((heads, 1), 0) == quotient(iota((1, lanes), 1), width) + tile * tile_heads
    log_ref[0] = exact_dot(totals, jnp.where(pick, 1.0, 0.0))


def local_ends(x, logdec, bc):
    count, positions, channels = x.shape
    heads, state = logdec.shape[1], bc.shape[2]
    width = channels // heads
    lanes = min(1024, channels)
    kernel = functools.partial(ends_kernel, heads=heads, width=width, state=state)
    return pl.pallas_call(
        kernel,
        grid=(count, channels // lanes),
        in_specs=[
            pl.BlockSpec((1, positions, lanes), lambda i, j: (i, 0, j)),
            pl.BlockSpec((1, heads, positions), lambda i, j: (i, 0, 0)),
            pl.BlockSpec((1, 1, state, positions), lambda i, j: (0, i, 0, 0)),
        ],
        out_specs=[
            pl.BlockSpec((1, state, lanes), lambda i, j: (i, 0, j)),
            pl.BlockSpec((1, 8, lanes), lambda i, j: (i, 0, j)),
        ],
        out_shape=[
            jax.ShapeDtypeStruct((count, state, channels), F32),
            jax.ShapeDtypeStruct((count, 8, channels), F32),
        ],
        scratch_shapes=[pltpu.VMEM((heads * state, positions), BF16)],
        compiler_params=pltpu.CompilerParams(vmem_limit_bytes=60 * 1024 * 1024),
        cost_estimate=pl.CostEstimate(
            flops=2 * 64 * x.size, bytes_accessed=2 * x.size, transcendentals=0),
        name="local_ends",
    )(x, logdec, bc)


def prepare(logs, b_rows, c_rows, w_ref, l_ref, c_ref, state):
    size = logs.shape[1]
    chunks = size // CHUNK
    half = CHUNK // 2
    src, dst = iota((size, 1), 0), iota((1, size), 1)
    middle = quotient(dst, CHUNK) * CHUNK + half - 1
    plus = (src > middle) & (src <= dst)
    minus = (src > dst) & (src <= middle)
    offset = exact_dot(logs, jnp.where(plus, 1.0, jnp.where(minus, -1.0, 0.0)))
    row_scale = hi_lo(jnp.exp(offset))
    in_scale = hi_lo(jnp.exp(-offset) * gain_of(logs))
    span = iota((1, 128), 1) == quotient(src + half, CHUNK)
    steps = hi_lo(jnp.exp(exact_dot(logs, jnp.where(span, 1.0, 0.0))))
    w_ref[pl.ds(0, size), :] = in_scale.T.astype(BF16)
    w_ref[pl.ds(size, size), :] = row_scale.T.astype(BF16)
    w_ref[pl.ds(2 * size, 16), :] = steps.T[:16].astype(BF16)

    scores = lax.dot_general(c_rows, b_rows, (((0,), (0,)), ((), ())), preferred_element_type=F32)
    keep = (dst <= src) & (quotient(dst, CHUNK) == quotient(src, CHUNK))
    l_ref[pl.ds(0, size), :] = jnp.where(keep, scores, 0.0).astype(BF16)
    rows = state * chunks
    mine = quotient(iota((rows, 1), 0), state) == quotient(dst, CHUNK)
    b_all = jnp.concatenate([b_rows.astype(F32)] * chunks, axis=0)
    l_ref[pl.ds(size, rows), :] = jnp.where(mine, b_all, 0.0).astype(BF16)
    c_all = jnp.concatenate([c_rows.astype(F32)] * chunks, axis=0)
    c_ref[...] = jnp.where(mine, c_all, 0.0).T.astype(BF16)


def layer_kernel(*refs, heads, width, state, has_start, with_reach, skip):
    x_ref, ld_ref, bc_ref = refs[:3]
    refs = refs[3 + skip:]
    if has_start:
        start_ref, refs = refs[0], refs[1:]
    y_ref, refs = refs[0], refs[1:]
    if with_reach:
        reach_ref, refs = refs[0], refs[1:]
        before_ref, refs = refs[-1], refs[:-1]
    w_ref, l_ref, c_ref, s_ref, far_ref = refs
    block, tile = pl.program_id(1), pl.program_id(2)
    size, lanes = x_ref.shape[1], x_ref.shape[2]
    chunks = size // CHUNK
    tile_heads = lanes // width

    @pl.when(tile == 0)
    def _():
        logs = ld_ref[0]
        c_rows = bc_ref[1, 0]
        prepare(logs, bc_ref[0, 0], c_rows, w_ref, l_ref, c_ref, state)
        far_ref[...] = head_distance(heads, width, 256)
        if with_reach:
            upto = jnp.where(iota((size, 1), 0) <= iota((1, size), 1), 1.0, 0.0)
            run = exact_dot(logs, upto)
            entered = jnp.where(block == 0, 0.0, before_ref[:, 0:1])
            run = run + entered
            before_ref[...] = jnp.broadcast_to(run[:, size - 1:size], before_ref.shape)
            reach = c_rows.astype(F32)[None, :, :] * jnp.exp(run)[:, None, :]
            reach_ref[0] = reach.reshape(heads * state, size).T.astype(BF16)

    for g in range(lanes // 256):
        cols = pl.ds(g * 256, 256)
        here = pl.ds(pl.multiple_of(tile * lanes + g * 256, 256), 256)
        first_head = tile * tile_heads + g * (256 // width)
        one_hot = jnp.where(far_ref[...] == first_head, 1.0, 0.0).astype(BF16)
        scales = jnp.dot(w_ref[...], one_hot, preferred_element_type=F32)
        scaled = (x_ref[0, :, cols].astype(F32) * scales[:size]).astype(BF16)
        both = jnp.dot(l_ref[...], scaled, preferred_element_type=F32)
        if has_start:
            first = start_ref[0, :, cols]
        else:
            first = jnp.zeros((state, 256), F32)
        entering = jnp.where(block == 0, first, s_ref[:, here])
        carry = scales[2 * size:2 * size + 1] * entering
        carries = []
        for c in range(chunks):
            carries.append(carry.astype(BF16))
            local = both[size + c * state:size + (c + 1) * state]
            carry = scales[2 * size + c + 1:2 * size + c + 2] * (carry + local)
        s_ref[:, here] = carry
        carried = jnp.dot(c_ref[...], jnp.concatenate(carries, axis=0), preferred_element_type=F32)
        out = (both[:size] + carried) * scales[size:2 * size]
        y_ref[0, :, cols] = out.astype(y_ref.dtype)


def layer(x, logdec, bc, start, out_type, with_reach, name, which=None, into=()):
    count, positions, channels = x.shape
    heads, state = logdec.shape[1], bc.shape[2]
    width = channels // heads
    lanes = min(1024, channels)
    blocks = positions // BLOCK
    chunks = BLOCK // CHUNK
    kernel = functools.partial(
        layer_kernel, heads=heads, width=width, state=state,
        has_start=start is not None, with_reach=with_reach, skip=len(into))
    base = 0 if which is None else which
    in_specs = [
        pl.BlockSpec((1, BLOCK, lanes), lambda i, b, j: (i + base, b, j)),
        pl.BlockSpec((1, heads, BLOCK), lambda i, b, j: (i + base, 0, b)),
        pl.BlockSpec((2, 1, state, BLOCK), lambda i, b, j: (0, i + base, 0, b)),
    ]
    args = [x, logdec, bc, *into]
    in_specs += [pl.BlockSpec(memory_space=pl.ANY)] * len(into)
    if start is not None:
        in_specs.append(pl.BlockSpec((1, state, lanes), lambda i, b, j: (i, 0, j)))
        args.append(start)
    out_specs = [pl.BlockSpec((1, BLOCK, lanes), lambda i, b, j: (i + base, b, j))]
    out_shape = [jax.ShapeDtypeStruct(x.shape, out_type)]
    scratch = [
        pltpu.VMEM((2 * BLOCK + 16, 2 * heads), BF16),
        pltpu.VMEM((BLOCK + chunks * state, BLOCK), BF16),
        pltpu.VMEM((BLOCK, chunks * state), BF16),
        pltpu.VMEM((state, channels), F32),
        pltpu.VMEM((2 * heads, 256), jnp.int32),
    ]
    if with_reach:
        out_specs.append(pl.BlockSpec((1, BLOCK, heads * state), lambda i, b, j: (i + base, b, 0)))
        out_shape.append(jax.ShapeDtypeStruct((count, positions, heads * state), BF16))
        scratch.append(pltpu.VMEM((heads, 128), F32))
    sequences = count if which is None else 1
    work = sequences * positions * channels
    return pl.pallas_call(
        kernel,
        grid=(sequences, blocks, channels // lanes),
        in_specs=in_specs,
        out_specs=out_specs,
        out_shape=out_shape,
        scratch_shapes=scratch,
        input_output_aliases={3 + i: i for i in range(len(into))},
        compiler_params=pltpu.CompilerParams(vmem_limit_bytes=VMEM_LIMIT),
        cost_estimate=pl.CostEstimate(
            flops=2 * 1152 * work, bytes_accessed=4 * work, transcendentals=0),
        name=name,
    )(*args)


def finish_kernel(len_ref, own_ref, reach_ref, start_ref, y_ref, *, width, state):
    branch = pl.program_id(0)
    tile = pl.program_id(1)
    positions, lanes = own_ref.shape[1], own_ref.shape[2]
    group = 128 // state
    span = group * width
    live = iota((positions, 1), 0) < len_ref[branch]
    own_head = quotient(iota((group * state, 1), 0), state) == quotient(iota((1, span), 1), width)
    for g in range(lanes // span):
        cols = pl.ds(g * span, span)
        first = (tile * (lanes // span) + g) * 128
        start = jnp.concatenate([start_ref[:, cols]] * group, axis=0)
        start = jnp.where(own_head, start, 0.0).astype(BF16)
        term = jnp.dot(reach_ref[0, :, pl.ds(pl.multiple_of(first, 128), 128)], start, preferred_element_type=F32)
        out = own_ref[0, :, cols].astype(F32) + term
        y_ref[0, :, cols] = jnp.where(live, out, 0.0).astype(BF16)


def finish(lengths, own, reach, start):
    count, positions, channels = own.shape
    state = start.shape[0]
    width = channels * state // reach.shape[2]
    lanes = min(1024, channels)
    return pl.pallas_call(
        functools.partial(finish_kernel, width=width, state=state),
        grid=(count, channels // lanes),
        in_specs=[
            pl.BlockSpec(memory_space=pltpu.SMEM),
            pl.BlockSpec((1, positions, lanes), lambda i, j: (i, 0, j)),
            pl.BlockSpec((1, positions, reach.shape[2]), lambda i, j: (i, 0, 0)),
            pl.BlockSpec((state, lanes), lambda i, j: (0, j)),
        ],
        out_specs=pl.BlockSpec((1, positions, lanes), lambda i, j: (i, 0, j)),
        out_shape=jax.ShapeDtypeStruct(own.shape, BF16),
        compiler_params=pltpu.CompilerParams(vmem_limit_bytes=VMEM_LIMIT),
        cost_estimate=pl.CostEstimate(
            flops=2 * 128 * own.size, bytes_accessed=6 * own.size, transcendentals=0),
        name="branch_finish",
    )(lengths, own, reach, start)


def swap_bit(value, bit, size):
    return lax.ppermute(value, "ctx", [(k, k ^ bit) for k in range(size)])


def pack(states, logs):
    lanes = states.shape[-1]
    return jnp.concatenate([states.reshape(-1, lanes), logs.reshape(-1, lanes)], axis=0)


def unpack(packed, count):
    lanes = packed.shape[-1]
    rows = packed.shape[0] - count
    return packed[:rows].reshape(count, rows // count, lanes), packed[rows:].reshape(count, 1, lanes)


def in_order(upper, mine, other):
    first = [jnp.where(upper, o, m) for m, o in zip(mine, other)]
    second = [jnp.where(upper, m, o) for m, o in zip(mine, other)]
    return first, second


def join(first, second):
    return jnp.exp(second[1]) * first[0] + second[0], first[1] + second[1]


def branch_prompts(chosen, pair_size):
    known = chosen
    while known.shape[0] < pair_size:
        step = known.shape[0]
        further = lax.ppermute(known, "pair", [((z + step) % pair_size, z) for z in range(pair_size)])
        known = jnp.concatenate([known, further])
    return known


def branch_start(total, wanted, ctx_size, pair_size):
    ctx, pair = lax.axis_index("ctx"), lax.axis_index("pair")
    owner = ctx * pair_size // ctx_size

    def pick(which):
        out = total[0]
        for i in range(1, total.shape[0]):
            out = jnp.where(which == i, total[i], out)
        return out

    parts = [jnp.where(pair == owner, pick(wanted[0]), 0.0)]
    for hop in range(1, pair_size):
        links = []
        for k in range(ctx_size):
            z = k * pair_size // ctx_size
            links.append((k * pair_size + z, k * pair_size + (z + hop) % pair_size))
        parts.append(lax.ppermute(pick(wanted[hop]), ("ctx", "pair"), links))
    return sum(parts)


def body(
    prompt_x,
    prompt_bc,
    prompt_logdec,
    branch_x,
    branch_bc,
    branch_logdec,
    branch_prompt,
    branch_len,
):
    size, pair_size = lax.axis_size("ctx"), lax.axis_size("pair")
    prompts, branches = prompt_x.shape[0], branch_x.shape[0]
    assert size == 2 * pair_size and size & (size - 1) == 0 and branch_prompt.shape[0] == 1
    mine = lax.axis_index("ctx")
    odd = (mine & 1) == 1
    wanted = branch_prompts(branch_prompt, pair_size)

    end, log = local_ends(prompt_x, prompt_logdec, prompt_bc)
    half = end.shape[2] // 2
    low, high = (end[:, :, :half], log[:, :1, :half]), (end[:, :, half:], log[:, :1, half:])
    keep = [jnp.where(odd, h, l) for l, h in zip(low, high)]
    send = [jnp.where(odd, l, h) for l, h in zip(low, high)]
    got = unpack(swap_bit(pack(*send), 1, size), prompts)
    first, second = in_order(odd, keep, got)
    total, total_log = join(first, second)
    before, before_log = jnp.zeros_like(total), jnp.zeros_like(total_log)

    own = ()
    works = iter(range(branches))
    bit = 2
    while bit < size:
        packed = pack(total, total_log)
        which = next(works, None)
        if which is not None:
            packed, branch_x = lax.optimization_barrier((packed, branch_x))
        got = swap_bit(packed, bit, size)
        if which is not None:
            own = layer(branch_x, branch_logdec, branch_bc, None, F32, True, "branch_own", which, own)
            got, own = lax.optimization_barrier((got, own))
        other = unpack(got, prompts)
        upper = (mine & bit) != 0
        before = jnp.where(upper, jnp.exp(before_log) * other[0] + before, before)
        before_log = jnp.where(upper, before_log + other[1], before_log)
        total, total_log = join(*in_order(upper, (total, total_log), other))
        bit *= 2
    for which in works:
        own = layer(branch_x, branch_logdec, branch_bc, None, F32, True, "branch_own", which, own)

    next_before = jnp.exp(first[1]) * before + first[0]
    got = swap_bit(jnp.where(odd, before, next_before), 1, size)
    keep = jnp.where(odd, next_before, before)
    entering = jnp.concatenate([jnp.where(odd, got, keep), jnp.where(odd, keep, got)], axis=2)
    start = branch_start(total, wanted, size, pair_size)
    (prompt_y,) = layer(prompt_x, prompt_logdec, prompt_bc, entering, BF16, False, "prompt_layer")
    start, prompt_y = lax.optimization_barrier((start, prompt_y))
    branch_y = finish(branch_len, *own, start)
    return prompt_y, branch_y


def solution(mesh):
    return jax.shard_map(
        body,
        mesh=mesh,
        in_specs=(
            P(None, "ctx", "pair"),
            P(None, None, None, "ctx"),
            P(None, "pair", "ctx"),
            P("pair", None, "ctx"),
            P(None, "pair", None, None),
            P("pair", "ctx", None),
            P("pair"),
            P("pair"),
        ),
        out_specs=(P(None, "ctx", "pair"), P("pair", None, "ctx")),
        check_vma=False,
    )
```

```python
import functools
import jax
import jax.numpy as jnp
from jax import lax
from jax.experimental import pallas as pl
from jax.experimental.pallas import tpu as pltpu
from jax.sharding import PartitionSpec as P

BLOCK = 256
CHUNK = 32
F32 = jnp.float32
BF16 = jnp.bfloat16
VMEM_LIMIT = 32 * 1024 * 1024


def iota(shape, dim):
    return lax.broadcasted_iota(jnp.int32, shape, dim)


def quotient(index, divisor):
    if divisor & (divisor - 1) == 0:
        return lax.shift_right_logical(index, divisor.bit_length() - 1)
    return lax.div(index, divisor)


def remainder(index, divisor):
    if divisor & (divisor - 1) == 0:
        return index & (divisor - 1)
    return lax.rem(index, divisor)


def exact_dot(a, b):
    return jnp.dot(a, b, preferred_element_type=F32, precision=lax.Precision.HIGHEST)


def gain_of(log_decay):
    z = 2.0 * log_decay
    series = 1.0 + z * (1.0 / 9.0)
    for k in (8, 7, 6, 5, 4, 3, 2):
        series = 1.0 + z * (1.0 / k) * series
    small = -z * series
    large = 1.0 - jnp.exp(z)
    return jnp.sqrt(jnp.maximum(jnp.where(z > -0.5, small, large), 0.0))


def hi_lo(value):
    high = value.astype(BF16).astype(F32)
    return jnp.concatenate([high, value - high], axis=0)


def in_hbm(array):
    return pltpu.with_memory_space_constraint(array, pltpu.HBM)


def split_dot(rows, one_hot):
    count = rows.shape[0]
    high = rows.astype(BF16).astype(F32)
    middle = (rows - high).astype(BF16).astype(F32)
    parts = jnp.concatenate([high, middle, rows - high - middle], axis=0).astype(BF16)
    out = jnp.dot(parts, one_hot, preferred_element_type=F32)
    return out[:count] + out[count:2 * count] + out[2 * count:]


def ends_kernel(
    x_ref, ld_in, bc_in, end_ref, log_ref, ld_ref, b_ref, held_ref, push_ref, sems, first_sems, *, width, lanes
):
    first_copies = [
        pltpu.make_async_copy(ld_in, ld_ref, first_sems.at[0]),
        pltpu.make_async_copy(bc_in.at[0], b_ref, first_sems.at[1]),
    ]
    for copy in first_copies:
        copy.start()
    count, heads, positions = ld_ref.shape
    state = end_ref.shape[1]
    channels = end_ref.shape[2]
    tiles = channels // lanes
    copies = {}
    for i in range(count):
        for j in range(tiles):
            cols = pl.ds(j * lanes, lanes)
            copies[i, j] = pltpu.make_async_copy(
                x_ref.at[i, :, cols], held_ref.at[i, :, cols], sems.at[i, j])
            copies[i, j].start()
    for copy in first_copies:
        copy.wait()
    logs = jnp.concatenate([ld_ref[i] for i in range(count)], axis=0)
    after = jnp.where(iota((positions, 1), 0) > iota((1, positions), 1), 1.0, 0.0)
    to_end = jnp.exp(exact_dot(logs, after)) * gain_of(logs)
    for i in range(count):
        b_rows = b_ref[i].astype(F32)
        push = b_rows[None, :, :] * to_end[i * heads:(i + 1) * heads][:, None, :]
        push_ref[i] = push.reshape(heads * state, positions).astype(BF16)
    group = 256 // width
    lane_head = quotient(iota((1, 256), 1), width)
    for i in range(count):
        totals = lax.dot_general(
            jnp.ones((16, positions), F32), ld_ref[i], (((1,), (1,)), ((), ())),
            preferred_element_type=F32, precision=lax.Precision.HIGHEST)
        for j in range(tiles):
            cols = pl.ds(j * lanes, lanes)
            pick = iota((heads, 1), 0) == quotient(iota((1, lanes), 1), width) + j * (lanes // width)
            log_ref[i, :, cols] = split_dot(totals, jnp.where(pick, 1.0, 0.0).astype(BF16))[:8]
    for i in range(count):
        for j in range(tiles):
            copies[i, j].wait()
            for g in range(lanes // 256):
                first = j * (lanes // width) + g * group
                cols = pl.ds(j * lanes + g * 256, 256)
                both = jnp.dot(
                    push_ref[i, pl.ds(first * state, group * state), :], held_ref[i, :, cols],
                    preferred_element_type=F32)
                end = jnp.where(lane_head == 0, both[:state], 0.0)
                for k in range(1, group):
                    end = jnp.where(lane_head == k, both[k * state:(k + 1) * state], end)
                end_ref[i, :, cols] = end


def local_ends(x, logdec, bc):
    count, positions, channels = x.shape
    heads, state = logdec.shape[1], bc.shape[2]
    width = channels // heads
    lanes = min(1024, channels)
    whole = pl.BlockSpec(memory_space=pltpu.VMEM)
    return pl.pallas_call(
        functools.partial(ends_kernel, width=width, lanes=lanes),
        in_specs=[pl.BlockSpec(memory_space=pltpu.HBM)] * 3,
        out_specs=[whole, whole],
        out_shape=[
            jax.ShapeDtypeStruct((count, state, channels), F32),
            jax.ShapeDtypeStruct((count, 8, channels), F32),
        ],
        scratch_shapes=[
            pltpu.VMEM(logdec.shape, F32),
            pltpu.VMEM(bc.shape[1:], BF16),
            pltpu.VMEM(x.shape, BF16),
            pltpu.VMEM((count, heads * state, positions), BF16),
            pltpu.SemaphoreType.DMA((count, channels // lanes)),
            pltpu.SemaphoreType.DMA((2,)),
        ],
        compiler_params=pltpu.CompilerParams(vmem_limit_bytes=VMEM_LIMIT),
        cost_estimate=pl.CostEstimate(
            flops=2 * 64 * x.size, bytes_accessed=2 * x.size, transcendentals=0),
        name="local_ends",
    )(in_hbm(x), in_hbm(logdec), in_hbm(bc))


def prepare(parts, logs, w_ref, lb_ref, lc_ref, state):
    size = logs.shape[1]
    heads = logs.shape[0] // len(parts)
    chunks = size // CHUNK
    half = CHUNK // 2
    src, dst = iota((size, 1), 0), iota((1, size), 1)
    middle = quotient(dst, CHUNK) * CHUNK + half - 1
    plus = (src > middle) & (src <= dst)
    minus = (src > dst) & (src <= middle)
    offset = exact_dot(logs, jnp.where(plus, 1.0, jnp.where(minus, -1.0, 0.0)))
    row_scale = jnp.exp(offset)
    in_scale = jnp.exp(-offset) * gain_of(logs)
    span = iota((1, 128), 1) == quotient(src + half, CHUNK)
    steps = jnp.exp(exact_dot(logs, jnp.where(span, 1.0, 0.0)))
    rows = state * chunks
    mine = quotient(iota((rows, 1), 0), state) == quotient(dst, CHUNK)
    keep = (dst <= src) & (quotient(dst, CHUNK) == quotient(src, CHUNK))
    for i, (b_rows, c_rows) in enumerate(parts):
        here = slice(i * heads, (i + 1) * heads)
        w_ref[i, pl.ds(0, size), :] = hi_lo(in_scale[here]).T.astype(BF16)
        w_ref[i, pl.ds(size, 16), :] = hi_lo(steps[here]).T[:16].astype(BF16)
        w_ref[i, pl.ds(size + 16, size), :] = hi_lo(row_scale[here]).T.astype(BF16)
        scores = lax.dot_general(c_rows, b_rows, (((0,), (0,)), ((), ())), preferred_element_type=F32)
        lc_ref[i, :, pl.ds(0, size)] = jnp.where(keep, scores, 0.0).astype(BF16)
        c_all = jnp.concatenate([c_rows.astype(F32)] * chunks, axis=0)
        lc_ref[i, :, pl.ds(size, rows)] = jnp.where(mine, c_all, 0.0).T.astype(BF16)
        b_all = jnp.concatenate([b_rows.astype(F32)] * chunks, axis=0)
        lb_ref[i] = jnp.where(mine, b_all, 0.0).astype(BF16)


def layer_kernel(*refs, width, has_start, with_reach, skip, lanes):
    x_ref, ld_ref, bc_ref = refs[:3]
    refs = refs[3 + skip:]
    if has_start:
        start_ref, refs = refs[0], refs[1:]
    y_ref, refs = refs[0], refs[1:]
    if with_reach:
        reach_ref, refs = refs[0], refs[1:]
    w_ref, lb_ref, lc_ref, hot_ref, s_ref = refs
    sequence, block, tile = pl.program_id(0), pl.program_id(1), pl.program_id(2)
    count, heads, positions = ld_ref.shape
    state, size = bc_ref.shape[2], x_ref.shape[1]
    blocks, chunks = positions // size, size // CHUNK
    channels = hot_ref.shape[1]

    @pl.when((sequence == 0) & (block == 0) & (tile == 0))
    def _():
        cuts = [(i, pl.ds(b * size, size)) for i in range(count) for b in range(blocks)]
        logs = jnp.concatenate([ld_ref[i, :, cut] for i, cut in cuts], axis=0)
        parts = [(bc_ref[0, i, :, cut], bc_ref[1, i, :, cut]) for i, cut in cuts]
        prepare(parts, logs, w_ref, lb_ref, lc_ref, state)
        row_head = remainder(iota((2 * heads, 1), 0), heads)
        for g in range(channels // 256):
            lane_head = quotient(iota((1, 256), 1), width) + g * (256 // width)
            hot_ref[:, pl.ds(g * 256, 256)] = jnp.where(row_head == lane_head, 1.0, 0.0).astype(BF16)
        if with_reach:
            upto = jnp.where(iota((size, 1), 0) <= iota((1, size), 1), 1.0, 0.0)
            runs = exact_dot(logs, upto)
            for k, (i, cut) in enumerate(cuts):
                run = runs[k * heads:(k + 1) * heads]
                if k % blocks:
                    run = run + entered
                entered = run[:, size - 1:size]
                reach = parts[k][1].astype(F32)[None, :, :] * jnp.exp(run)[:, None, :]
                reach_ref[i, cut, :] = reach.reshape(heads * state, size).T.astype(BF16)

    at = sequence * blocks + block
    tiles = lanes // 256
    scaled, steps, carries, ones = {}, {}, {}, {}

    def scale(g):
        ones[g] = hot_ref[:, pl.ds(pl.multiple_of(tile * lanes + g * 256, 256), 256)]
        wide = jnp.dot(w_ref[at, pl.ds(0, size + 16), :], ones[g], preferred_element_type=F32)
        steps[g] = wide[size:]
        scaled[g] = (x_ref[0, :, pl.ds(g * 256, 256)].astype(F32) * wide[:size]).astype(BF16)

    def pass_on(g):
        local = jnp.dot(lb_ref[at], scaled[g], preferred_element_type=F32)
        if has_start:
            entering = start_ref[0, :, pl.ds(g * 256, 256)]
        else:
            entering = jnp.zeros((state, 256), F32)
        if blocks > 1:
            here = pl.ds(pl.multiple_of(tile * lanes + g * 256, 256), 256)
            entering = jnp.where(block == 0, entering, s_ref[:, here])
        carry = steps[g][0:1] * entering
        rows = []
        for c in range(chunks):
            rows.append(carry.astype(BF16))
            if c < chunks - 1 or blocks > 1:
                carry = steps[g][c + 1:c + 2] * (carry + local[c * state:(c + 1) * state])
        if blocks > 1:
            s_ref[:, here] = carry
        carries[g] = jnp.concatenate(rows, axis=0)

    def give(g):
        both = jnp.concatenate([scaled[g], carries[g]], axis=0)
        out = jnp.dot(lc_ref[at], both, preferred_element_type=F32)
        rows = jnp.dot(w_ref[at, pl.ds(size + 16, size), :], ones[g], preferred_element_type=F32)
        y_ref[0, :, pl.ds(g * 256, 256)] = (out * rows).astype(y_ref.dtype)

    for g in range(tiles + 2):
        if g < tiles:
            scale(g)
        if 0 <= g - 1 < tiles:
            pass_on(g - 1)
        if 0 <= g - 2:
            give(g - 2)


def layer(x, logdec, bc, start, out_type, with_reach, name, which=None, into=()):
    count, positions, channels = x.shape
    heads, state = logdec.shape[1], bc.shape[2]
    width = channels // heads
    lanes = min(1024, channels)
    blocks = positions // BLOCK
    rows = BLOCK // CHUNK * state
    kernel = functools.partial(
        layer_kernel, width=width, has_start=start is not None, with_reach=with_reach,
        skip=len(into), lanes=lanes)
    base = 0 if which is None else which
    sequences = count if which is None else 1
    in_specs = [
        pl.BlockSpec((1, BLOCK, lanes), lambda i, b, j: (i + base, b, j)),
        pl.BlockSpec((sequences, heads, positions), lambda i, b, j: (base, 0, 0)),
        pl.BlockSpec((2, sequences, state, positions), lambda i, b, j: (0, base, 0, 0)),
    ]
    args = [in_hbm(x), logdec, bc, *into]
    in_specs += [pl.BlockSpec(memory_space=pl.ANY)] * len(into)
    if start is not None:
        in_specs.append(pl.BlockSpec((1, state, lanes), lambda i, b, j: (i, 0, j)))
        args.append(start)
    out_specs = [pl.BlockSpec((1, BLOCK, lanes), lambda i, b, j: (i + base, b, j))]
    out_shape = [jax.ShapeDtypeStruct(x.shape, out_type)]
    if with_reach:
        out_specs.append(pl.BlockSpec((sequences, positions, heads * state), lambda i, b, j: (base, 0, 0)))
        out_shape.append(jax.ShapeDtypeStruct((count, positions, heads * state), BF16))
    cuts = sequences * blocks
    work = sequences * positions * channels
    return pl.pallas_call(
        kernel,
        grid=(sequences, blocks, channels // lanes),
        in_specs=in_specs,
        out_specs=out_specs,
        out_shape=out_shape,
        scratch_shapes=[
            pltpu.VMEM((cuts, 2 * BLOCK + 16, 2 * heads), BF16),
            pltpu.VMEM((cuts, rows, BLOCK), BF16),
            pltpu.VMEM((cuts, BLOCK, BLOCK + rows), BF16),
            pltpu.VMEM((2 * heads, channels), BF16),
            pltpu.VMEM((state, channels), F32),
        ],
        input_output_aliases={3 + i: i for i in range(len(into))},
        compiler_params=pltpu.CompilerParams(vmem_limit_bytes=VMEM_LIMIT),
        cost_estimate=pl.CostEstimate(
            flops=2 * 1152 * work, bytes_accessed=4 * work, transcendentals=0),
        name=name,
    )(*args)


def finish_kernel(len_ref, own_ref, reach_ref, start_ref, y_ref, *, width):
    branch, tile = pl.program_id(0), pl.program_id(1)
    positions, lanes = y_ref.shape[1], y_ref.shape[2]
    state = start_ref.shape[0]
    group = 128 // state
    span = group * width
    live = iota((positions, span), 0) < len_ref[branch]
    own_head = quotient(iota((128, 1), 0), state) == quotient(iota((1, span), 1), width)
    for g in range(lanes // span):
        here = pl.ds(pl.multiple_of(tile * lanes + g * span, span), span)
        first = pl.ds(pl.multiple_of((tile * (lanes // span) + g) * 128, 128), 128)
        start = jnp.concatenate([start_ref[:, here]] * group, axis=0)
        start = jnp.where(own_head, start, 0.0).astype(BF16)
        term = jnp.dot(reach_ref[branch, :, first], start, preferred_element_type=F32)
        out = jnp.where(live, own_ref[branch, :, here] + term, 0.0)
        y_ref[0, :, pl.ds(g * span, span)] = out.astype(BF16)


def finish(lengths, own, reach, start):
    count, positions, channels = own.shape
    width = channels * start.shape[0] // reach.shape[2]
    lanes = min(1024, channels)
    whole = pl.BlockSpec(memory_space=pltpu.VMEM)
    return pl.pallas_call(
        functools.partial(finish_kernel, width=width),
        grid=(count, channels // lanes),
        in_specs=[pl.BlockSpec(memory_space=pltpu.SMEM), whole, whole, whole],
        out_specs=pl.BlockSpec((1, positions, lanes), lambda i, j: (i, 0, j)),
        out_shape=jax.ShapeDtypeStruct(own.shape, BF16),
        compiler_params=pltpu.CompilerParams(vmem_limit_bytes=VMEM_LIMIT),
        cost_estimate=pl.CostEstimate(
            flops=2 * 128 * own.size, bytes_accessed=6 * own.size, transcendentals=0),
        name="branch_finish",
    )(lengths, own, reach, start)


def swap_bit(value, bit, size):
    return lax.ppermute(value, "ctx", [(k, k ^ bit) for k in range(size)])


def pack(states, logs):
    lanes = states.shape[-1]
    return jnp.concatenate([states.reshape(-1, lanes), logs.reshape(-1, lanes)], axis=0)


def unpack(packed, count):
    lanes = packed.shape[-1]
    rows = packed.shape[0] - count
    return packed[:rows].reshape(count, rows // count, lanes), packed[rows:].reshape(count, 1, lanes)


def in_order(upper, mine, other):
    first = [jnp.where(upper, o, m) for m, o in zip(mine, other)]
    second = [jnp.where(upper, m, o) for m, o in zip(mine, other)]
    return first, second


def join(first, second):
    return jnp.exp(second[1]) * first[0] + second[0], first[1] + second[1]


def branch_prompts(chosen, pair_size):
    known = chosen
    while known.shape[0] < pair_size:
        step = known.shape[0]
        further = lax.ppermute(known, "pair", [((z + step) % pair_size, z) for z in range(pair_size)])
        known = jnp.concatenate([known, further])
    return known


def branch_start(total, wanted, ctx_size, pair_size):
    ctx, pair = lax.axis_index("ctx"), lax.axis_index("pair")
    owner = ctx * pair_size // ctx_size

    def pick(which):
        out = total[0]
        for i in range(1, total.shape[0]):
            out = jnp.where(which == i, total[i], out)
        return out

    parts = [jnp.where(pair == owner, pick(wanted[0]), 0.0)]
    for hop in range(1, pair_size):
        links = []
        for k in range(ctx_size):
            z = k * pair_size // ctx_size
            links.append((k * pair_size + z, k * pair_size + (z + hop) % pair_size))
        parts.append(lax.ppermute(pick(wanted[hop]), ("ctx", "pair"), links))
    return sum(parts)


def body(
    prompt_x,
    prompt_bc,
    prompt_logdec,
    branch_x,
    branch_bc,
    branch_logdec,
    branch_prompt,
    branch_len,
):
    size, pair_size = lax.axis_size("ctx"), lax.axis_size("pair")
    prompts, branches = prompt_x.shape[0], branch_x.shape[0]
    assert size == 2 * pair_size and size & (size - 1) == 0 and branch_prompt.shape[0] == 1
    mine = lax.axis_index("ctx")
    odd = (mine & 1) == 1
    wanted = branch_prompts(branch_prompt, pair_size)

    end, log = local_ends(prompt_x, prompt_logdec, prompt_bc)
    half = end.shape[2] // 2
    low, high = (end[:, :, :half], log[:, :1, :half]), (end[:, :, half:], log[:, :1, half:])
    keep = [jnp.where(odd, h, l) for l, h in zip(low, high)]
    send = [jnp.where(odd, l, h) for l, h in zip(low, high)]
    got = unpack(swap_bit(pack(*send), 1, size), prompts)
    first, second = in_order(odd, keep, got)
    total, total_log = join(first, second)
    before, before_log = jnp.zeros_like(total), jnp.zeros_like(total_log)

    own = ()
    works = iter(range(branches))
    bit = 2
    while bit < size:
        packed = pack(total, total_log)
        which = next(works, None)
        if which is not None:
            packed, branch_x = lax.optimization_barrier((packed, branch_x))
        got = swap_bit(packed, bit, size)
        if which is not None:
            own = layer(branch_x, branch_logdec, branch_bc, None, F32, True, "branch_own", which, own)
            got, own = lax.optimization_barrier((got, own))
        other = unpack(got, prompts)
        upper = (mine & bit) != 0
        before = jnp.where(upper, jnp.exp(before_log) * other[0] + before, before)
        before_log = jnp.where(upper, before_log + other[1], before_log)
        total, total_log = join(*in_order(upper, (total, total_log), other))
        bit *= 2
    for which in works:
        own = layer(branch_x, branch_logdec, branch_bc, None, F32, True, "branch_own", which, own)

    next_before = jnp.exp(first[1]) * before + first[0]
    got = swap_bit(jnp.where(odd, before, next_before), 1, size)
    keep = jnp.where(odd, next_before, before)
    entering = jnp.concatenate([jnp.where(odd, got, keep), jnp.where(odd, keep, got)], axis=2)
    start = branch_start(total, wanted, size, pair_size)
    (prompt_y,) = layer(prompt_x, prompt_logdec, prompt_bc, entering, BF16, False, "prompt_layer")
    start, prompt_y = lax.optimization_barrier((start, prompt_y))
    branch_y = finish(branch_len, *own, start)
    return prompt_y, branch_y


def solution(mesh):
    return jax.shard_map(
        body,
        mesh=mesh,
        in_specs=(
            P(None, "ctx", "pair"),
            P(None, None, None, "ctx"),
            P(None, "pair", "ctx"),
            P("pair", None, "ctx"),
            P(None, "pair", None, None),
            P("pair", "ctx", None),
            P("pair"),
            P("pair"),
        ),
        out_specs=(P(None, "ctx", "pair"), P("pair", None, "ctx")),
        check_vma=False,
    )
```

```python
import functools
import jax
import jax.numpy as jnp
from jax import lax
from jax.experimental import pallas as pl
from jax.experimental.pallas import tpu as pltpu
from jax.sharding import PartitionSpec as P

BLOCK = 256
CHUNK = 32
F32 = jnp.float32
BF16 = jnp.bfloat16
VMEM_LIMIT = 32 * 1024 * 1024


def iota(shape, dim):
    return lax.broadcasted_iota(jnp.int32, shape, dim)


def quotient(index, divisor):
    if divisor & (divisor - 1) == 0:
        return lax.shift_right_logical(index, divisor.bit_length() - 1)
    return lax.div(index, divisor)


def remainder(index, divisor):
    if divisor & (divisor - 1) == 0:
        return index & (divisor - 1)
    return lax.rem(index, divisor)


def exact_dot(a, b):
    return jnp.dot(a, b, preferred_element_type=F32, precision=lax.Precision.HIGHEST)


def gain_of(log_decay):
    z = 2.0 * log_decay
    series = 1.0 + z * (1.0 / 9.0)
    for k in (8, 7, 6, 5, 4, 3, 2):
        series = 1.0 + z * (1.0 / k) * series
    small = -z * series
    large = 1.0 - jnp.exp(z)
    return jnp.sqrt(jnp.maximum(jnp.where(z > -0.5, small, large), 0.0))


def hi_lo(value):
    high = value.astype(BF16).astype(F32)
    return jnp.concatenate([high, value - high], axis=0)


def in_hbm(array):
    return pltpu.with_memory_space_constraint(array, pltpu.HBM)


def split_dot(rows, one_hot):
    count = rows.shape[0]
    high = rows.astype(BF16).astype(F32)
    middle = (rows - high).astype(BF16).astype(F32)
    parts = jnp.concatenate([high, middle, rows - high - middle], axis=0).astype(BF16)
    out = jnp.dot(parts, one_hot, preferred_element_type=F32)
    return out[:count] + out[count:2 * count] + out[2 * count:]


def ends_kernel(
    x_ref, ld_in, bc_in, end_ref, log_ref, held_ref, ld_ref, b_ref, push_ref, sems, first_sems, *, width, lanes
):
    first_copies = [
        pltpu.make_async_copy(ld_in, ld_ref, first_sems.at[0]),
        pltpu.make_async_copy(bc_in.at[0], b_ref, first_sems.at[1]),
    ]
    for copy in first_copies:
        copy.start()
    count, heads, positions = ld_ref.shape
    state = end_ref.shape[1]
    channels = end_ref.shape[2]
    tiles = channels // lanes
    copies = {}
    for i in range(count):
        for j in range(tiles):
            cols = pl.ds(j * lanes, lanes)
            copies[i, j] = pltpu.make_async_copy(
                x_ref.at[i, :, cols], held_ref.at[i, :, cols], sems.at[i, j])
            copies[i, j].start()
    for copy in first_copies:
        copy.wait()
    logs = jnp.concatenate([ld_ref[i] for i in range(count)], axis=0)
    after = jnp.where(iota((positions, 1), 0) > iota((1, positions), 1), 1.0, 0.0)
    to_end = jnp.exp(exact_dot(logs, after)) * gain_of(logs)
    for i in range(count):
        b_rows = b_ref[i].astype(F32)
        push = b_rows[None, :, :] * to_end[i * heads:(i + 1) * heads][:, None, :]
        push_ref[i] = push.reshape(heads * state, positions).astype(BF16)
    group = 256 // width
    lane_head = quotient(iota((1, 256), 1), width)
    for i in range(count):
        totals = lax.dot_general(
            jnp.ones((16, positions), F32), ld_ref[i], (((1,), (1,)), ((), ())),
            preferred_element_type=F32, precision=lax.Precision.HIGHEST)
        for j in range(tiles):
            cols = pl.ds(j * lanes, lanes)
            pick = iota((heads, 1), 0) == quotient(iota((1, lanes), 1), width) + j * (lanes // width)
            log_ref[i, :, cols] = split_dot(totals, jnp.where(pick, 1.0, 0.0).astype(BF16))[:8]
    for i in range(count):
        for j in range(tiles):
            copies[i, j].wait()
            for g in range(lanes // 256):
                first = j * (lanes // width) + g * group
                cols = pl.ds(j * lanes + g * 256, 256)
                both = jnp.dot(
                    push_ref[i, pl.ds(first * state, group * state), :], held_ref[i, :, cols],
                    preferred_element_type=F32)
                end = jnp.where(lane_head == 0, both[:state], 0.0)
                for k in range(1, group):
                    end = jnp.where(lane_head == k, both[k * state:(k + 1) * state], end)
                end_ref[i, :, cols] = end


def local_ends(x, logdec, bc):
    count, positions, channels = x.shape
    heads, state = logdec.shape[1], bc.shape[2]
    width = channels // heads
    lanes = min(1024, channels)
    whole = pl.BlockSpec(memory_space=pltpu.VMEM)
    return pl.pallas_call(
        functools.partial(ends_kernel, width=width, lanes=lanes),
        in_specs=[pl.BlockSpec(memory_space=pltpu.HBM)] * 3,
        out_specs=[whole, whole, whole],
        out_shape=[
            jax.ShapeDtypeStruct((count, state, channels), F32),
            jax.ShapeDtypeStruct((count, 8, channels), F32),
            jax.ShapeDtypeStruct(x.shape, BF16),
        ],
        scratch_shapes=[
            pltpu.VMEM(logdec.shape, F32),
            pltpu.VMEM(bc.shape[1:], BF16),
            pltpu.VMEM((count, heads * state, positions), BF16),
            pltpu.SemaphoreType.DMA((count, channels // lanes)),
            pltpu.SemaphoreType.DMA((2,)),
        ],
        compiler_params=pltpu.CompilerParams(vmem_limit_bytes=VMEM_LIMIT),
        cost_estimate=pl.CostEstimate(
            flops=2 * 64 * x.size, bytes_accessed=2 * x.size, transcendentals=0),
        name="local_ends",
    )(in_hbm(x), in_hbm(logdec), in_hbm(bc))


def prepare(parts, logs, lv_ref, lc_ref, state):
    size = logs.shape[1]
    chunks = size // CHUNK
    half = CHUNK // 2
    src, dst = iota((size, 1), 0), iota((1, size), 1)
    middle = quotient(dst, CHUNK) * CHUNK + half - 1
    plus = (src > middle) & (src <= dst)
    minus = (src > dst) & (src <= middle)
    offset = exact_dot(logs, jnp.where(plus, 1.0, jnp.where(minus, -1.0, 0.0)))
    row_scale = jnp.exp(offset)
    in_scale = jnp.exp(-offset) * gain_of(logs)
    span = iota((1, 128), 1) == quotient(src + half, CHUNK)
    steps = jnp.exp(exact_dot(logs, jnp.where(span, 1.0, 0.0)))
    rows = state * chunks
    mine = quotient(iota((rows, 1), 0), state) == quotient(dst, CHUNK)
    keep = (dst <= src) & (quotient(dst, CHUNK) == quotient(src, CHUNK))
    for i, (b_rows, c_rows) in enumerate(parts):
        b_all = jnp.concatenate([b_rows.astype(F32)] * chunks, axis=0)
        lv_ref[i, pl.ds(0, rows), :] = jnp.where(mine, b_all, 0.0).astype(BF16)
        scores = lax.dot_general(c_rows, b_rows, (((0,), (0,)), ((), ())), preferred_element_type=F32)
        lv_ref[i, pl.ds(rows, size), :] = jnp.where(keep, scores, 0.0).astype(BF16)
        c_all = jnp.concatenate([c_rows.astype(F32)] * chunks, axis=0)
        lc_ref[i] = jnp.where(mine, c_all, 0.0).T.astype(BF16)
    return in_scale, row_scale, steps


def cuts_of(ld_ref):
    count, _, positions = ld_ref.shape
    return [(i, pl.ds(b * BLOCK, BLOCK)) for i in range(count) for b in range(positions // BLOCK)]


def prepare_kernel(
    pld_ref, pbc_ref, bld_ref, bbc_ref,
    pv_ref, pu_ref, ps_ref, plv_ref, plc_ref, w_ref, hot_ref, blv_ref, blc_ref, reach_ref, *, width
):
    state = pbc_ref.shape[2]

    def collect(ld_ref, bc_ref):
        cuts = cuts_of(ld_ref)
        logs = jnp.concatenate([ld_ref[i, :, cut] for i, cut in cuts], axis=0)
        return cuts, logs, [(bc_ref[0, i, :, cut], bc_ref[1, i, :, cut]) for i, cut in cuts]

    cuts, logs, parts = collect(bld_ref, bbc_ref)
    heads = bld_ref.shape[1]
    blocks = len(cuts) // bld_ref.shape[0]
    in_scale, row_scale, steps = prepare(parts, logs, blv_ref, blc_ref, state)
    for k in range(len(cuts)):
        here = slice(k * heads, (k + 1) * heads)
        w_ref[k, pl.ds(0, BLOCK), :] = hi_lo(in_scale[here]).T.astype(BF16)
        w_ref[k, pl.ds(BLOCK, 16), :] = hi_lo(steps[here]).T[:16].astype(BF16)
        w_ref[k, pl.ds(BLOCK + 16, BLOCK), :] = hi_lo(row_scale[here]).T.astype(BF16)
    row_head = remainder(iota((2 * heads, 1), 0), heads)
    for g in range(hot_ref.shape[1] // 256):
        lane_head = quotient(iota((1, 256), 1), width) + g * (256 // width)
        hot_ref[:, pl.ds(g * 256, 256)] = jnp.where(row_head == lane_head, 1.0, 0.0).astype(BF16)
    upto = jnp.where(iota((BLOCK, 1), 0) <= iota((1, BLOCK), 1), 1.0, 0.0)
    runs = exact_dot(logs, upto)
    for k, (i, cut) in enumerate(cuts):
        run = runs[k * heads:(k + 1) * heads]
        if k % blocks:
            run = run + entered
        entered = run[:, BLOCK - 1:BLOCK]
        reach = parts[k][1].astype(F32)[None, :, :] * jnp.exp(run)[:, None, :]
        reach_ref[i, cut, :] = reach.reshape(heads * state, BLOCK).T.astype(BF16)

    cuts, logs, parts = collect(pld_ref, pbc_ref)
    heads = pld_ref.shape[1] // 2
    in_scale, row_scale, steps = prepare(parts, logs, plv_ref, plc_ref, state)
    for k in range(len(cuts)):
        for h in range(2):
            here = slice((2 * k + h) * heads, (2 * k + h + 1) * heads)
            pv_ref[k, h] = in_scale[here].T
            pu_ref[k, h] = row_scale[here].T
            ps_ref[k, h] = steps[here].T[:16]


def prepare_all(prompt_logdec, prompt_bc, branch_logdec, branch_bc, branch_channels):
    state = prompt_bc.shape[2]
    rows = BLOCK // CHUNK * state
    prompt_cuts = prompt_logdec.shape[0] * (prompt_logdec.shape[2] // BLOCK)
    branches, heads, positions = branch_logdec.shape
    branch_cuts = branches * (positions // BLOCK)
    half = prompt_logdec.shape[1] // 2
    shapes = [
        ((prompt_cuts, 2, BLOCK, half), F32),
        ((prompt_cuts, 2, BLOCK, half), F32),
        ((prompt_cuts, 2, 16, half), F32),
        ((prompt_cuts, rows + BLOCK, BLOCK), BF16),
        ((prompt_cuts, BLOCK, rows), BF16),
        ((branch_cuts, 2 * BLOCK + 16, 2 * heads), BF16),
        ((2 * heads, branch_channels), BF16),
        ((branch_cuts, rows + BLOCK, BLOCK), BF16),
        ((branch_cuts, BLOCK, rows), BF16),
        ((branches, positions, heads * state), BF16),
    ]
    whole = pl.BlockSpec(memory_space=pltpu.VMEM)
    out = pl.pallas_call(
        functools.partial(prepare_kernel, width=branch_channels // heads),
        in_specs=[whole] * 4,
        out_specs=[whole] * len(shapes),
        out_shape=[jax.ShapeDtypeStruct(*shape) for shape in shapes],
        compiler_params=pltpu.CompilerParams(vmem_limit_bytes=VMEM_LIMIT),
        cost_estimate=pl.CostEstimate(flops=10**8, bytes_accessed=10**6, transcendentals=0),
        name="prepare",
    )(prompt_logdec, prompt_bc, branch_logdec, branch_bc)
    return out[:5], out[5:9], out[9]


def run_tiles(jobs):
    scaled, passed = {}, {}
    for g in range(len(jobs) + 2):
        if g < len(jobs):
            scaled[g] = jobs[g][0]()
        if 0 <= g - 1 < len(jobs):
            passed[g - 1] = jobs[g - 1][1](scaled.pop(g - 1))
        if 0 <= g - 2:
            jobs[g - 2][2](passed.pop(g - 2))


def through_chunks(both, steps, entering, state, chunks):
    rows, carry = [], steps[0:1] * entering
    for c in range(chunks):
        rows.append(carry.astype(BF16))
        carry = steps[c + 1:c + 2] * (carry + both[c * state:(c + 1) * state])
    return jnp.concatenate(rows, axis=0), carry


def branch_kernel(*refs, which, skip):
    x_in, w_ref, hot_ref, lv_ref, lc_ref = refs[:5]
    own_ref, x_ref, s_ref, sems = refs[5 + skip:]
    positions, channels = x_ref.shape
    state = s_ref.shape[0]
    chunks = BLOCK // CHUNK
    rows = chunks * state
    blocks = positions // BLOCK
    lanes = min(1024, channels)
    copies = {}
    for b in range(blocks):
        for j in range(channels // lanes):
            part = (pl.ds(b * BLOCK, BLOCK), pl.ds(j * lanes, lanes))
            copies[b, j] = pltpu.make_async_copy(x_in.at[(which, *part)], x_ref.at[part], sems.at[b, j])
            copies[b, j].start()

    def job(b, g):
        at = which * blocks + b
        spot = (pl.ds(b * BLOCK, BLOCK), pl.ds(g * 256, 256))

        def scale():
            if g * 256 % lanes == 0:
                copies[b, g * 256 // lanes].wait()
            wide = jnp.dot(w_ref[at], hot_ref[:, pl.ds(g * 256, 256)], preferred_element_type=F32)
            scaled = (x_ref[spot].astype(F32) * wide[:BLOCK]).astype(BF16)
            return scaled, wide[BLOCK:BLOCK + 16], wide[BLOCK + 16:]

        def pass_on(given):
            scaled, steps, out_scale = given
            both = jnp.dot(lv_ref[at], scaled, preferred_element_type=F32)
            here = pl.ds(g * 256, 256)
            entering = s_ref[:, here] if b else jnp.zeros((state, 256), F32)
            carries, carry = through_chunks(both, steps, entering, state, chunks)
            if b < blocks - 1:
                s_ref[:, here] = carry
            return both[rows:], carries, out_scale

        def give(given):
            inner, carries, out_scale = given
            carried = jnp.dot(lc_ref[at], carries, preferred_element_type=F32)
            own_ref[(which, *spot)] = (inner + carried) * out_scale

        return scale, pass_on, give

    run_tiles([job(b, g) for b in range(blocks) for g in range(channels // 256)])


def branch_own(x, ready, which, into):
    _, positions, channels = x.shape
    state = ready[3].shape[2] * CHUNK // BLOCK
    whole = pl.BlockSpec(memory_space=pltpu.VMEM)
    lanes = min(1024, channels)
    work = positions * channels
    return pl.pallas_call(
        functools.partial(branch_kernel, which=which, skip=len(into)),
        in_specs=[pl.BlockSpec(memory_space=pltpu.HBM)] + [whole] * (4 + len(into)),
        out_specs=whole,
        out_shape=jax.ShapeDtypeStruct(x.shape, F32),
        scratch_shapes=[
            pltpu.VMEM((positions, channels), BF16),
            pltpu.VMEM((state, channels), F32),
            pltpu.SemaphoreType.DMA((positions // BLOCK, channels // lanes)),
        ],
        input_output_aliases={5 + i: i for i in range(len(into))},
        compiler_params=pltpu.CompilerParams(vmem_limit_bytes=VMEM_LIMIT),
        cost_estimate=pl.CostEstimate(
            flops=2 * 1152 * work, bytes_accessed=4 * work, transcendentals=0),
        name="branch_own",
    )(in_hbm(x), *ready, *into)


def prompt_kernel(*refs, width, skip):
    half_ref, x_ref, v_ref, u_ref, s_ref, lv_ref, lc_ref, start_ref = refs[:8]
    y_out, y_ref, sems = refs[8 + skip:]
    count, positions, channels = y_ref.shape
    state = start_ref.shape[1]
    chunks = BLOCK // CHUNK
    rows = chunks * state
    blocks = positions // BLOCK
    lanes = min(512, channels)
    half = half_ref[0]
    left = iota((1, 128), 1) < width
    entered, copies = {}, []

    def widen(scales, g):
        def pair(k):
            return jnp.where(left, scales[:, k:k + 1], scales[:, k + 1:k + 2])

        first = g * (256 // width)
        return jnp.concatenate([pair(first + k) for k in range(0, 256 // width, 2)], axis=1)

    def job(i, b, g):
        at = i * blocks + b
        spot = (i, pl.ds(b * BLOCK, BLOCK), pl.ds(g * 256, 256))

        def scale():
            cols = pl.ds(pl.multiple_of(half * channels + g * 256, 256), 256)
            wide = widen(v_ref[at, half], g)
            return (x_ref[i, pl.ds(b * BLOCK, BLOCK), cols].astype(F32) * wide).astype(BF16)

        def pass_on(scaled):
            both = jnp.dot(lv_ref[at], scaled, preferred_element_type=F32)
            entering = entered[i, g] if b else start_ref[i, :, pl.ds(g * 256, 256)]
            steps = widen(s_ref[at, half], g)
            carries, entered[i, g] = through_chunks(both, steps, entering, state, chunks)
            return both[rows:], carries

        def give(given):
            inner, carries = given
            carried = jnp.dot(lc_ref[at], carries, preferred_element_type=F32)
            y_ref[spot] = ((inner + carried) * widen(u_ref[at, half], g)).astype(BF16)
            if (g + 1) * 256 % lanes == 0:
                j = (g + 1) * 256 // lanes - 1
                there = pl.ds(pl.multiple_of(half * channels + j * lanes, lanes), lanes)
                copy = pltpu.make_async_copy(
                    y_ref.at[i, pl.ds(b * BLOCK, BLOCK), pl.ds(j * lanes, lanes)],
                    y_out.at[i, pl.ds(b * BLOCK, BLOCK), there], sems.at[at, j])
                copy.start()
                copies.append(copy)

        return scale, pass_on, give

    run_tiles([job(i, b, g) for i in range(count) for b in range(blocks) for g in range(channels // 256)])
    for copy in copies:
        copy.wait()


def prompt_half(half, x, ready, start, into):
    count, positions, channels = x.shape
    width = channels // (2 * ready[0].shape[3])
    part = channels // 2
    whole = pl.BlockSpec(memory_space=pltpu.VMEM)
    hbm = pl.BlockSpec(memory_space=pltpu.HBM)
    work = count * positions * part
    return pl.pallas_call(
        functools.partial(prompt_kernel, width=width, skip=len(into)),
        in_specs=[pl.BlockSpec(memory_space=pltpu.SMEM)] + [whole] * 7 + [hbm] * len(into),
        out_specs=hbm,
        out_shape=jax.ShapeDtypeStruct(x.shape, BF16),
        scratch_shapes=[
            pltpu.VMEM((count, positions, part), BF16),
            pltpu.SemaphoreType.DMA((count * (positions // BLOCK), part // min(512, part))),
        ],
        input_output_aliases={8 + i: i for i in range(len(into))},
        compiler_params=pltpu.CompilerParams(vmem_limit_bytes=VMEM_LIMIT),
        cost_estimate=pl.CostEstimate(
            flops=2 * 1152 * work, bytes_accessed=4 * work, transcendentals=0),
        name="prompt_half",
    )(half, x, *ready, start, *into)


def finish_kernel(len_ref, own_ref, reach_ref, start_ref, y_ref, *, width):
    branch, tile = pl.program_id(0), pl.program_id(1)
    positions, lanes = y_ref.shape[1], y_ref.shape[2]
    state = start_ref.shape[0]
    group = 128 // state
    span = group * width
    live = iota((positions, span), 0) < len_ref[branch]
    own_head = quotient(iota((128, 1), 0), state) == quotient(iota((1, span), 1), width)
    for g in range(lanes // span):
        here = pl.ds(pl.multiple_of(tile * lanes + g * span, span), span)
        first = pl.ds(pl.multiple_of((tile * (lanes // span) + g) * 128, 128), 128)
        start = jnp.concatenate([start_ref[:, here]] * group, axis=0)
        start = jnp.where(own_head, start, 0.0).astype(BF16)
        term = jnp.dot(reach_ref[branch, :, first], start, preferred_element_type=F32)
        out = jnp.where(live, own_ref[branch, :, here] + term, 0.0)
        y_ref[0, :, pl.ds(g * span, span)] = out.astype(BF16)


def finish(lengths, own, reach, start):
    count, positions, channels = own.shape
    width = channels * start.shape[0] // reach.shape[2]
    lanes = min(1024, channels)
    whole = pl.BlockSpec(memory_space=pltpu.VMEM)
    return pl.pallas_call(
        functools.partial(finish_kernel, width=width),
        grid=(count, channels // lanes),
        in_specs=[pl.BlockSpec(memory_space=pltpu.SMEM), whole, whole, whole],
        out_specs=pl.BlockSpec((1, positions, lanes), lambda i, j: (i, 0, j)),
        out_shape=jax.ShapeDtypeStruct(own.shape, BF16),
        compiler_params=pltpu.CompilerParams(vmem_limit_bytes=VMEM_LIMIT),
        cost_estimate=pl.CostEstimate(
            flops=2 * 128 * own.size, bytes_accessed=6 * own.size, transcendentals=0),
        name="branch_finish",
    )(lengths, own, reach, start)


def swap_bit(value, bit, size):
    return lax.ppermute(value, "ctx", [(k, k ^ bit) for k in range(size)])


def pack(states, logs):
    lanes = states.shape[-1]
    return jnp.concatenate([states.reshape(-1, lanes), logs.reshape(-1, lanes)], axis=0)


def unpack(packed, count):
    lanes = packed.shape[-1]
    rows = packed.shape[0] - count
    return packed[:rows].reshape(count, rows // count, lanes), packed[rows:].reshape(count, 1, lanes)


def in_order(upper, mine, other):
    first = [jnp.where(upper, o, m) for m, o in zip(mine, other)]
    second = [jnp.where(upper, m, o) for m, o in zip(mine, other)]
    return first, second


def join(first, second):
    return jnp.exp(second[1]) * first[0] + second[0], first[1] + second[1]


def spread_step(value, hop, ctx_size, pair_size):
    owner = lax.axis_index("ctx") * pair_size // ctx_size
    known = [m for m in range(pair_size) if m & (2 * hop - 1) == 0]
    links = []
    for k in range(ctx_size):
        z = k * pair_size // ctx_size
        links += [(k * pair_size + (z ^ m), k * pair_size + (z ^ m ^ hop)) for m in known]
    got = lax.ppermute(value, ("ctx", "pair"), links)
    has = ((lax.axis_index("pair") ^ owner) & (2 * hop - 1)) == 0
    return got, has


def body(
    prompt_x,
    prompt_bc,
    prompt_logdec,
    branch_x,
    branch_bc,
    branch_logdec,
    branch_prompt,
    branch_len,
):
    size, pair_size = lax.axis_size("ctx"), lax.axis_size("pair")
    prompts, branches = prompt_x.shape[0], branch_x.shape[0]
    assert size == 2 * pair_size and size & (size - 1) == 0 and branch_prompt.shape[0] == 1
    mine = lax.axis_index("ctx")
    odd = (mine & 1) == 1

    def beside(exchange, value, work, *given):
        value, given = lax.optimization_barrier((value, given))
        got = exchange(value)
        return lax.optimization_barrier((got, work(*given)))

    end, log, held = local_ends(prompt_x, prompt_logdec, prompt_bc)
    half = end.shape[2] // 2
    low, high = (end[:, :, :half], log[:, :1, :half]), (end[:, :, half:], log[:, :1, half:])
    keep = [jnp.where(odd, h, l) for l, h in zip(low, high)]
    send = [jnp.where(odd, l, h) for l, h in zip(low, high)]
    got, (prompt_ready, branch_ready, reach) = beside(
        lambda v: swap_bit(v, 1, size),
        pack(*send),
        lambda ld: prepare_all(prompt_logdec, prompt_bc, ld, branch_bc, branch_x.shape[2]),
        branch_logdec,
    )
    got = unpack(got, prompts)
    first, second = in_order(odd, keep, got)
    total, total_log = join(first, second)
    before, before_log = jnp.zeros_like(total), jnp.zeros_like(total_log)

    own = ()
    works = iter(range(branches))
    bit = 2
    while bit < size:
        which = next(works, None)
        swap = functools.partial(swap_bit, bit=bit, size=size)
        if which is None:
            got = swap(pack(total, total_log))
        else:
            got, own = beside(
                swap, pack(total, total_log),
                lambda x, own: (branch_own(x, branch_ready, which, own),), branch_x, own)
        other = unpack(got, prompts)
        upper = (mine & bit) != 0
        before = jnp.where(upper, jnp.exp(before_log) * other[0] + before, before)
        before_log = jnp.where(upper, before_log + other[1], before_log)
        total, total_log = join(*in_order(upper, (total, total_log), other))
        bit *= 2
    for which in works:
        own = (branch_own(branch_x, branch_ready, which, own),)

    next_before = jnp.exp(first[1]) * before + first[0]
    keep = jnp.where(odd, next_before, before)
    others = swap_bit(jnp.where(odd, before, next_before), 1, size)
    here = jnp.reshape(mine & 1, (1,))
    sides = [(here, keep), (1 - here, others)]
    prompt_y = ()
    hop = pair_size // 2
    while hop:
        step = functools.partial(spread_step, hop=hop, ctx_size=size, pair_size=pair_size)
        if sides:
            side, entering = sides.pop(0)
            (got, has), prompt_y = beside(
                step, total,
                lambda entering, y: (prompt_half(side, held, prompt_ready, entering, y),), entering, prompt_y)
        else:
            got, has = step(total)
        total = jnp.where(has, total, got)
        hop //= 2
    for side, entering in sides:
        prompt_y = (prompt_half(side, held, prompt_ready, entering, prompt_y),)
    start = total[0]
    for which in range(1, prompts):
        start = jnp.where(branch_prompt[0] == which, total[which], start)
    branch_y = finish(branch_len, *own, reach, start)
    return prompt_y[0], branch_y


def solution(mesh):
    return jax.shard_map(
        body,
        mesh=mesh,
        in_specs=(
            P(None, "ctx", "pair"),
            P(None, None, None, "ctx"),
            P(None, "pair", "ctx"),
            P("pair", None, "ctx"),
            P(None, "pair", None, None),
            P("pair", "ctx", None),
            P("pair"),
            P("pair"),
        ),
        out_specs=(P(None, "ctx", "pair"), P("pair", None, "ctx")),
        check_vma=False,
    )
```

```python
import functools
import jax
import jax.numpy as jnp
from jax import lax
from jax.experimental import pallas as pl
from jax.experimental.pallas import tpu as pltpu
from jax.sharding import PartitionSpec as P

BLOCK = 256
CHUNK = 32
F32 = jnp.float32
BF16 = jnp.bfloat16
VMEM_LIMIT = 16 * 1024 * 1024


def iota(shape, dim):
    return lax.broadcasted_iota(jnp.int32, shape, dim)


def quotient(index, divisor):
    if divisor & (divisor - 1) == 0:
        return lax.shift_right_logical(index, divisor.bit_length() - 1)
    return lax.div(index, divisor)


def remainder(index, divisor):
    if divisor & (divisor - 1) == 0:
        return index & (divisor - 1)
    return lax.rem(index, divisor)


def exact_dot(a, b):
    return jnp.dot(a, b, preferred_element_type=F32, precision=lax.Precision.HIGHEST)


def gain_of(log_decay):
    z = 2.0 * log_decay
    series = 1.0 + z * (1.0 / 9.0)
    for k in (8, 7, 6, 5, 4, 3, 2):
        series = 1.0 + z * (1.0 / k) * series
    small = -z * series
    large = 1.0 - jnp.exp(z)
    return jnp.sqrt(jnp.maximum(jnp.where(z > -0.5, small, large), 0.0))


def hi_lo(value):
    high = value.astype(BF16).astype(F32)
    return jnp.concatenate([high, value - high], axis=0)


def in_hbm(array):
    return pltpu.with_memory_space_constraint(array, pltpu.HBM)


def split_dot(rows, one_hot):
    count = rows.shape[0]
    high = rows.astype(BF16).astype(F32)
    middle = (rows - high).astype(BF16).astype(F32)
    parts = jnp.concatenate([high, middle, rows - high - middle], axis=0).astype(BF16)
    out = jnp.dot(parts, one_hot, preferred_element_type=F32)
    return out[:count] + out[count:2 * count] + out[2 * count:]


def ends_kernel(
    x_ref, ld_in, bc_in, end_ref, log_ref, held_ref, ld_ref, b_ref, push_ref, sems, first_sems, *, width, lanes
):
    first_copies = [
        pltpu.make_async_copy(ld_in, ld_ref, first_sems.at[0]),
        pltpu.make_async_copy(bc_in.at[0], b_ref, first_sems.at[1]),
    ]
    for copy in first_copies:
        copy.start()
    count, heads, positions = ld_ref.shape
    state = end_ref.shape[1]
    channels = end_ref.shape[2]
    tiles = channels // lanes
    copies = {}
    for i in range(count):
        for j in range(tiles):
            cols = pl.ds(j * lanes, lanes)
            copies[i, j] = pltpu.make_async_copy(
                x_ref.at[i, :, cols], held_ref.at[i, :, cols], sems.at[i, j])
            copies[i, j].start()
    for copy in first_copies:
        copy.wait()
    logs = jnp.concatenate([ld_ref[i] for i in range(count)], axis=0)
    after = jnp.where(iota((positions, 1), 0) > iota((1, positions), 1), 1.0, 0.0)
    to_end = jnp.exp(exact_dot(logs, after)) * gain_of(logs)
    for i in range(count):
        b_rows = b_ref[i].astype(F32)
        push = b_rows[None, :, :] * to_end[i * heads:(i + 1) * heads][:, None, :]
        push_ref[i] = push.reshape(heads * state, positions).astype(BF16)
    group = 256 // width
    lane_head = quotient(iota((1, 256), 1), width)
    for i in range(count):
        totals = lax.dot_general(
            jnp.ones((16, positions), F32), ld_ref[i], (((1,), (1,)), ((), ())),
            preferred_element_type=F32, precision=lax.Precision.HIGHEST)
        for j in range(tiles):
            cols = pl.ds(j * lanes, lanes)
            pick = iota((heads, 1), 0) == quotient(iota((1, lanes), 1), width) + j * (lanes // width)
            log_ref[i, :, cols] = split_dot(totals, jnp.where(pick, 1.0, 0.0).astype(BF16))[:8]
    for i in range(count):
        for j in range(tiles):
            copies[i, j].wait()
            for g in range(lanes // 256):
                first = j * (lanes // width) + g * group
                cols = pl.ds(j * lanes + g * 256, 256)
                both = jnp.dot(
                    push_ref[i, pl.ds(first * state, group * state), :], held_ref[i, :, cols],
                    preferred_element_type=F32)
                end = jnp.where(lane_head == 0, both[:state], 0.0)
                for k in range(1, group):
                    end = jnp.where(lane_head == k, both[k * state:(k + 1) * state], end)
                end_ref[i, :, cols] = end


def local_ends(x, logdec, bc):
    count, positions, channels = x.shape
    heads, state = logdec.shape[1], bc.shape[2]
    width = channels // heads
    lanes = min(1024, channels)
    whole = pl.BlockSpec(memory_space=pltpu.VMEM)
    return pl.pallas_call(
        functools.partial(ends_kernel, width=width, lanes=lanes),
        in_specs=[pl.BlockSpec(memory_space=pltpu.HBM)] * 3,
        out_specs=[whole, whole],
        out_shape=[
            jax.ShapeDtypeStruct((count, state, channels), F32),
            jax.ShapeDtypeStruct((count, 8, channels), F32),
        ],
        scratch_shapes=[
            pltpu.VMEM(x.shape, BF16),
            pltpu.VMEM(logdec.shape, F32),
            pltpu.VMEM(bc.shape[1:], BF16),
            pltpu.VMEM((count, heads * state, positions), BF16),
            pltpu.SemaphoreType.DMA((count, channels // lanes)),
            pltpu.SemaphoreType.DMA((2,)),
        ],
        compiler_params=pltpu.CompilerParams(vmem_limit_bytes=VMEM_LIMIT),
        cost_estimate=pl.CostEstimate(
            flops=2 * 64 * x.size, bytes_accessed=2 * x.size, transcendentals=0),
        name="local_ends",
    )(in_hbm(x), in_hbm(logdec), in_hbm(bc))


def prepare(parts, logs, lv_ref, lc_ref, state, heads):
    size = logs.shape[1]
    chunks = size // CHUNK
    half = CHUNK // 2
    src, dst = iota((size, 1), 0), iota((1, size), 1)
    middle = quotient(dst, CHUNK) * CHUNK + half - 1
    plus = (src > middle) & (src <= dst)
    minus = (src > dst) & (src <= middle)
    offset = exact_dot(logs, jnp.where(plus, 1.0, jnp.where(minus, -1.0, 0.0)))
    row_scale = jnp.exp(offset)
    in_scale = jnp.exp(-offset) * gain_of(logs)
    span = iota((1, 128), 1) == quotient(src + half, CHUNK)
    steps = jnp.exp(exact_dot(logs, jnp.where(span, 1.0, 0.0)))
    rows = state * chunks
    mine = quotient(iota((rows, 1), 0), state) == quotient(dst, CHUNK)
    keep = (dst <= src) & (quotient(dst, CHUNK) == quotient(src, CHUNK))
    for i, (b_rows, c_rows) in enumerate(parts):
        b_all = jnp.concatenate([b_rows.astype(F32)] * chunks, axis=0)
        lv_ref[i, pl.ds(0, rows), :] = jnp.where(mine, b_all, 0.0).astype(BF16)
        scores = lax.dot_general(c_rows, b_rows, (((0,), (0,)), ((), ())), preferred_element_type=F32)
        lv_ref[i, pl.ds(rows, size), :] = jnp.where(keep, scores, 0.0).astype(BF16)
        c_all = jnp.concatenate([c_rows.astype(F32)] * chunks, axis=0)
        lc_ref[i] = jnp.where(mine, c_all, 0.0).T.astype(BF16)
    scales = []
    for first in range(0, logs.shape[0], heads):
        here = slice(first, first + heads)
        columns = [hi_lo(in_scale[here]).T, hi_lo(steps[here]).T[:16], hi_lo(row_scale[here]).T]
        scales.append(jnp.concatenate(columns, axis=0).astype(BF16))
    return scales


def cuts_of(ld_ref):
    count, _, positions = ld_ref.shape
    return [(i, pl.ds(b * BLOCK, BLOCK)) for i in range(count) for b in range(positions // BLOCK)]


def prepare_kernel(
    pld_ref, pbc_ref, bld_ref, bbc_ref,
    hot_ref, pw_ref, plv_ref, plc_ref, bw_ref, blv_ref, blc_ref, reach_ref, *, width
):
    state = pbc_ref.shape[2]

    def collect(ld_ref, bc_ref):
        cuts = cuts_of(ld_ref)
        logs = jnp.concatenate([ld_ref[i, :, cut] for i, cut in cuts], axis=0)
        return cuts, logs, [(bc_ref[0, i, :, cut], bc_ref[1, i, :, cut]) for i, cut in cuts]

    cuts, logs, parts = collect(bld_ref, bbc_ref)
    heads = bld_ref.shape[1]
    blocks = len(cuts) // bld_ref.shape[0]
    for k, w in enumerate(prepare(parts, logs, blv_ref, blc_ref, state, heads)):
        bw_ref[k] = w
    row_head = remainder(iota((2 * heads, 1), 0), heads)
    for g in range(hot_ref.shape[1] // 256):
        lane_head = quotient(iota((1, 256), 1), width) + g * (256 // width)
        hot_ref[:, pl.ds(g * 256, 256)] = jnp.where(row_head == lane_head, 1.0, 0.0).astype(BF16)
    upto = jnp.where(iota((BLOCK, 1), 0) <= iota((1, BLOCK), 1), 1.0, 0.0)
    runs = exact_dot(logs, upto)
    for k, (i, cut) in enumerate(cuts):
        run = runs[k * heads:(k + 1) * heads]
        if k % blocks:
            run = run + entered
        entered = run[:, BLOCK - 1:BLOCK]
        reach = parts[k][1].astype(F32)[None, :, :] * jnp.exp(run)[:, None, :]
        reach_ref[i, cut, :] = reach.reshape(heads * state, BLOCK).T.astype(BF16)

    cuts, logs, parts = collect(pld_ref, pbc_ref)
    heads = pld_ref.shape[1] // 2
    for k, w in enumerate(prepare(parts, logs, plv_ref, plc_ref, state, heads)):
        pw_ref[k // 2, k % 2] = w


def prepare_all(prompt_logdec, prompt_bc, branch_logdec, branch_bc, branch_channels):
    state = prompt_bc.shape[2]
    rows = BLOCK // CHUNK * state
    prompt_cuts = prompt_logdec.shape[0] * (prompt_logdec.shape[2] // BLOCK)
    branches, heads, positions = branch_logdec.shape
    branch_cuts = branches * (positions // BLOCK)
    half = prompt_logdec.shape[1] // 2
    shapes = [
        ((2 * heads, branch_channels), BF16),
        ((prompt_cuts, 2, 2 * BLOCK + 16, 2 * half), BF16),
        ((prompt_cuts, rows + BLOCK, BLOCK), BF16),
        ((prompt_cuts, BLOCK, rows), BF16),
        ((branch_cuts, 2 * BLOCK + 16, 2 * heads), BF16),
        ((branch_cuts, rows + BLOCK, BLOCK), BF16),
        ((branch_cuts, BLOCK, rows), BF16),
        ((branches, positions, heads * state), BF16),
    ]
    whole = pl.BlockSpec(memory_space=pltpu.VMEM)
    out = pl.pallas_call(
        functools.partial(prepare_kernel, width=branch_channels // heads),
        in_specs=[whole] * 4,
        out_specs=[pl.BlockSpec(shape, lambda rank=len(shape): (0,) * rank) for shape, _ in shapes],
        out_shape=[jax.ShapeDtypeStruct(*shape) for shape in shapes],
        compiler_params=pltpu.CompilerParams(vmem_limit_bytes=VMEM_LIMIT),
        cost_estimate=pl.CostEstimate(flops=10**8, bytes_accessed=10**6, transcendentals=0),
        name="prepare",
    )(prompt_logdec, prompt_bc, branch_logdec, branch_bc)
    return out[:4], (out[0], *out[4:7]), out[7]


def run_tiles(jobs):
    scaled, passed = {}, {}
    for g in range(len(jobs) + 2):
        if g < len(jobs):
            scaled[g] = jobs[g][0]()
        if 0 <= g - 1 < len(jobs):
            passed[g - 1] = jobs[g - 1][1](scaled.pop(g - 1))
        if 0 <= g - 2:
            jobs[g - 2][2](passed.pop(g - 2))


def tile_job(ready_refs, at, g, x_of, entering_of, leave, write):
    hot_ref, w_ref, lv_ref, lc_ref = ready_refs
    w_at, at = at
    rows = lc_ref.shape[2]
    chunks = BLOCK // CHUNK
    state = rows // chunks

    def scale():
        wide = jnp.dot(w_ref[w_at], hot_ref[:, pl.ds(g * 256, 256)], preferred_element_type=F32)
        scaled = (x_of().astype(F32) * wide[:BLOCK]).astype(BF16)
        return scaled, wide[BLOCK:BLOCK + 16], wide[BLOCK + 16:]

    def pass_on(given):
        scaled, steps, out_scale = given
        both = jnp.dot(lv_ref[at], scaled, preferred_element_type=F32)
        carries, carry = [], steps[0:1] * entering_of()
        for c in range(chunks):
            carries.append(carry.astype(BF16))
            carry = steps[c + 1:c + 2] * (carry + both[c * state:(c + 1) * state])
        leave(carry)
        return both[rows:], jnp.concatenate(carries, axis=0), out_scale

    def give(given):
        inner, carries, out_scale = given
        carried = jnp.dot(lc_ref[at], carries, preferred_element_type=F32)
        write((inner + carried) * out_scale)

    return scale, pass_on, give


class Copies:
    def __init__(self, sems):
        self.sems, self.started = sems, {}

    def start(self, key, source, target):
        copy = pltpu.make_async_copy(source, target, self.sems.at[key])
        copy.start()
        self.started[key] = copy

    def wait(self, key):
        self.started.pop(key).wait()

    def wait_all(self):
        for key in list(self.started):
            self.wait(key)


def branch_kernel(*refs, which, skip):
    x_in, ready = refs[0], refs[1:5]
    own_out, x_ref, own_ref, s_ref, in_sems, out_sems = refs[5 + skip:]
    positions, channels = x_ref.shape
    state = s_ref.shape[0]
    blocks = positions // BLOCK
    lanes = channels // in_sems.shape[1]
    came, left = Copies(in_sems), Copies(out_sems)

    def spot(b, j):
        return pl.ds(b * BLOCK, BLOCK), pl.ds(j * lanes, lanes)

    for b in range(blocks):
        for j in range(channels // lanes):
            came.start((b, j), x_in.at[(which, *spot(b, j))], x_ref.at[spot(b, j)])

    def job(b, g):
        cols = pl.ds(g * 256, 256)
        here = (pl.ds(b * BLOCK, BLOCK), cols)

        def x_of():
            if g * 256 % lanes == 0:
                came.wait((b, g * 256 // lanes))
            return x_ref[here]

        def leave(carry):
            if b < blocks - 1:
                s_ref[:, cols] = carry

        def write(out):
            own_ref[here] = out
            if (g + 1) * 256 % lanes == 0:
                j = g * 256 // lanes
                left.start((b, j), own_ref.at[spot(b, j)], own_out.at[(which, *spot(b, j))])

        def entering_of():
            return s_ref[:, cols] if b else jnp.zeros((state, 256), F32)

        at = which * blocks + b
        return tile_job(ready, (at, at), g, x_of, entering_of, leave, write)

    run_tiles([job(b, g) for b in range(blocks) for g in range(channels // 256)])
    left.wait_all()


def branch_own(x, ready, which, into):
    _, positions, channels = x.shape
    state = ready[3].shape[2] * CHUNK // BLOCK
    whole = pl.BlockSpec(memory_space=pltpu.VMEM)
    hbm = pl.BlockSpec(memory_space=pltpu.HBM)
    anywhere = pl.BlockSpec(memory_space=pl.ANY)
    parts = (positions // BLOCK, channels // min(512, channels))
    work = positions * channels
    return pl.pallas_call(
        functools.partial(branch_kernel, which=which, skip=len(into)),
        in_specs=[hbm] + [whole] * 4 + [anywhere] * len(into),
        out_specs=anywhere,
        out_shape=jax.ShapeDtypeStruct(x.shape, F32),
        scratch_shapes=[
            pltpu.VMEM((positions, channels), BF16),
            pltpu.VMEM((positions, channels), F32),
            pltpu.VMEM((state, channels), F32),
            pltpu.SemaphoreType.DMA(parts),
            pltpu.SemaphoreType.DMA(parts),
        ],
        input_output_aliases={5 + i: i for i in range(len(into))},
        compiler_params=pltpu.CompilerParams(vmem_limit_bytes=VMEM_LIMIT),
        cost_estimate=pl.CostEstimate(
            flops=2 * 1152 * work, bytes_accessed=4 * work, transcendentals=0),
        name="branch_own",
    )(in_hbm(x), *ready, *into)


def prompt_kernel(*refs, skip):
    half_ref, x_in, *ready, start_ref = refs[:7]
    y_out, x_ref, y_ref, in_sems, out_sems = refs[7 + skip:]
    count, positions, channels = y_ref.shape
    blocks = positions // BLOCK
    lanes = channels // in_sems.shape[2]
    half = half_ref[0]
    came, left = Copies(in_sems), Copies(out_sems)
    entered = {}

    def spots(i, b, j):
        there = pl.ds(pl.multiple_of(half * channels + j * lanes, lanes), lanes)
        rows = pl.ds(b * BLOCK, BLOCK)
        return (i, rows, there), (i, rows, pl.ds(j * lanes, lanes))

    for i in range(count):
        for b in range(blocks):
            for j in range(channels // lanes):
                there, here = spots(i, b, j)
                came.start((i, b, j), x_in.at[there], x_ref.at[here])

    def job(i, b, g):
        here = (i, pl.ds(b * BLOCK, BLOCK), pl.ds(g * 256, 256))
        j = g * 256 // lanes

        def x_of():
            if g * 256 % lanes == 0:
                came.wait((i, b, j))
            return x_ref[here]

        def leave(carry):
            entered[i, g] = carry

        def entering_of():
            return entered[i, g] if b else start_ref[i, :, pl.ds(g * 256, 256)]

        def write(out):
            y_ref[here] = out.astype(BF16)
            if (g + 1) * 256 % lanes == 0:
                there, staged = spots(i, b, j)
                left.start((i, b, j), y_ref.at[staged], y_out.at[there])

        at = i * blocks + b
        return tile_job(ready, ((at, half), at), g, x_of, entering_of, leave, write)

    run_tiles([job(i, b, g) for i in range(count) for b in range(blocks) for g in range(channels // 256)])
    left.wait_all()


def prompt_half(half, x, ready, start, into):
    count, positions, channels = x.shape
    part = channels // 2
    whole = pl.BlockSpec(memory_space=pltpu.VMEM)
    hbm = pl.BlockSpec(memory_space=pltpu.HBM)
    parts = (count, positions // BLOCK, part // min(512, part))
    work = count * positions * part
    return pl.pallas_call(
        functools.partial(prompt_kernel, skip=len(into)),
        in_specs=[pl.BlockSpec(memory_space=pltpu.SMEM), hbm] + [whole] * 5 + [hbm] * len(into),
        out_specs=hbm,
        out_shape=jax.ShapeDtypeStruct(x.shape, BF16),
        scratch_shapes=[
            pltpu.VMEM((count, positions, part), BF16),
            pltpu.VMEM((count, positions, part), BF16),
            pltpu.SemaphoreType.DMA(parts),
            pltpu.SemaphoreType.DMA(parts),
        ],
        input_output_aliases={7 + i: i for i in range(len(into))},
        compiler_params=pltpu.CompilerParams(vmem_limit_bytes=VMEM_LIMIT),
        cost_estimate=pl.CostEstimate(
            flops=2 * 1152 * work, bytes_accessed=4 * work, transcendentals=0),
        name="prompt_half",
    )(half, in_hbm(x), *ready, start, *into)


def finish_kernel(len_ref, own_ref, reach_ref, start_ref, y_out, y_ref, sems, *, width):
    count, positions, channels = y_ref.shape
    state = start_ref.shape[0]
    group = 128 // state
    span = group * width
    left = Copies(sems)
    own_head = quotient(iota((128, 1), 0), state) == quotient(iota((1, span), 1), width)
    starts = []
    for g in range(channels // span):
        start = jnp.concatenate([start_ref[:, pl.ds(g * span, span)]] * group, axis=0)
        starts.append(jnp.where(own_head, start, 0.0).astype(BF16))
    for i in range(count):
        for g in range(channels // span):
            for b in range(positions // BLOCK):
                rows, cols = pl.ds(b * BLOCK, BLOCK), pl.ds(g * span, span)
                term = jnp.dot(
                    reach_ref[i, rows, pl.ds(g * 128, 128)], starts[g], preferred_element_type=F32)
                live = iota((BLOCK, span), 0) < len_ref[i] - b * BLOCK
                y_ref[i, rows, cols] = jnp.where(live, own_ref[i, rows, cols] + term, 0.0).astype(BF16)
                left.start((i, b, g), y_ref.at[i, rows, cols], y_out.at[i, rows, cols])
    left.wait_all()


def finish(lengths, own, reach, start):
    count, positions, channels = own.shape
    state = start.shape[0]
    width = channels * state // reach.shape[2]
    whole = pl.BlockSpec(memory_space=pltpu.VMEM)
    return pl.pallas_call(
        functools.partial(finish_kernel, width=width),
        in_specs=[pl.BlockSpec(memory_space=pltpu.SMEM), whole, whole, whole],
        out_specs=pl.BlockSpec(memory_space=pltpu.HBM),
        out_shape=jax.ShapeDtypeStruct(own.shape, BF16),
        scratch_shapes=[
            pltpu.VMEM(own.shape, BF16),
            pltpu.SemaphoreType.DMA((count, positions // BLOCK, reach.shape[2] // 128)),
        ],
        compiler_params=pltpu.CompilerParams(vmem_limit_bytes=VMEM_LIMIT),
        cost_estimate=pl.CostEstimate(
            flops=2 * 128 * own.size, bytes_accessed=6 * own.size, transcendentals=0),
        name="branch_finish",
    )(lengths, own, reach, start)


def swap_bit(value, bit, size):
    return lax.ppermute(value, "ctx", [(k, k ^ bit) for k in range(size)])


def pack(states, logs):
    lanes = states.shape[-1]
    return jnp.concatenate([states.reshape(-1, lanes), logs.reshape(-1, lanes)], axis=0)


def unpack(packed, count):
    lanes = packed.shape[-1]
    rows = packed.shape[0] - count
    return packed[:rows].reshape(count, rows // count, lanes), packed[rows:].reshape(count, 1, lanes)


def in_order(upper, mine, other):
    first = [jnp.where(upper, o, m) for m, o in zip(mine, other)]
    second = [jnp.where(upper, m, o) for m, o in zip(mine, other)]
    return first, second


def join(first, second):
    return jnp.exp(second[1]) * first[0] + second[0], first[1] + second[1]


def spread_step(value, hop, ctx_size, pair_size):
    owner = lax.axis_index("ctx") * pair_size // ctx_size
    known = [m for m in range(pair_size) if m & (2 * hop - 1) == 0]
    links = []
    for k in range(ctx_size):
        z = k * pair_size // ctx_size
        links += [(k * pair_size + (z ^ m), k * pair_size + (z ^ m ^ hop)) for m in known]
    got = lax.ppermute(value, ("ctx", "pair"), links)
    has = ((lax.axis_index("pair") ^ owner) & (2 * hop - 1)) == 0
    return got, has


def body(
    prompt_x,
    prompt_bc,
    prompt_logdec,
    branch_x,
    branch_bc,
    branch_logdec,
    branch_prompt,
    branch_len,
):
    size, pair_size = lax.axis_size("ctx"), lax.axis_size("pair")
    prompts, branches = prompt_x.shape[0], branch_x.shape[0]
    assert size == 2 * pair_size and size & (size - 1) == 0 and branch_prompt.shape[0] == 1
    mine = lax.axis_index("ctx")
    odd = (mine & 1) == 1

    def beside(exchange, value, work, *given):
        value, given = lax.optimization_barrier((value, given))
        got = exchange(value)
        return lax.optimization_barrier((got, work(*given)))

    end, log = local_ends(prompt_x, prompt_logdec, prompt_bc)
    half = end.shape[2] // 2
    low, high = (end[:, :, :half], log[:, :1, :half]), (end[:, :, half:], log[:, :1, half:])
    keep = [jnp.where(odd, h, l) for l, h in zip(low, high)]
    send = [jnp.where(odd, l, h) for l, h in zip(low, high)]
    got, (prompt_ready, branch_ready, reach) = beside(
        lambda v: swap_bit(v, 1, size),
        pack(*send),
        lambda ld: prepare_all(prompt_logdec, prompt_bc, ld, branch_bc, branch_x.shape[2]),
        branch_logdec,
    )
    got = unpack(got, prompts)
    first, second = in_order(odd, keep, got)
    total, total_log = join(first, second)
    before, before_log = jnp.zeros_like(total), jnp.zeros_like(total_log)

    own = ()
    works = iter(range(branches))
    bit = 2
    while bit < size:
        which = next(works, None)
        swap = functools.partial(swap_bit, bit=bit, size=size)
        if which is None:
            got = swap(pack(total, total_log))
        else:
            got, own = beside(
                swap, pack(total, total_log),
                lambda x, own: (branch_own(x, branch_ready, which, own),), branch_x, own)
        other = unpack(got, prompts)
        upper = (mine & bit) != 0
        before = jnp.where(upper, jnp.exp(before_log) * other[0] + before, before)
        before_log = jnp.where(upper, before_log + other[1], before_log)
        total, total_log = join(*in_order(upper, (total, total_log), other))
        bit *= 2
    for which in works:
        own = (branch_own(branch_x, branch_ready, which, own),)

    next_before = jnp.exp(first[1]) * before + first[0]
    keep = jnp.where(odd, next_before, before)
    others = swap_bit(jnp.where(odd, before, next_before), 1, size)
    here = jnp.reshape(mine & 1, (1,))
    sides = [(here, keep), (1 - here, others)]
    prompt_y = ()
    hop = pair_size // 2
    while hop:
        step = functools.partial(spread_step, hop=hop, ctx_size=size, pair_size=pair_size)
        if sides:
            side, entering = sides.pop(0)
            (got, has), prompt_y = beside(
                step, total,
                lambda entering, y: (prompt_half(side, prompt_x, prompt_ready, entering, y),), entering, prompt_y)
        else:
            got, has = step(total)
        total = jnp.where(has, total, got)
        hop //= 2
    for side, entering in sides:
        prompt_y = (prompt_half(side, prompt_x, prompt_ready, entering, prompt_y),)
    start = total[0]
    for which in range(1, prompts):
        start = jnp.where(branch_prompt[0] == which, total[which], start)
    branch_y = finish(branch_len, *own, reach, start)
    return prompt_y[0], branch_y


def solution(mesh):
    return jax.shard_map(
        body,
        mesh=mesh,
        in_specs=(
            P(None, "ctx", "pair"),
            P(None, None, None, "ctx"),
            P(None, "pair", "ctx"),
            P("pair", None, "ctx"),
            P(None, "pair", None, None),
            P("pair", "ctx", None),
            P("pair"),
            P("pair"),
        ),
        out_specs=(P(None, "ctx", "pair"), P("pair", None, "ctx")),
        check_vma=False,
    )
```

```python
import functools
import jax
import jax.numpy as jnp
from jax import lax
from jax.experimental import pallas as pl
from jax.experimental.pallas import tpu as pltpu
from jax.sharding import PartitionSpec as P

BLOCK = 256
CHUNK = 32
F32 = jnp.float32
BF16 = jnp.bfloat16
VMEM_LIMIT = 16 * 1024 * 1024


def iota(shape, dim):
    return lax.broadcasted_iota(jnp.int32, shape, dim)


def quotient(index, divisor):
    if divisor & (divisor - 1) == 0:
        return lax.shift_right_logical(index, divisor.bit_length() - 1)
    return lax.div(index, divisor)


def remainder(index, divisor):
    if divisor & (divisor - 1) == 0:
        return index & (divisor - 1)
    return lax.rem(index, divisor)


def exact_dot(a, b):
    return jnp.dot(a, b, preferred_element_type=F32, precision=lax.Precision.HIGHEST)


def gain_of(log_decay):
    z = 2.0 * log_decay
    series = 1.0 + z * (1.0 / 9.0)
    for k in (8, 7, 6, 5, 4, 3, 2):
        series = 1.0 + z * (1.0 / k) * series
    small = -z * series
    large = 1.0 - jnp.exp(z)
    return jnp.sqrt(jnp.maximum(jnp.where(z > -0.5, small, large), 0.0))


def hi_lo(value):
    high = value.astype(BF16).astype(F32)
    return jnp.concatenate([high, value - high], axis=0)


def in_hbm(array):
    return pltpu.with_memory_space_constraint(array, pltpu.HBM)


def split_dot(rows, one_hot):
    count = rows.shape[0]
    high = rows.astype(BF16).astype(F32)
    middle = (rows - high).astype(BF16).astype(F32)
    parts = jnp.concatenate([high, middle, rows - high - middle], axis=0).astype(BF16)
    out = jnp.dot(parts, one_hot, preferred_element_type=F32)
    return out[:count] + out[count:2 * count] + out[2 * count:]


def ends_kernel(
    x_ref, ld_in, bc_in, end_ref, log_ref, held_ref, ld_ref, b_ref, push_ref, sems, first_sems, *, width, lanes
):
    first_copies = [
        pltpu.make_async_copy(ld_in, ld_ref, first_sems.at[0]),
        pltpu.make_async_copy(bc_in.at[0], b_ref, first_sems.at[1]),
    ]
    for copy in first_copies:
        copy.start()
    count, heads, positions = ld_ref.shape
    state = end_ref.shape[1]
    channels = end_ref.shape[2]
    tiles = channels // lanes
    copies = {}
    for i in range(count):
        for j in range(tiles):
            cols = pl.ds(j * lanes, lanes)
            copies[i, j] = pltpu.make_async_copy(
                x_ref.at[i, :, cols], held_ref.at[i, :, cols], sems.at[i, j])
            copies[i, j].start()
    for copy in first_copies:
        copy.wait()
    logs = jnp.concatenate([ld_ref[i] for i in range(count)], axis=0)
    after = jnp.where(iota((positions, 1), 0) > iota((1, positions), 1), 1.0, 0.0)
    to_end = jnp.exp(exact_dot(logs, after)) * gain_of(logs)
    for i in range(count):
        b_rows = b_ref[i].astype(F32)
        push = b_rows[None, :, :] * to_end[i * heads:(i + 1) * heads][:, None, :]
        push_ref[i] = push.reshape(heads * state, positions).astype(BF16)
    group = 256 // width
    lane_head = quotient(iota((1, 256), 1), width)
    for i in range(count):
        totals = lax.dot_general(
            jnp.ones((16, positions), F32), ld_ref[i], (((1,), (1,)), ((), ())),
            preferred_element_type=F32, precision=lax.Precision.HIGHEST)
        for j in range(tiles):
            cols = pl.ds(j * lanes, lanes)
            pick = iota((heads, 1), 0) == quotient(iota((1, lanes), 1), width) + j * (lanes // width)
            log_ref[i, :, cols] = split_dot(totals, jnp.where(pick, 1.0, 0.0).astype(BF16))[:8]
    for i in range(count):
        for j in range(tiles):
            copies[i, j].wait()
            for g in range(lanes // 256):
                first = j * (lanes // width) + g * group
                cols = pl.ds(j * lanes + g * 256, 256)
                both = jnp.dot(
                    push_ref[i, pl.ds(first * state, group * state), :], held_ref[i, :, cols],
                    preferred_element_type=F32)
                end = jnp.where(lane_head == 0, both[:state], 0.0)
                for k in range(1, group):
                    end = jnp.where(lane_head == k, both[k * state:(k + 1) * state], end)
                end_ref[i, :, cols] = end


def local_ends(x, logdec, bc):
    count, positions, channels = x.shape
    heads, state = logdec.shape[1], bc.shape[2]
    width = channels // heads
    lanes = min(1024, channels)
    whole = pl.BlockSpec(memory_space=pltpu.VMEM)
    return pl.pallas_call(
        functools.partial(ends_kernel, width=width, lanes=lanes),
        in_specs=[pl.BlockSpec(memory_space=pltpu.HBM)] * 3,
        out_specs=[whole, whole],
        out_shape=[
            jax.ShapeDtypeStruct((count, state, channels), F32),
            jax.ShapeDtypeStruct((count, 8, channels), F32),
        ],
        scratch_shapes=[
            pltpu.VMEM(x.shape, BF16),
            pltpu.VMEM(logdec.shape, F32),
            pltpu.VMEM(bc.shape[1:], BF16),
            pltpu.VMEM((count, heads * state, positions), BF16),
            pltpu.SemaphoreType.DMA((count, channels // lanes)),
            pltpu.SemaphoreType.DMA((2,)),
        ],
        compiler_params=pltpu.CompilerParams(vmem_limit_bytes=VMEM_LIMIT),
        cost_estimate=pl.CostEstimate(
            flops=2 * 64 * x.size, bytes_accessed=2 * x.size, transcendentals=0),
        name="local_ends",
    )(in_hbm(x), in_hbm(logdec), in_hbm(bc))


def prepare(parts, logs, lv_ref, lc_ref, state, heads):
    size = logs.shape[1]
    chunks = size // CHUNK
    half = CHUNK // 2
    src, dst = iota((size, 1), 0), iota((1, size), 1)
    middle = quotient(dst, CHUNK) * CHUNK + half - 1
    plus = (src > middle) & (src <= dst)
    minus = (src > dst) & (src <= middle)
    offset = exact_dot(logs, jnp.where(plus, 1.0, jnp.where(minus, -1.0, 0.0)))
    row_scale = jnp.exp(offset)
    in_scale = jnp.exp(-offset) * gain_of(logs)
    span = iota((1, 128), 1) == quotient(src + half, CHUNK)
    steps = jnp.exp(exact_dot(logs, jnp.where(span, 1.0, 0.0)))
    rows = state * chunks
    mine = quotient(iota((rows, 1), 0), state) == quotient(dst, CHUNK)
    keep = (dst <= src) & (quotient(dst, CHUNK) == quotient(src, CHUNK))
    for i, (b_rows, c_rows) in enumerate(parts):
        b_all = jnp.concatenate([b_rows.astype(F32)] * chunks, axis=0)
        lv_ref[i, pl.ds(0, rows), :] = jnp.where(mine, b_all, 0.0).astype(BF16)
        scores = lax.dot_general(c_rows, b_rows, (((0,), (0,)), ((), ())), preferred_element_type=F32)
        lv_ref[i, pl.ds(rows, size), :] = jnp.where(keep, scores, 0.0).astype(BF16)
        c_all = jnp.concatenate([c_rows.astype(F32)] * chunks, axis=0)
        lc_ref[i] = jnp.where(mine, c_all, 0.0).T.astype(BF16)
    scales = []
    for first in range(0, logs.shape[0], heads):
        here = slice(first, first + heads)
        columns = [hi_lo(in_scale[here]).T, hi_lo(steps[here]).T[:16], hi_lo(row_scale[here]).T]
        scales.append(jnp.concatenate(columns, axis=0).astype(BF16))
    return scales


def cuts_of(ld_ref):
    count, _, positions = ld_ref.shape
    return [(i, pl.ds(b * BLOCK, BLOCK)) for i in range(count) for b in range(positions // BLOCK)]


def prepare_kernel(
    pld_ref, pbc_ref, bld_ref, bbc_ref,
    hot_ref, pw_ref, plv_ref, plc_ref, bw_ref, blv_ref, blc_ref, reach_ref, *, width
):
    state = pbc_ref.shape[2]

    def collect(ld_ref, bc_ref):
        cuts = cuts_of(ld_ref)
        logs = jnp.concatenate([ld_ref[i, :, cut] for i, cut in cuts], axis=0)
        return cuts, logs, [(bc_ref[0, i, :, cut], bc_ref[1, i, :, cut]) for i, cut in cuts]

    cuts, logs, parts = collect(bld_ref, bbc_ref)
    heads = bld_ref.shape[1]
    blocks = len(cuts) // bld_ref.shape[0]
    for k, w in enumerate(prepare(parts, logs, blv_ref, blc_ref, state, heads)):
        bw_ref[k] = w
    row_head = remainder(iota((2 * heads, 1), 0), heads)
    for g in range(hot_ref.shape[1] // 256):
        lane_head = quotient(iota((1, 256), 1), width) + g * (256 // width)
        hot_ref[:, pl.ds(g * 256, 256)] = jnp.where(row_head == lane_head, 1.0, 0.0).astype(BF16)
    upto = jnp.where(iota((BLOCK, 1), 0) <= iota((1, BLOCK), 1), 1.0, 0.0)
    runs = exact_dot(logs, upto)
    for k, (i, cut) in enumerate(cuts):
        run = runs[k * heads:(k + 1) * heads]
        if k % blocks:
            run = run + entered
        entered = run[:, BLOCK - 1:BLOCK]
        reach = parts[k][1].astype(F32)[None, :, :] * jnp.exp(run)[:, None, :]
        reach_ref[i, cut, :] = reach.reshape(heads * state, BLOCK).T.astype(BF16)

    cuts, logs, parts = collect(pld_ref, pbc_ref)
    heads = pld_ref.shape[1] // 2
    for k, w in enumerate(prepare(parts, logs, plv_ref, plc_ref, state, heads)):
        pw_ref[k // 2, k % 2] = w


def prepare_all(prompt_logdec, prompt_bc, branch_logdec, branch_bc, branch_channels):
    state = prompt_bc.shape[2]
    rows = BLOCK // CHUNK * state
    prompt_cuts = prompt_logdec.shape[0] * (prompt_logdec.shape[2] // BLOCK)
    branches, heads, positions = branch_logdec.shape
    branch_cuts = branches * (positions // BLOCK)
    half = prompt_logdec.shape[1] // 2
    shapes = [
        ((2 * heads, branch_channels), BF16),
        ((prompt_cuts, 2, 2 * BLOCK + 16, 2 * half), BF16),
        ((prompt_cuts, rows + BLOCK, BLOCK), BF16),
        ((prompt_cuts, BLOCK, rows), BF16),
        ((branch_cuts, 2 * BLOCK + 16, 2 * heads), BF16),
        ((branch_cuts, rows + BLOCK, BLOCK), BF16),
        ((branch_cuts, BLOCK, rows), BF16),
        ((branches, positions, heads * state), BF16),
    ]
    whole = pl.BlockSpec(memory_space=pltpu.VMEM)
    out = pl.pallas_call(
        functools.partial(prepare_kernel, width=branch_channels // heads),
        in_specs=[whole] * 4,
        out_specs=[pl.BlockSpec(shape, lambda rank=len(shape): (0,) * rank) for shape, _ in shapes],
        out_shape=[jax.ShapeDtypeStruct(*shape) for shape in shapes],
        compiler_params=pltpu.CompilerParams(vmem_limit_bytes=VMEM_LIMIT),
        cost_estimate=pl.CostEstimate(flops=10**8, bytes_accessed=10**6, transcendentals=0),
        name="prepare",
    )(prompt_logdec, prompt_bc, branch_logdec, branch_bc)
    return out[:4], (out[0], *out[4:7]), out[7]


def run_tiles(jobs):
    scaled, passed = {}, {}
    for g in range(len(jobs) + 2):
        if g < len(jobs):
            scaled[g] = jobs[g][0]()
        if 0 <= g - 1 < len(jobs):
            passed[g - 1] = jobs[g - 1][1](scaled.pop(g - 1))
        if 0 <= g - 2:
            jobs[g - 2][2](passed.pop(g - 2))


def tile_job(ready_refs, at, g, x_of, entering_of, leave, write):
    hot_ref, w_ref, lv_ref, lc_ref = ready_refs
    w_at, at = at
    rows = lc_ref.shape[2]
    chunks = BLOCK // CHUNK
    state = rows // chunks

    def scale():
        wide = jnp.dot(w_ref[w_at], hot_ref[:, pl.ds(g * 256, 256)], preferred_element_type=F32)
        scaled = (x_of().astype(F32) * wide[:BLOCK]).astype(BF16)
        return scaled, wide[BLOCK:BLOCK + 16], wide[BLOCK + 16:]

    def pass_on(given):
        scaled, steps, out_scale = given
        both = jnp.dot(lv_ref[at], scaled, preferred_element_type=F32)
        carries, carry = [], steps[0:1] * entering_of()
        for c in range(chunks):
            carries.append(carry.astype(BF16))
            carry = steps[c + 1:c + 2] * (carry + both[c * state:(c + 1) * state])
        leave(carry)
        return both[rows:], jnp.concatenate(carries, axis=0), out_scale

    def give(given):
        inner, carries, out_scale = given
        carried = jnp.dot(lc_ref[at], carries, preferred_element_type=F32)
        write((inner + carried) * out_scale)

    return scale, pass_on, give


class Copies:
    def __init__(self, sems):
        self.sems, self.started = sems, {}

    def start(self, key, source, target):
        copy = pltpu.make_async_copy(source, target, self.sems.at[key])
        copy.start()
        self.started[key] = copy

    def wait(self, key):
        self.started.pop(key).wait()

    def wait_all(self):
        for key in list(self.started):
            self.wait(key)


def branch_kernel(x_in, *refs, which):
    ready = refs[:4]
    own_ref, x_ref, s_ref, in_sems = refs[4:]
    positions, channels = x_ref.shape
    state = s_ref.shape[0]
    blocks = positions // BLOCK
    lanes = channels // in_sems.shape[1]
    came = Copies(in_sems)
    for b in range(blocks):
        for j in range(channels // lanes):
            spot = (pl.ds(b * BLOCK, BLOCK), pl.ds(j * lanes, lanes))
            came.start((b, j), x_in.at[(which, *spot)], x_ref.at[spot])

    def job(b, g):
        cols = pl.ds(g * 256, 256)
        here = (pl.ds(b * BLOCK, BLOCK), cols)

        def x_of():
            if g * 256 % lanes == 0:
                came.wait((b, g * 256 // lanes))
            return x_ref[here]

        def leave(carry):
            if b < blocks - 1:
                s_ref[:, cols] = carry

        def write(out):
            own_ref[here] = out

        def entering_of():
            return s_ref[:, cols] if b else jnp.zeros((state, 256), F32)

        at = which * blocks + b
        return tile_job(ready, (at, at), g, x_of, entering_of, leave, write)

    run_tiles([job(b, g) for b in range(blocks) for g in range(channels // 256)])


def branch_own(x, ready, which):
    _, positions, channels = x.shape
    state = ready[3].shape[2] * CHUNK // BLOCK
    whole = pl.BlockSpec(memory_space=pltpu.VMEM)
    work = positions * channels
    return pl.pallas_call(
        functools.partial(branch_kernel, which=which),
        in_specs=[pl.BlockSpec(memory_space=pltpu.HBM)] + [whole] * 4,
        out_specs=whole,
        out_shape=jax.ShapeDtypeStruct(x.shape[1:], F32),
        scratch_shapes=[
            pltpu.VMEM((positions, channels), BF16),
            pltpu.VMEM((state, channels), F32),
            pltpu.SemaphoreType.DMA((positions // BLOCK, channels // min(512, channels))),
        ],
        compiler_params=pltpu.CompilerParams(vmem_limit_bytes=VMEM_LIMIT),
        cost_estimate=pl.CostEstimate(
            flops=2 * 1152 * work, bytes_accessed=4 * work, transcendentals=0),
        name="branch_own",
    )(in_hbm(x), *ready)


def prompt_kernel(*refs, skip):
    half_ref, x_in, *ready, start_ref = refs[:7]
    y_out, x_ref, in_sems, out_sems = refs[7 + skip:]
    count, positions, channels = x_ref.shape
    blocks = positions // BLOCK
    lanes = channels // in_sems.shape[2]
    half = half_ref[0]
    came, left = Copies(in_sems), Copies(out_sems)
    entered = {}

    def spots(i, b, j):
        there = pl.ds(pl.multiple_of(half * channels + j * lanes, lanes), lanes)
        rows = pl.ds(b * BLOCK, BLOCK)
        return (i, rows, there), (i, rows, pl.ds(j * lanes, lanes))

    for i in range(count):
        for b in range(blocks):
            for j in range(channels // lanes):
                there, here = spots(i, b, j)
                came.start((i, b, j), x_in.at[there], x_ref.at[here])

    def job(i, b, g):
        here = (i, pl.ds(b * BLOCK, BLOCK), pl.ds(g * 256, 256))
        j = g * 256 // lanes

        def x_of():
            if g * 256 % lanes == 0:
                came.wait((i, b, j))
            return x_ref[here]

        def leave(carry):
            entered[i, g] = carry

        def entering_of():
            return entered[i, g] if b else start_ref[i, :, pl.ds(g * 256, 256)]

        def write(out):
            x_ref[here] = out.astype(BF16)
            if (g + 1) * 256 % lanes == 0:
                there, staged = spots(i, b, j)
                left.start((i, b, j), x_ref.at[staged], y_out.at[there])

        at = i * blocks + b
        return tile_job(ready, ((at, half), at), g, x_of, entering_of, leave, write)

    run_tiles([job(i, b, g) for i in range(count) for b in range(blocks) for g in range(channels // 256)])
    left.wait_all()


def prompt_half(half, x, ready, start, into):
    count, positions, channels = x.shape
    part = channels // 2
    whole = pl.BlockSpec(memory_space=pltpu.VMEM)
    hbm = pl.BlockSpec(memory_space=pltpu.HBM)
    parts = (count, positions // BLOCK, part // min(512, part))
    work = count * positions * part
    return pl.pallas_call(
        functools.partial(prompt_kernel, skip=len(into)),
        in_specs=[pl.BlockSpec(memory_space=pltpu.SMEM), hbm] + [whole] * 5 + [hbm] * len(into),
        out_specs=hbm,
        out_shape=jax.ShapeDtypeStruct(x.shape, BF16),
        scratch_shapes=[
            pltpu.VMEM((count, positions, part), BF16),
            pltpu.SemaphoreType.DMA(parts),
            pltpu.SemaphoreType.DMA(parts),
        ],
        input_output_aliases={7 + i: i for i in range(len(into))},
        compiler_params=pltpu.CompilerParams(vmem_limit_bytes=VMEM_LIMIT),
        cost_estimate=pl.CostEstimate(
            flops=2 * 1152 * work, bytes_accessed=4 * work, transcendentals=0),
        name="prompt_half",
    )(half, in_hbm(x), *ready, start, *into)


def finish_kernel(len_ref, reach_ref, start_ref, *refs, width):
    own_refs, (y_out, y_ref, sems) = refs[:-3], refs[-3:]
    count, positions, channels = y_ref.shape
    state = start_ref.shape[0]
    group = 128 // state
    span = group * width
    left = Copies(sems)
    own_head = quotient(iota((128, 1), 0), state) == quotient(iota((1, span), 1), width)
    starts = []
    for g in range(channels // span):
        start = jnp.concatenate([start_ref[:, pl.ds(g * span, span)]] * group, axis=0)
        starts.append(jnp.where(own_head, start, 0.0).astype(BF16))
    for i in range(count):
        for g in range(channels // span):
            for b in range(positions // BLOCK):
                rows, cols = pl.ds(b * BLOCK, BLOCK), pl.ds(g * span, span)
                term = jnp.dot(
                    reach_ref[i, rows, pl.ds(g * 128, 128)], starts[g], preferred_element_type=F32)
                live = iota((BLOCK, span), 0) < len_ref[i] - b * BLOCK
                y_ref[i, rows, cols] = jnp.where(live, own_refs[i][rows, cols] + term, 0.0).astype(BF16)
                left.start((i, b, g), y_ref.at[i, rows, cols], y_out.at[i, rows, cols])
    left.wait_all()


def finish(lengths, reach, start, own):
    count, (positions, channels) = len(own), own[0].shape
    state = start.shape[0]
    width = channels * state // reach.shape[2]
    whole = pl.BlockSpec(memory_space=pltpu.VMEM)
    return pl.pallas_call(
        functools.partial(finish_kernel, width=width),
        in_specs=[pl.BlockSpec(memory_space=pltpu.SMEM)] + [whole] * (2 + count),
        out_specs=pl.BlockSpec(memory_space=pltpu.HBM),
        out_shape=jax.ShapeDtypeStruct((count, positions, channels), BF16),
        scratch_shapes=[
            pltpu.VMEM((count, positions, channels), BF16),
            pltpu.SemaphoreType.DMA((count, positions // BLOCK, reach.shape[2] // 128)),
        ],
        compiler_params=pltpu.CompilerParams(vmem_limit_bytes=VMEM_LIMIT),
        cost_estimate=pl.CostEstimate(
            flops=2**28, bytes_accessed=2**23, transcendentals=0),
        name="branch_finish",
    )(lengths, reach, start, *own)


def swap_bit(value, bit, size):
    return lax.ppermute(value, "ctx", [(k, k ^ bit) for k in range(size)])


def pack(states, logs):
    lanes = states.shape[-1]
    return jnp.concatenate([states.reshape(-1, lanes), logs.reshape(-1, lanes)], axis=0)


def unpack(packed, count):
    lanes = packed.shape[-1]
    rows = packed.shape[0] - count
    return packed[:rows].reshape(count, rows // count, lanes), packed[rows:].reshape(count, 1, lanes)


def in_order(upper, mine, other):
    first = [jnp.where(upper, o, m) for m, o in zip(mine, other)]
    second = [jnp.where(upper, m, o) for m, o in zip(mine, other)]
    return first, second


def join(first, second):
    return jnp.exp(second[1]) * first[0] + second[0], first[1] + second[1]


def spread_step(value, hop, ctx_size, pair_size):
    owner = lax.axis_index("ctx") * pair_size // ctx_size
    known = [m for m in range(pair_size) if m & (2 * hop - 1) == 0]
    links = []
    for k in range(ctx_size):
        z = k * pair_size // ctx_size
        links += [(k * pair_size + (z ^ m), k * pair_size + (z ^ m ^ hop)) for m in known]
    got = lax.ppermute(value, ("ctx", "pair"), links)
    has = ((lax.axis_index("pair") ^ owner) & (2 * hop - 1)) == 0
    return got, has


def body(
    prompt_x,
    prompt_bc,
    prompt_logdec,
    branch_x,
    branch_bc,
    branch_logdec,
    branch_prompt,
    branch_len,
):
    size, pair_size = lax.axis_size("ctx"), lax.axis_size("pair")
    prompts, branches = prompt_x.shape[0], branch_x.shape[0]
    assert size == 2 * pair_size and size & (size - 1) == 0 and branch_prompt.shape[0] == 1
    mine = lax.axis_index("ctx")
    odd = (mine & 1) == 1

    def beside(exchange, value, work, *given):
        value, given = lax.optimization_barrier((value, given))
        got = exchange(value)
        return lax.optimization_barrier((got, work(*given)))

    end, log = local_ends(prompt_x, prompt_logdec, prompt_bc)
    half = end.shape[2] // 2
    low, high = (end[:, :, :half], log[:, :1, :half]), (end[:, :, half:], log[:, :1, half:])
    keep = [jnp.where(odd, h, l) for l, h in zip(low, high)]
    send = [jnp.where(odd, l, h) for l, h in zip(low, high)]
    got, (prompt_ready, branch_ready, reach) = beside(
        lambda v: swap_bit(v, 1, size),
        pack(*send),
        lambda ld: prepare_all(prompt_logdec, prompt_bc, ld, branch_bc, branch_x.shape[2]),
        branch_logdec,
    )
    got = unpack(got, prompts)
    first, second = in_order(odd, keep, got)
    total, total_log = join(first, second)
    before, before_log = jnp.zeros_like(total), jnp.zeros_like(total_log)

    own = ()
    works = iter(range(branches))
    bit = 2
    while bit < size:
        which = next(works, None)
        swap = functools.partial(swap_bit, bit=bit, size=size)
        if which is None:
            got = swap(pack(total, total_log))
        else:
            got, own = beside(
                swap, pack(total, total_log),
                lambda x, own: (*own, branch_own(x, branch_ready, which)), branch_x, own)
        other = unpack(got, prompts)
        upper = (mine & bit) != 0
        before = jnp.where(upper, jnp.exp(before_log) * other[0] + before, before)
        before_log = jnp.where(upper, before_log + other[1], before_log)
        total, total_log = join(*in_order(upper, (total, total_log), other))
        bit *= 2
    for which in works:
        own = (*own, branch_own(branch_x, branch_ready, which))

    next_before = jnp.exp(first[1]) * before + first[0]
    keep = jnp.where(odd, next_before, before)
    others = swap_bit(jnp.where(odd, before, next_before), 1, size)
    here = jnp.reshape(mine & 1, (1,))
    sides = [(here, keep), (1 - here, others)]
    prompt_y = ()
    hop = pair_size // 2
    while hop:
        step = functools.partial(spread_step, hop=hop, ctx_size=size, pair_size=pair_size)
        if sides:
            side, entering = sides.pop(0)
            (got, has), prompt_y = beside(
                step, total,
                lambda entering, y: (prompt_half(side, prompt_x, prompt_ready, entering, y),), entering, prompt_y)
        else:
            got, has = step(total)
        total = jnp.where(has, total, got)
        hop //= 2
    for side, entering in sides:
        prompt_y = (prompt_half(side, prompt_x, prompt_ready, entering, prompt_y),)
    start = total[0]
    for which in range(1, prompts):
        start = jnp.where(branch_prompt[0] == which, total[which], start)
    branch_y = finish(branch_len, reach, start, own)
    return prompt_y[0], branch_y


def solution(mesh):
    return jax.shard_map(
        body,
        mesh=mesh,
        in_specs=(
            P(None, "ctx", "pair"),
            P(None, None, None, "ctx"),
            P(None, "pair", "ctx"),
            P("pair", None, "ctx"),
            P(None, "pair", None, None),
            P("pair", "ctx", None),
            P("pair"),
            P("pair"),
        ),
        out_specs=(P(None, "ctx", "pair"), P("pair", None, "ctx")),
        check_vma=False,
    )
```

```python
import functools
import jax
import jax.numpy as jnp
from jax import lax
from jax.experimental import pallas as pl
from jax.experimental.pallas import tpu as pltpu
from jax.sharding import PartitionSpec as P

BLOCK = 256
CHUNK = 32
F32 = jnp.float32
BF16 = jnp.bfloat16
VMEM_LIMIT = 16 * 1024 * 1024


def iota(shape, dim):
    return lax.broadcasted_iota(jnp.int32, shape, dim)


def quotient(index, divisor):
    if divisor & (divisor - 1) == 0:
        return lax.shift_right_logical(index, divisor.bit_length() - 1)
    return lax.div(index, divisor)


def remainder(index, divisor):
    if divisor & (divisor - 1) == 0:
        return index & (divisor - 1)
    return lax.rem(index, divisor)


def exact_dot(a, b):
    return jnp.dot(a, b, preferred_element_type=F32, precision=lax.Precision.HIGHEST)


def gain_of(log_decay):
    z = 2.0 * log_decay
    series = 1.0 + z * (1.0 / 9.0)
    for k in (8, 7, 6, 5, 4, 3, 2):
        series = 1.0 + z * (1.0 / k) * series
    small = -z * series
    large = 1.0 - jnp.exp(z)
    return jnp.sqrt(jnp.maximum(jnp.where(z > -0.5, small, large), 0.0))


def hi_lo(value):
    high = value.astype(BF16).astype(F32)
    return jnp.concatenate([high, value - high], axis=0)


def in_hbm(array):
    return pltpu.with_memory_space_constraint(array, pltpu.HBM)


def split_dot(rows, one_hot):
    count = rows.shape[0]
    high = rows.astype(BF16).astype(F32)
    middle = (rows - high).astype(BF16).astype(F32)
    parts = jnp.concatenate([high, middle, rows - high - middle], axis=0).astype(BF16)
    out = jnp.dot(parts, one_hot, preferred_element_type=F32)
    return out[:count] + out[count:2 * count] + out[2 * count:]


def ends_kernel(
    x_ref, ld_in, bc_in, end_ref, log_ref, held_ref, ld_ref, b_ref, push_ref, sems, first_sems, *, width, lanes
):
    first_copies = [
        pltpu.make_async_copy(ld_in, ld_ref, first_sems.at[0]),
        pltpu.make_async_copy(bc_in.at[0], b_ref, first_sems.at[1]),
    ]
    for copy in first_copies:
        copy.start()
    count, heads, positions = ld_ref.shape
    state = end_ref.shape[1]
    channels = end_ref.shape[2]
    tiles = channels // lanes
    copies = {}
    for i in range(count):
        for j in range(tiles):
            cols = pl.ds(j * lanes, lanes)
            copies[i, j] = pltpu.make_async_copy(
                x_ref.at[i, :, cols], held_ref.at[i, :, cols], sems.at[i, j])
            copies[i, j].start()
    for copy in first_copies:
        copy.wait()
    logs = jnp.concatenate([ld_ref[i] for i in range(count)], axis=0)
    after = jnp.where(iota((positions, 1), 0) > iota((1, positions), 1), 1.0, 0.0)
    to_end = jnp.exp(exact_dot(logs, after)) * gain_of(logs)
    for i in range(count):
        b_rows = b_ref[i].astype(F32)
        push = b_rows[None, :, :] * to_end[i * heads:(i + 1) * heads][:, None, :]
        push_ref[i] = push.reshape(heads * state, positions).astype(BF16)
    group = 256 // width
    lane_head = quotient(iota((1, 256), 1), width)
    for i in range(count):
        totals = lax.dot_general(
            jnp.ones((16, positions), F32), ld_ref[i], (((1,), (1,)), ((), ())),
            preferred_element_type=F32, precision=lax.Precision.HIGHEST)
        for j in range(tiles):
            cols = pl.ds(j * lanes, lanes)
            pick = iota((heads, 1), 0) == quotient(iota((1, lanes), 1), width) + j * (lanes // width)
            log_ref[i, :, cols] = split_dot(totals, jnp.where(pick, 1.0, 0.0).astype(BF16))[:8]
    for i in range(count):
        for j in range(tiles):
            copies[i, j].wait()
            for g in range(lanes // 256):
                first = j * (lanes // width) + g * group
                cols = pl.ds(j * lanes + g * 256, 256)
                both = jnp.dot(
                    push_ref[i, pl.ds(first * state, group * state), :], held_ref[i, :, cols],
                    preferred_element_type=F32)
                end = jnp.where(lane_head == 0, both[:state], 0.0)
                for k in range(1, group):
                    end = jnp.where(lane_head == k, both[k * state:(k + 1) * state], end)
                end_ref[i, :, cols] = end


def local_ends(x, logdec, bc):
    count, positions, channels = x.shape
    heads, state = logdec.shape[1], bc.shape[2]
    width = channels // heads
    lanes = min(1024, channels)
    whole = pl.BlockSpec(memory_space=pltpu.VMEM)
    return pl.pallas_call(
        functools.partial(ends_kernel, width=width, lanes=lanes),
        in_specs=[pl.BlockSpec(memory_space=pltpu.HBM)] * 3,
        out_specs=[whole, whole],
        out_shape=[
            jax.ShapeDtypeStruct((count, state, channels), F32),
            jax.ShapeDtypeStruct((count, 8, channels), F32),
        ],
        scratch_shapes=[
            pltpu.VMEM(x.shape, BF16),
            pltpu.VMEM(logdec.shape, F32),
            pltpu.VMEM(bc.shape[1:], BF16),
            pltpu.VMEM((count, heads * state, positions), BF16),
            pltpu.SemaphoreType.DMA((count, channels // lanes)),
            pltpu.SemaphoreType.DMA((2,)),
        ],
        compiler_params=pltpu.CompilerParams(vmem_limit_bytes=VMEM_LIMIT),
        cost_estimate=pl.CostEstimate(
            flops=2 * 64 * x.size, bytes_accessed=2 * x.size, transcendentals=0),
        name="local_ends",
    )(in_hbm(x), in_hbm(logdec), in_hbm(bc))


def prepare(parts, logs, lv_ref, lc_ref, state, heads):
    size = logs.shape[1]
    chunks = size // CHUNK
    half = CHUNK // 2
    src, dst = iota((size, 1), 0), iota((1, size), 1)
    middle = quotient(dst, CHUNK) * CHUNK + half - 1
    plus = (src > middle) & (src <= dst)
    minus = (src > dst) & (src <= middle)
    offset = exact_dot(logs, jnp.where(plus, 1.0, jnp.where(minus, -1.0, 0.0)))
    row_scale = jnp.exp(offset)
    in_scale = jnp.exp(-offset) * gain_of(logs)
    span = iota((1, 128), 1) == quotient(src + half, CHUNK)
    steps = jnp.exp(exact_dot(logs, jnp.where(span, 1.0, 0.0)))
    rows = state * chunks
    mine = quotient(iota((rows, 1), 0), state) == quotient(dst, CHUNK)
    keep = (dst <= src) & (quotient(dst, CHUNK) == quotient(src, CHUNK))
    for i, (b_rows, c_rows) in enumerate(parts):
        b_all = jnp.concatenate([b_rows.astype(F32)] * chunks, axis=0)
        lv_ref[i, pl.ds(0, rows), :] = jnp.where(mine, b_all, 0.0).astype(BF16)
        scores = lax.dot_general(c_rows, b_rows, (((0,), (0,)), ((), ())), preferred_element_type=F32)
        lv_ref[i, pl.ds(rows, size), :] = jnp.where(keep, scores, 0.0).astype(BF16)
        c_all = jnp.concatenate([c_rows.astype(F32)] * chunks, axis=0)
        lc_ref[i] = jnp.where(mine, c_all, 0.0).T.astype(BF16)
    scales = []
    for first in range(0, logs.shape[0], heads):
        here = slice(first, first + heads)
        columns = [hi_lo(in_scale[here]).T, hi_lo(steps[here]).T[:16], hi_lo(row_scale[here]).T]
        scales.append(jnp.concatenate(columns, axis=0).astype(BF16))
    return scales


def cuts_of(ld_ref):
    count, _, positions = ld_ref.shape
    return [(i, pl.ds(b * BLOCK, BLOCK)) for i in range(count) for b in range(positions // BLOCK)]


def prepare_kernel(
    pld_ref, pbc_ref, bld_ref, bbc_ref,
    hot_ref, pw_ref, plv_ref, plc_ref, bw_ref, blv_ref, blc_ref, reach_out, reach_ref, sems, *, width
):
    state = pbc_ref.shape[2]

    def collect(ld_ref, bc_ref):
        cuts = cuts_of(ld_ref)
        logs = jnp.concatenate([ld_ref[i, :, cut] for i, cut in cuts], axis=0)
        return cuts, logs, [(bc_ref[0, i, :, cut], bc_ref[1, i, :, cut]) for i, cut in cuts]

    cuts, logs, parts = collect(bld_ref, bbc_ref)
    heads = bld_ref.shape[1]
    blocks = len(cuts) // bld_ref.shape[0]
    for k, w in enumerate(prepare(parts, logs, blv_ref, blc_ref, state, heads)):
        bw_ref[k] = w
    row_head = remainder(iota((2 * heads, 1), 0), heads)
    for g in range(hot_ref.shape[1] // 256):
        lane_head = quotient(iota((1, 256), 1), width) + g * (256 // width)
        hot_ref[:, pl.ds(g * 256, 256)] = jnp.where(row_head == lane_head, 1.0, 0.0).astype(BF16)
    left = Copies(sems)
    upto = jnp.where(iota((BLOCK, 1), 0) <= iota((1, BLOCK), 1), 1.0, 0.0)
    runs = exact_dot(logs, upto)
    for k, (i, cut) in enumerate(cuts):
        run = runs[k * heads:(k + 1) * heads]
        if k % blocks:
            run = run + entered
        entered = run[:, BLOCK - 1:BLOCK]
        reach = parts[k][1].astype(F32)[None, :, :] * jnp.exp(run)[:, None, :]
        reach_ref[i, cut, :] = reach.reshape(heads * state, BLOCK).T.astype(BF16)
        left.start((k,), reach_ref.at[i, cut, :], reach_out.at[i, cut, :])

    cuts, logs, parts = collect(pld_ref, pbc_ref)
    heads = pld_ref.shape[1] // 2
    for k, w in enumerate(prepare(parts, logs, plv_ref, plc_ref, state, heads)):
        pw_ref[k // 2, k % 2] = w
    left.wait_all()


def prepare_all(prompt_logdec, prompt_bc, branch_logdec, branch_bc, branch_channels):
    state = prompt_bc.shape[2]
    rows = BLOCK // CHUNK * state
    prompt_cuts = prompt_logdec.shape[0] * (prompt_logdec.shape[2] // BLOCK)
    branches, heads, positions = branch_logdec.shape
    branch_cuts = branches * (positions // BLOCK)
    half = prompt_logdec.shape[1] // 2
    shapes = [
        ((2 * heads, branch_channels), BF16),
        ((prompt_cuts, 2, 2 * BLOCK + 16, 2 * half), BF16),
        ((prompt_cuts, rows + BLOCK, BLOCK), BF16),
        ((prompt_cuts, BLOCK, rows), BF16),
        ((branch_cuts, 2 * BLOCK + 16, 2 * heads), BF16),
        ((branch_cuts, rows + BLOCK, BLOCK), BF16),
        ((branch_cuts, BLOCK, rows), BF16),
        ((branches, positions, heads * state), BF16),
    ]
    whole = pl.BlockSpec(memory_space=pltpu.VMEM)
    out = pl.pallas_call(
        functools.partial(prepare_kernel, width=branch_channels // heads),
        in_specs=[whole] * 4,
        out_specs=[
            pl.BlockSpec(shape, lambda rank=len(shape): (0,) * rank) for shape, _ in shapes[:-1]
        ] + [pl.BlockSpec(memory_space=pltpu.HBM)],
        out_shape=[jax.ShapeDtypeStruct(*shape) for shape in shapes],
        scratch_shapes=[pltpu.VMEM(*shapes[-1]), pltpu.SemaphoreType.DMA((branch_cuts,))],
        compiler_params=pltpu.CompilerParams(vmem_limit_bytes=VMEM_LIMIT),
        cost_estimate=pl.CostEstimate(flops=10**8, bytes_accessed=10**6, transcendentals=0),
        name="prepare",
    )(prompt_logdec, prompt_bc, branch_logdec, branch_bc)
    return out[:4], (out[0], *out[4:7]), out[7]


def run_tiles(jobs):
    scaled, passed = {}, {}
    for g in range(len(jobs) + 2):
        if g < len(jobs):
            scaled[g] = jobs[g][0]()
        if 0 <= g - 1 < len(jobs):
            passed[g - 1] = jobs[g - 1][1](scaled.pop(g - 1))
        if 0 <= g - 2:
            jobs[g - 2][2](passed.pop(g - 2))


def tile_job(ready_refs, at, g, x_of, entering_of, leave, write):
    hot_ref, w_ref, lv_ref, lc_ref = ready_refs
    w_at, at = at
    rows = lc_ref.shape[2]
    chunks = BLOCK // CHUNK
    state = rows // chunks

    def scale():
        wide = jnp.dot(w_ref[w_at], hot_ref[:, pl.ds(g * 256, 256)], preferred_element_type=F32)
        scaled = (x_of().astype(F32) * wide[:BLOCK]).astype(BF16)
        return scaled, wide[BLOCK:BLOCK + 16], wide[BLOCK + 16:]

    def pass_on(given):
        scaled, steps, out_scale = given
        both = jnp.dot(lv_ref[at], scaled, preferred_element_type=F32)
        carries, carry = [], steps[0:1] * entering_of()
        for c in range(chunks):
            carries.append(carry.astype(BF16))
            carry = steps[c + 1:c + 2] * (carry + both[c * state:(c + 1) * state])
        leave(carry)
        return both[rows:], jnp.concatenate(carries, axis=0), out_scale

    def give(given):
        inner, carries, out_scale = given
        carried = jnp.dot(lc_ref[at], carries, preferred_element_type=F32)
        write((inner + carried) * out_scale)

    return scale, pass_on, give


class Copies:
    def __init__(self, sems):
        self.sems, self.started = sems, {}

    def start(self, key, source, target):
        copy = pltpu.make_async_copy(source, target, self.sems.at[key])
        copy.start()
        self.started[key] = copy

    def wait(self, key):
        self.started.pop(key).wait()

    def wait_all(self):
        for key in list(self.started):
            self.wait(key)


def branch_kernel(x_in, *refs, which):
    ready = refs[:4]
    own_out, x_ref, own_ref, s_ref, in_sems, out_sems = refs[4:]
    positions, channels = x_ref.shape
    state = s_ref.shape[0]
    blocks = positions // BLOCK
    lanes = channels // in_sems.shape[1]
    came, left = Copies(in_sems), Copies(out_sems)
    for b in range(blocks):
        for j in range(channels // lanes):
            spot = (pl.ds(b * BLOCK, BLOCK), pl.ds(j * lanes, lanes))
            came.start((b, j), x_in.at[(which, *spot)], x_ref.at[spot])

    def job(b, g):
        cols = pl.ds(g * 256, 256)
        here = (pl.ds(b * BLOCK, BLOCK), cols)

        def x_of():
            if g * 256 % lanes == 0:
                came.wait((b, g * 256 // lanes))
            return x_ref[here]

        def leave(carry):
            if b < blocks - 1:
                s_ref[:, cols] = carry

        def write(out):
            own_ref[here] = out
            left.start((b, g), own_ref.at[here], own_out.at[here])

        def entering_of():
            return s_ref[:, cols] if b else jnp.zeros((state, 256), F32)

        at = which * blocks + b
        return tile_job(ready, (at, at), g, x_of, entering_of, leave, write)

    run_tiles([job(b, g) for b in range(blocks) for g in range(channels // 256)])
    left.wait_all()


def branch_own(x, ready, which):
    _, positions, channels = x.shape
    state = ready[3].shape[2] * CHUNK // BLOCK
    whole = pl.BlockSpec(memory_space=pltpu.VMEM)
    work = positions * channels
    return pl.pallas_call(
        functools.partial(branch_kernel, which=which),
        in_specs=[pl.BlockSpec(memory_space=pltpu.HBM)] + [whole] * 4,
        out_specs=pl.BlockSpec(memory_space=pltpu.HBM),
        out_shape=jax.ShapeDtypeStruct(x.shape[1:], F32),
        scratch_shapes=[
            pltpu.VMEM((positions, channels), BF16),
            pltpu.VMEM((positions, channels), F32),
            pltpu.VMEM((state, channels), F32),
            pltpu.SemaphoreType.DMA((positions // BLOCK, channels // min(512, channels))),
            pltpu.SemaphoreType.DMA((positions // BLOCK, channels // 256)),
        ],
        compiler_params=pltpu.CompilerParams(vmem_limit_bytes=VMEM_LIMIT),
        cost_estimate=pl.CostEstimate(
            flops=2 * 1152 * work, bytes_accessed=4 * work, transcendentals=0),
        name="branch_own",
    )(in_hbm(x), *ready)


def prompt_kernel(*refs, skip):
    half_ref, x_in, *ready, start_ref = refs[:7]
    y_out, x_ref, in_sems, out_sems = refs[7 + skip:]
    count, positions, channels = x_ref.shape
    blocks = positions // BLOCK
    lanes = channels // in_sems.shape[2]
    half = half_ref[0]
    came, left = Copies(in_sems), Copies(out_sems)
    entered = {}

    def spots(i, b, j):
        there = pl.ds(pl.multiple_of(half * channels + j * lanes, lanes), lanes)
        rows = pl.ds(b * BLOCK, BLOCK)
        return (i, rows, there), (i, rows, pl.ds(j * lanes, lanes))

    for i in range(count):
        for b in range(blocks):
            for j in range(channels // lanes):
                there, here = spots(i, b, j)
                came.start((i, b, j), x_in.at[there], x_ref.at[here])

    def job(i, b, g):
        here = (i, pl.ds(b * BLOCK, BLOCK), pl.ds(g * 256, 256))
        j = g * 256 // lanes

        def x_of():
            if g * 256 % lanes == 0:
                came.wait((i, b, j))
            return x_ref[here]

        def leave(carry):
            entered[i, g] = carry

        def entering_of():
            return entered[i, g] if b else start_ref[i, :, pl.ds(g * 256, 256)]

        def write(out):
            x_ref[here] = out.astype(BF16)
            if (g + 1) * 256 % lanes == 0:
                there, staged = spots(i, b, j)
                left.start((i, b, j), x_ref.at[staged], y_out.at[there])

        at = i * blocks + b
        return tile_job(ready, ((at, half), at), g, x_of, entering_of, leave, write)

    run_tiles([job(i, b, g) for i in range(count) for b in range(blocks) for g in range(channels // 256)])
    left.wait_all()


def prompt_half(half, x, ready, start, into):
    count, positions, channels = x.shape
    part = channels // 2
    whole = pl.BlockSpec(memory_space=pltpu.VMEM)
    hbm = pl.BlockSpec(memory_space=pltpu.HBM)
    parts = (count, positions // BLOCK, part // min(512, part))
    work = count * positions * part
    return pl.pallas_call(
        functools.partial(prompt_kernel, skip=len(into)),
        in_specs=[pl.BlockSpec(memory_space=pltpu.SMEM), hbm] + [whole] * 5 + [hbm] * len(into),
        out_specs=hbm,
        out_shape=jax.ShapeDtypeStruct(x.shape, BF16),
        scratch_shapes=[
            pltpu.VMEM((count, positions, part), BF16),
            pltpu.SemaphoreType.DMA(parts),
            pltpu.SemaphoreType.DMA(parts),
        ],
        input_output_aliases={7 + i: i for i in range(len(into))},
        compiler_params=pltpu.CompilerParams(vmem_limit_bytes=VMEM_LIMIT),
        cost_estimate=pl.CostEstimate(
            flops=2 * 1152 * work, bytes_accessed=4 * work, transcendentals=0),
        name="prompt_half",
    )(half, in_hbm(x), *ready, start, *into)


def finish_kernel(len_ref, reach_ref, start_ref, *refs, width):
    own_refs, (y_out, y_ref, sems) = refs[:-3], refs[-3:]
    count, positions, channels = y_ref.shape
    state = start_ref.shape[0]
    group = 128 // state
    span = group * width
    left = Copies(sems)
    own_head = quotient(iota((128, 1), 0), state) == quotient(iota((1, span), 1), width)
    starts = []
    for g in range(channels // span):
        start = jnp.concatenate([start_ref[:, pl.ds(g * span, span)]] * group, axis=0)
        starts.append(jnp.where(own_head, start, 0.0).astype(BF16))
    for i in range(count):
        for g in range(channels // span):
            for b in range(positions // BLOCK):
                rows, cols = pl.ds(b * BLOCK, BLOCK), pl.ds(g * span, span)
                term = jnp.dot(
                    reach_ref[i, rows, pl.ds(g * 128, 128)], starts[g], preferred_element_type=F32)
                live = iota((BLOCK, span), 0) < len_ref[i] - b * BLOCK
                y_ref[i, rows, cols] = jnp.where(live, own_refs[i][rows, cols] + term, 0.0).astype(BF16)
                left.start((i, b, g), y_ref.at[i, rows, cols], y_out.at[i, rows, cols])
    left.wait_all()


def finish(lengths, reach, start, own):
    count, (positions, channels) = len(own), own[0].shape
    state = start.shape[0]
    width = channels * state // reach.shape[2]
    whole = pl.BlockSpec(memory_space=pltpu.VMEM)
    return pl.pallas_call(
        functools.partial(finish_kernel, width=width),
        in_specs=[pl.BlockSpec(memory_space=pltpu.SMEM)] + [whole] * (2 + count),
        out_specs=pl.BlockSpec(memory_space=pltpu.HBM),
        out_shape=jax.ShapeDtypeStruct((count, positions, channels), BF16),
        scratch_shapes=[
            pltpu.VMEM((count, positions, channels), BF16),
            pltpu.SemaphoreType.DMA((count, positions // BLOCK, reach.shape[2] // 128)),
        ],
        compiler_params=pltpu.CompilerParams(vmem_limit_bytes=VMEM_LIMIT),
        cost_estimate=pl.CostEstimate(
            flops=2**28, bytes_accessed=2**23, transcendentals=0),
        name="branch_finish",
    )(lengths, reach, start, *own)


def swap_bit(value, bit, size):
    return lax.ppermute(value, "ctx", [(k, k ^ bit) for k in range(size)])


def pack(states, logs):
    lanes = states.shape[-1]
    return jnp.concatenate([states.reshape(-1, lanes), logs.reshape(-1, lanes)], axis=0)


def unpack(packed, count):
    lanes = packed.shape[-1]
    rows = packed.shape[0] - count
    return packed[:rows].reshape(count, rows // count, lanes), packed[rows:].reshape(count, 1, lanes)


def in_order(upper, mine, other):
    first = [jnp.where(upper, o, m) for m, o in zip(mine, other)]
    second = [jnp.where(upper, m, o) for m, o in zip(mine, other)]
    return first, second


def join(first, second):
    return jnp.exp(second[1]) * first[0] + second[0], first[1] + second[1]


def spread_step(value, hop, ctx_size, pair_size):
    owner = lax.axis_index("ctx") * pair_size // ctx_size
    known = [m for m in range(pair_size) if m & (2 * hop - 1) == 0]
    links = []
    for k in range(ctx_size):
        z = k * pair_size // ctx_size
        links += [(k * pair_size + (z ^ m), k * pair_size + (z ^ m ^ hop)) for m in known]
    got = lax.ppermute(value, ("ctx", "pair"), links)
    has = ((lax.axis_index("pair") ^ owner) & (2 * hop - 1)) == 0
    return got, has


def body(
    prompt_x,
    prompt_bc,
    prompt_logdec,
    branch_x,
    branch_bc,
    branch_logdec,
    branch_prompt,
    branch_len,
):
    size, pair_size = lax.axis_size("ctx"), lax.axis_size("pair")
    prompts, branches = prompt_x.shape[0], branch_x.shape[0]
    assert size == 2 * pair_size and size & (size - 1) == 0 and branch_prompt.shape[0] == 1
    mine = lax.axis_index("ctx")
    odd = (mine & 1) == 1

    def beside(exchange, value, work, *given):
        value, given = lax.optimization_barrier((value, given))
        got = exchange(value)
        return lax.optimization_barrier((got, work(*given)))

    end, log = local_ends(prompt_x, prompt_logdec, prompt_bc)
    half = end.shape[2] // 2
    low, high = (end[:, :, :half], log[:, :1, :half]), (end[:, :, half:], log[:, :1, half:])
    keep = [jnp.where(odd, h, l) for l, h in zip(low, high)]
    send = [jnp.where(odd, l, h) for l, h in zip(low, high)]
    got, (prompt_ready, branch_ready, reach) = beside(
        lambda v: swap_bit(v, 1, size),
        pack(*send),
        lambda ld: prepare_all(prompt_logdec, prompt_bc, ld, branch_bc, branch_x.shape[2]),
        branch_logdec,
    )
    got = unpack(got, prompts)
    first, second = in_order(odd, keep, got)
    total, total_log = join(first, second)
    before, before_log = jnp.zeros_like(total), jnp.zeros_like(total_log)

    own = ()
    works = iter(range(branches))
    bit = 2
    while bit < size:
        which = next(works, None)
        swap = functools.partial(swap_bit, bit=bit, size=size)
        if which is None:
            got = swap(pack(total, total_log))
        else:
            got, own = beside(
                swap, pack(total, total_log),
                lambda x, own: (*own, branch_own(x, branch_ready, which)), branch_x, own)
        other = unpack(got, prompts)
        upper = (mine & bit) != 0
        before = jnp.where(upper, jnp.exp(before_log) * other[0] + before, before)
        before_log = jnp.where(upper, before_log + other[1], before_log)
        total, total_log = join(*in_order(upper, (total, total_log), other))
        bit *= 2
    for which in works:
        own = (*own, branch_own(branch_x, branch_ready, which))

    next_before = jnp.exp(first[1]) * before + first[0]
    keep = jnp.where(odd, next_before, before)
    others = swap_bit(jnp.where(odd, before, next_before), 1, size)
    here = jnp.reshape(mine & 1, (1,))
    sides = [(here, keep), (1 - here, others)]
    prompt_y = ()
    hop = pair_size // 2
    while hop:
        step = functools.partial(spread_step, hop=hop, ctx_size=size, pair_size=pair_size)
        if sides:
            side, entering = sides.pop(0)
            (got, has), prompt_y = beside(
                step, total,
                lambda entering, y: (prompt_half(side, prompt_x, prompt_ready, entering, y),), entering, prompt_y)
        else:
            got, has = step(total)
        total = jnp.where(has, total, got)
        hop //= 2
    for side, entering in sides:
        prompt_y = (prompt_half(side, prompt_x, prompt_ready, entering, prompt_y),)
    start = total[0]
    for which in range(1, prompts):
        start = jnp.where(branch_prompt[0] == which, total[which], start)
    branch_y = finish(branch_len, reach, start, own)
    return prompt_y[0], branch_y


def solution(mesh):
    return jax.shard_map(
        body,
        mesh=mesh,
        in_specs=(
            P(None, "ctx", "pair"),
            P(None, None, None, "ctx"),
            P(None, "pair", "ctx"),
            P("pair", None, "ctx"),
            P(None, "pair", None, None),
            P("pair", "ctx", None),
            P("pair"),
            P("pair"),
        ),
        out_specs=(P(None, "ctx", "pair"), P("pair", None, "ctx")),
        check_vma=False,
    )
```

```python
import functools
import jax
import jax.numpy as jnp
from jax import lax
from jax.experimental import pallas as pl
from jax.experimental.pallas import tpu as pltpu
from jax.sharding import PartitionSpec as P

BLOCK = 256
CHUNK = 32
F32 = jnp.float32
BF16 = jnp.bfloat16
VMEM_LIMIT = 16 * 1024 * 1024


def iota(shape, dim):
    return lax.broadcasted_iota(jnp.int32, shape, dim)


def quotient(index, divisor):
    if divisor & (divisor - 1) == 0:
        return lax.shift_right_logical(index, divisor.bit_length() - 1)
    return lax.div(index, divisor)


def remainder(index, divisor):
    if divisor & (divisor - 1) == 0:
        return index & (divisor - 1)
    return lax.rem(index, divisor)


def exact_dot(a, b):
    return jnp.dot(a, b, preferred_element_type=F32, precision=lax.Precision.HIGHEST)


def gain_of(log_decay):
    z = 2.0 * log_decay
    series = 1.0 + z * (1.0 / 9.0)
    for k in (8, 7, 6, 5, 4, 3, 2):
        series = 1.0 + z * (1.0 / k) * series
    small = -z * series
    large = 1.0 - jnp.exp(z)
    return jnp.sqrt(jnp.maximum(jnp.where(z > -0.5, small, large), 0.0))


def hi_lo(value):
    high = value.astype(BF16).astype(F32)
    return jnp.concatenate([high, value - high], axis=0)


def in_hbm(array):
    return pltpu.with_memory_space_constraint(array, pltpu.HBM)


def split_dot(rows, one_hot):
    count = rows.shape[0]
    high = rows.astype(BF16).astype(F32)
    middle = (rows - high).astype(BF16).astype(F32)
    parts = jnp.concatenate([high, middle, rows - high - middle], axis=0).astype(BF16)
    out = jnp.dot(parts, one_hot, preferred_element_type=F32)
    return out[:count] + out[count:2 * count] + out[2 * count:]


def ends_kernel(
    x_ref, ld_in, bc_in, end_ref, log_ref, held_ref, ld_ref, b_ref, push_ref, sems, first_sems, *, width, lanes
):
    first_copies = [
        pltpu.make_async_copy(ld_in, ld_ref, first_sems.at[0]),
        pltpu.make_async_copy(bc_in.at[0], b_ref, first_sems.at[1]),
    ]
    for copy in first_copies:
        copy.start()
    count, heads, positions = ld_ref.shape
    state = end_ref.shape[1]
    channels = end_ref.shape[2]
    tiles = channels // lanes
    copies = {}
    for i in range(count):
        for j in range(tiles):
            cols = pl.ds(j * lanes, lanes)
            copies[i, j] = pltpu.make_async_copy(
                x_ref.at[i, :, cols], held_ref.at[i, :, cols], sems.at[i, j])
            copies[i, j].start()
    for copy in first_copies:
        copy.wait()
    logs = jnp.concatenate([ld_ref[i] for i in range(count)], axis=0)
    after = jnp.where(iota((positions, 1), 0) > iota((1, positions), 1), 1.0, 0.0)
    to_end = jnp.exp(exact_dot(logs, after)) * gain_of(logs)
    for i in range(count):
        b_rows = b_ref[i].astype(F32)
        push = b_rows[None, :, :] * to_end[i * heads:(i + 1) * heads][:, None, :]
        push_ref[i] = push.reshape(heads * state, positions).astype(BF16)
    group = 256 // width
    lane_head = quotient(iota((1, 256), 1), width)
    for i in range(count):
        totals = lax.dot_general(
            jnp.ones((16, positions), F32), ld_ref[i], (((1,), (1,)), ((), ())),
            preferred_element_type=F32, precision=lax.Precision.HIGHEST)
        for j in range(tiles):
            cols = pl.ds(j * lanes, lanes)
            pick = iota((heads, 1), 0) == quotient(iota((1, lanes), 1), width) + j * (lanes // width)
            log_ref[i, :, cols] = split_dot(totals, jnp.where(pick, 1.0, 0.0).astype(BF16))[:8]
    for i in range(count):
        for j in range(tiles):
            copies[i, j].wait()
            for g in range(lanes // 256):
                first = j * (lanes // width) + g * group
                cols = pl.ds(j * lanes + g * 256, 256)
                both = jnp.dot(
                    push_ref[i, pl.ds(first * state, group * state), :], held_ref[i, :, cols],
                    preferred_element_type=F32)
                end = jnp.where(lane_head == 0, both[:state], 0.0)
                for k in range(1, group):
                    end = jnp.where(lane_head == k, both[k * state:(k + 1) * state], end)
                end_ref[i, :, cols] = end


def local_ends(x, logdec, bc):
    count, positions, channels = x.shape
    heads, state = logdec.shape[1], bc.shape[2]
    width = channels // heads
    lanes = min(1024, channels)
    whole = pl.BlockSpec(memory_space=pltpu.VMEM)
    return pl.pallas_call(
        functools.partial(ends_kernel, width=width, lanes=lanes),
        in_specs=[pl.BlockSpec(memory_space=pltpu.HBM)] * 3,
        out_specs=[whole, whole],
        out_shape=[
            jax.ShapeDtypeStruct((count, state, channels), F32),
            jax.ShapeDtypeStruct((count, 8, channels), F32),
        ],
        scratch_shapes=[
            pltpu.VMEM(x.shape, BF16),
            pltpu.VMEM(logdec.shape, F32),
            pltpu.VMEM(bc.shape[1:], BF16),
            pltpu.VMEM((count, heads * state, positions), BF16),
            pltpu.SemaphoreType.DMA((count, channels // lanes)),
            pltpu.SemaphoreType.DMA((2,)),
        ],
        compiler_params=pltpu.CompilerParams(vmem_limit_bytes=VMEM_LIMIT),
        cost_estimate=pl.CostEstimate(
            flops=2 * 64 * x.size, bytes_accessed=2 * x.size, transcendentals=0),
        name="local_ends",
    )(in_hbm(x), in_hbm(logdec), in_hbm(bc))


def prepare(parts, logs, lv_ref, lc_ref, state, heads):
    size = logs.shape[1]
    chunks = size // CHUNK
    half = CHUNK // 2
    src, dst = iota((size, 1), 0), iota((1, size), 1)
    middle = quotient(dst, CHUNK) * CHUNK + half - 1
    plus = (src > middle) & (src <= dst)
    minus = (src > dst) & (src <= middle)
    offset = exact_dot(logs, jnp.where(plus, 1.0, jnp.where(minus, -1.0, 0.0)))
    row_scale = jnp.exp(offset)
    in_scale = jnp.exp(-offset) * gain_of(logs)
    span = iota((1, 128), 1) == quotient(src + half, CHUNK)
    steps = jnp.exp(exact_dot(logs, jnp.where(span, 1.0, 0.0)))
    rows = state * chunks
    mine = quotient(iota((rows, 1), 0), state) == quotient(dst, CHUNK)
    keep = (dst <= src) & (quotient(dst, CHUNK) == quotient(src, CHUNK))
    for i, (b_rows, c_rows) in enumerate(parts):
        b_all = jnp.concatenate([b_rows.astype(F32)] * chunks, axis=0)
        lv_ref[i, pl.ds(0, rows), :] = jnp.where(mine, b_all, 0.0).astype(BF16)
        scores = lax.dot_general(c_rows, b_rows, (((0,), (0,)), ((), ())), preferred_element_type=F32)
        lv_ref[i, pl.ds(rows, size), :] = jnp.where(keep, scores, 0.0).astype(BF16)
        c_all = jnp.concatenate([c_rows.astype(F32)] * chunks, axis=0)
        lc_ref[i] = jnp.where(mine, c_all, 0.0).T.astype(BF16)
    scales = []
    for first in range(0, logs.shape[0], heads):
        here = slice(first, first + heads)
        columns = [hi_lo(in_scale[here]).T, hi_lo(steps[here]).T[:16], hi_lo(row_scale[here]).T]
        scales.append(jnp.concatenate(columns, axis=0).astype(BF16))
    return scales


def prepare_hot(hot_ref, heads, width):
    row_head = remainder(iota((2 * heads, 1), 0), heads)
    for g in range(hot_ref.shape[1] // 256):
        lane_head = quotient(iota((1, 256), 1), width) + g * (256 // width)
        hot_ref[:, pl.ds(g * 256, 256)] = jnp.where(row_head == lane_head, 1.0, 0.0).astype(BF16)


def blocks_of(ld_ref, bc_ref):
    count, _, positions = ld_ref.shape
    cuts = [(i, pl.ds(b * BLOCK, BLOCK)) for i in range(count) for b in range(positions // BLOCK)]
    logs = jnp.concatenate([ld_ref[i, :, cut] for i, cut in cuts], axis=0)
    return cuts, logs, [(bc_ref[0, i, :, cut], bc_ref[1, i, :, cut]) for i, cut in cuts]


def prepare_kernel(ld_ref, bc_ref, hot_ref, w_ref, lv_ref, lc_ref, *, width):
    heads = ld_ref.shape[1] // 2
    prepare_hot(hot_ref, heads, width)
    _, logs, parts = blocks_of(ld_ref, bc_ref)
    for k, w in enumerate(prepare(parts, logs, lv_ref, lc_ref, bc_ref.shape[2], heads)):
        w_ref[k // 2, k % 2] = w


def prepare_prompts(logdec, bc, channels):
    count, heads, positions = logdec.shape
    rows = BLOCK // CHUNK * bc.shape[2]
    cuts = count * (positions // BLOCK)
    half = heads // 2
    shapes = [
        (2 * half, channels // 2),
        (cuts, 2, 2 * BLOCK + 16, 2 * half),
        (cuts, rows + BLOCK, BLOCK),
        (cuts, BLOCK, rows),
    ]
    whole = pl.BlockSpec(memory_space=pltpu.VMEM)
    return pl.pallas_call(
        functools.partial(prepare_kernel, width=channels // heads),
        in_specs=[whole] * 2,
        out_specs=[pl.BlockSpec(shape, lambda rank=len(shape): (0,) * rank) for shape in shapes],
        out_shape=[jax.ShapeDtypeStruct(shape, BF16) for shape in shapes],
        compiler_params=pltpu.CompilerParams(vmem_limit_bytes=VMEM_LIMIT),
        cost_estimate=pl.CostEstimate(flops=10**8, bytes_accessed=10**6, transcendentals=0),
        name="prepare",
    )(logdec, bc)


def run_tiles(jobs):
    scaled, passed = {}, {}
    for g in range(len(jobs) + 2):
        if g < len(jobs):
            scaled[g] = jobs[g][0]()
        if 0 <= g - 1 < len(jobs):
            passed[g - 1] = jobs[g - 1][1](scaled.pop(g - 1))
        if 0 <= g - 2:
            jobs[g - 2][2](passed.pop(g - 2))


def tile_job(ready_refs, at, cols, x_of, entering_of, leave, write):
    hot_ref, w_ref, lv_ref, lc_ref = ready_refs
    w_at, at = at
    rows = lc_ref.shape[2]
    chunks = BLOCK // CHUNK
    state = rows // chunks

    def scale():
        wide = jnp.dot(w_ref[w_at], hot_ref[:, cols], preferred_element_type=F32)
        scaled = (x_of().astype(F32) * wide[:BLOCK]).astype(BF16)
        return scaled, wide[BLOCK:BLOCK + 16], wide[BLOCK + 16:]

    def pass_on(given):
        scaled, steps, out_scale = given
        both = jnp.dot(lv_ref[at], scaled, preferred_element_type=F32)
        carries, carry = [], steps[0:1] * entering_of()
        for c in range(chunks):
            carries.append(carry.astype(BF16))
            carry = steps[c + 1:c + 2] * (carry + both[c * state:(c + 1) * state])
        leave(carry)
        return both[rows:], jnp.concatenate(carries, axis=0), out_scale

    def give(given):
        inner, carries, out_scale = given
        carried = jnp.dot(lc_ref[at], carries, preferred_element_type=F32)
        write((inner + carried) * out_scale)

    return scale, pass_on, give


class Copies:
    def __init__(self, sems):
        self.sems, self.started = sems, {}

    def start(self, key, source, target):
        copy = pltpu.make_async_copy(source, target, self.sems.at[key])
        copy.start()
        self.started[key] = copy

    def wait(self, key):
        self.started.pop(key).wait()

    def wait_all(self):
        for key in list(self.started):
            self.wait(key)


def branch_kernel(x_ref, ld_ref, bc_ref, *refs, skip, width):
    own_ref, reach_ref, hot_ref, w_ref, lv_ref, lc_ref, s_ref = refs[skip:]
    block, tile = pl.program_id(0), pl.program_id(1)
    heads = ld_ref.shape[1]
    lanes = x_ref.shape[2]
    state = s_ref.shape[0]

    @pl.when((block == 0) & (tile == 0))
    def _():
        prepare_hot(hot_ref, heads, width)
        cuts, logs, parts = blocks_of(ld_ref, bc_ref)
        for k, w in enumerate(prepare(parts, logs, lv_ref, lc_ref, state, heads)):
            w_ref[k] = w
        upto = jnp.where(iota((BLOCK, 1), 0) <= iota((1, BLOCK), 1), 1.0, 0.0)
        runs = exact_dot(logs, upto)
        for k, (_, cut) in enumerate(cuts):
            run = runs[k * heads:(k + 1) * heads]
            if k:
                run = run + entered
            entered = run[:, BLOCK - 1:BLOCK]
            reach = parts[k][1].astype(F32)[None, :, :] * jnp.exp(run)[:, None, :]
            reach_ref[0, cut, :] = reach.reshape(heads * state, BLOCK).T.astype(BF16)

    def job(g):
        cols = pl.ds(g * 256, 256)
        here = pl.ds(pl.multiple_of(tile * lanes + g * 256, 256), 256)

        def entering_of():
            return jnp.where(block == 0, 0.0, s_ref[:, here])

        def leave(carry):
            s_ref[:, here] = carry

        def write(out):
            own_ref[0, :, cols] = out

        ready = (hot_ref, w_ref, lv_ref, lc_ref)
        return tile_job(ready, (block, block), here, lambda: x_ref[0, :, cols], entering_of, leave, write)

    run_tiles([job(g) for g in range(lanes // 256)])


def branch_own(x, logdec, bc, which, into):
    count, positions, channels = x.shape
    heads, state = logdec.shape[1], bc.shape[2]
    blocks, rows = positions // BLOCK, BLOCK // CHUNK * state
    lanes = min(1024, channels)
    work = positions * channels
    return pl.pallas_call(
        functools.partial(branch_kernel, skip=len(into), width=channels // heads),
        grid=(blocks, channels // lanes),
        in_specs=[
            pl.BlockSpec((1, BLOCK, lanes), lambda b, j: (which, b, j)),
            pl.BlockSpec((1, heads, positions), lambda b, j: (which, 0, 0)),
            pl.BlockSpec((2, 1, state, positions), lambda b, j: (0, which, 0, 0)),
        ] + [pl.BlockSpec(memory_space=pl.ANY)] * len(into),
        out_specs=[
            pl.BlockSpec((1, BLOCK, lanes), lambda b, j: (which, b, j)),
            pl.BlockSpec((1, positions, heads * state), lambda b, j: (which, 0, 0)),
        ],
        out_shape=[
            jax.ShapeDtypeStruct(x.shape, F32),
            jax.ShapeDtypeStruct((count, positions, heads * state), BF16),
        ],
        scratch_shapes=[
            pltpu.VMEM((2 * heads, channels), BF16),
            pltpu.VMEM((blocks, 2 * BLOCK + 16, 2 * heads), BF16),
            pltpu.VMEM((blocks, rows + BLOCK, BLOCK), BF16),
            pltpu.VMEM((blocks, BLOCK, rows), BF16),
            pltpu.VMEM((state, channels), F32),
        ],
        input_output_aliases={3 + i: i for i in range(len(into))},
        compiler_params=pltpu.CompilerParams(vmem_limit_bytes=32 * 1024 * 1024),
        cost_estimate=pl.CostEstimate(
            flops=2 * 1152 * work, bytes_accessed=4 * work, transcendentals=0),
        name="branch_own",
    )(in_hbm(x), logdec, bc, *into)


def prompt_kernel(*refs, skip):
    half_ref, x_in, *ready, start_ref = refs[:7]
    y_out, x_ref, in_sems, out_sems = refs[7 + skip:]
    count, positions, channels = x_ref.shape
    blocks = positions // BLOCK
    lanes = channels // in_sems.shape[2]
    half = half_ref[0]
    came, left = Copies(in_sems), Copies(out_sems)
    entered = {}

    def spots(i, b, j):
        there = pl.ds(pl.multiple_of(half * channels + j * lanes, lanes), lanes)
        rows = pl.ds(b * BLOCK, BLOCK)
        return (i, rows, there), (i, rows, pl.ds(j * lanes, lanes))

    for i in range(count):
        for b in range(blocks):
            for j in range(channels // lanes):
                there, here = spots(i, b, j)
                came.start((i, b, j), x_in.at[there], x_ref.at[here])

    def job(i, b, g):
        here = (i, pl.ds(b * BLOCK, BLOCK), pl.ds(g * 256, 256))
        j = g * 256 // lanes

        def x_of():
            if g * 256 % lanes == 0:
                came.wait((i, b, j))
            return x_ref[here]

        def leave(carry):
            entered[i, g] = carry

        def entering_of():
            return entered[i, g] if b else start_ref[i, :, pl.ds(g * 256, 256)]

        def write(out):
            x_ref[here] = out.astype(BF16)
            if (g + 1) * 256 % lanes == 0:
                there, staged = spots(i, b, j)
                left.start((i, b, j), x_ref.at[staged], y_out.at[there])

        at = i * blocks + b
        return tile_job(ready, ((at, half), at), pl.ds(g * 256, 256), x_of, entering_of, leave, write)

    run_tiles([job(i, b, g) for i in range(count) for b in range(blocks) for g in range(channels // 256)])
    left.wait_all()


def prompt_half(half, x, ready, start, into):
    count, positions, channels = x.shape
    part = channels // 2
    whole = pl.BlockSpec(memory_space=pltpu.VMEM)
    hbm = pl.BlockSpec(memory_space=pltpu.HBM)
    parts = (count, positions // BLOCK, part // min(512, part))
    work = count * positions * part
    return pl.pallas_call(
        functools.partial(prompt_kernel, skip=len(into)),
        in_specs=[pl.BlockSpec(memory_space=pltpu.SMEM), hbm] + [whole] * 5 + [hbm] * len(into),
        out_specs=hbm,
        out_shape=jax.ShapeDtypeStruct(x.shape, BF16),
        scratch_shapes=[
            pltpu.VMEM((count, positions, part), BF16),
            pltpu.SemaphoreType.DMA(parts),
            pltpu.SemaphoreType.DMA(parts),
        ],
        input_output_aliases={7 + i: i for i in range(len(into))},
        compiler_params=pltpu.CompilerParams(vmem_limit_bytes=VMEM_LIMIT),
        cost_estimate=pl.CostEstimate(
            flops=2 * 1152 * work, bytes_accessed=4 * work, transcendentals=0),
        name="prompt_half",
    )(half, in_hbm(x), *ready, start, *into)


def finish_kernel(len_ref, own_ref, reach_ref, start_ref, y_out, y_ref, sems, *, width):
    count, positions, channels = y_ref.shape
    state = start_ref.shape[0]
    group = 128 // state
    span = group * width
    left = Copies(sems)
    own_head = quotient(iota((128, 1), 0), state) == quotient(iota((1, span), 1), width)
    starts = []
    for g in range(channels // span):
        start = jnp.concatenate([start_ref[:, pl.ds(g * span, span)]] * group, axis=0)
        starts.append(jnp.where(own_head, start, 0.0).astype(BF16))
    for i in range(count):
        for g in range(channels // span):
            for b in range(positions // BLOCK):
                rows, cols = pl.ds(b * BLOCK, BLOCK), pl.ds(g * span, span)
                term = jnp.dot(
                    reach_ref[i, rows, pl.ds(g * 128, 128)], starts[g], preferred_element_type=F32)
                live = iota((BLOCK, span), 0) < len_ref[i] - b * BLOCK
                y_ref[i, rows, cols] = jnp.where(live, own_ref[i, rows, cols] + term, 0.0).astype(BF16)
                left.start((i, b, g), y_ref.at[i, rows, cols], y_out.at[i, rows, cols])
    left.wait_all()


def finish(lengths, own, reach, start):
    count, positions, channels = own.shape
    state = start.shape[0]
    width = channels * state // reach.shape[2]
    whole = pl.BlockSpec(memory_space=pltpu.VMEM)
    return pl.pallas_call(
        functools.partial(finish_kernel, width=width),
        in_specs=[pl.BlockSpec(memory_space=pltpu.SMEM)] + [whole] * 3,
        out_specs=pl.BlockSpec(memory_space=pltpu.HBM),
        out_shape=jax.ShapeDtypeStruct((count, positions, channels), BF16),
        scratch_shapes=[
            pltpu.VMEM((count, positions, channels), BF16),
            pltpu.SemaphoreType.DMA((count, positions // BLOCK, reach.shape[2] // 128)),
        ],
        compiler_params=pltpu.CompilerParams(vmem_limit_bytes=VMEM_LIMIT),
        cost_estimate=pl.CostEstimate(
            flops=2**28, bytes_accessed=2**23, transcendentals=0),
        name="branch_finish",
    )(lengths, own, reach, start)


def swap_bit(value, bit, size):
    return lax.ppermute(value, "ctx", [(k, k ^ bit) for k in range(size)])


def pack(states, logs):
    lanes = states.shape[-1]
    return jnp.concatenate([states.reshape(-1, lanes), logs.reshape(-1, lanes)], axis=0)


def unpack(packed, count):
    lanes = packed.shape[-1]
    rows = packed.shape[0] - count
    return packed[:rows].reshape(count, rows // count, lanes), packed[rows:].reshape(count, 1, lanes)


def in_order(upper, mine, other):
    first = [jnp.where(upper, o, m) for m, o in zip(mine, other)]
    second = [jnp.where(upper, m, o) for m, o in zip(mine, other)]
    return first, second


def join(first, second):
    return jnp.exp(second[1]) * first[0] + second[0], first[1] + second[1]


def spread_step(value, hop, ctx_size, pair_size):
    owner = lax.axis_index("ctx") * pair_size // ctx_size
    known = [m for m in range(pair_size) if m & (2 * hop - 1) == 0]
    links = []
    for k in range(ctx_size):
        z = k * pair_size // ctx_size
        links += [(k * pair_size + (z ^ m), k * pair_size + (z ^ m ^ hop)) for m in known]
    got = lax.ppermute(value, ("ctx", "pair"), links)
    has = ((lax.axis_index("pair") ^ owner) & (2 * hop - 1)) == 0
    return got, has


def body(
    prompt_x,
    prompt_bc,
    prompt_logdec,
    branch_x,
    branch_bc,
    branch_logdec,
    branch_prompt,
    branch_len,
):
    size, pair_size = lax.axis_size("ctx"), lax.axis_size("pair")
    prompts, branches = prompt_x.shape[0], branch_x.shape[0]
    assert size == 2 * pair_size and size & (size - 1) == 0 and branch_prompt.shape[0] == 1
    mine = lax.axis_index("ctx")
    odd = (mine & 1) == 1

    def beside(exchange, value, work, *given):
        value, given = lax.optimization_barrier((value, given))
        got = exchange(value)
        return lax.optimization_barrier((got, work(*given)))

    end, log = local_ends(prompt_x, prompt_logdec, prompt_bc)
    half = end.shape[2] // 2
    low, high = (end[:, :, :half], log[:, :1, :half]), (end[:, :, half:], log[:, :1, half:])
    keep = [jnp.where(odd, h, l) for l, h in zip(low, high)]
    send = [jnp.where(odd, l, h) for l, h in zip(low, high)]
    got, ready = beside(
        lambda v: swap_bit(v, 1, size),
        pack(*send),
        lambda logdec: prepare_prompts(logdec, prompt_bc, prompt_x.shape[2]),
        prompt_logdec,
    )
    got = unpack(got, prompts)
    first, second = in_order(odd, keep, got)
    total, total_log = join(first, second)
    before, before_log = jnp.zeros_like(total), jnp.zeros_like(total_log)

    own = ()
    works = iter(range(branches))
    bit = 2
    while bit < size:
        which = next(works, None)
        swap = functools.partial(swap_bit, bit=bit, size=size)
        if which is None:
            got = swap(pack(total, total_log))
        else:
            got, own = beside(
                swap, pack(total, total_log),
                lambda x, own: branch_own(x, branch_logdec, branch_bc, which, own), branch_x, own)
        other = unpack(got, prompts)
        upper = (mine & bit) != 0
        before = jnp.where(upper, jnp.exp(before_log) * other[0] + before, before)
        before_log = jnp.where(upper, before_log + other[1], before_log)
        total, total_log = join(*in_order(upper, (total, total_log), other))
        bit *= 2
    for which in works:
        own = branch_own(branch_x, branch_logdec, branch_bc, which, own)

    next_before = jnp.exp(first[1]) * before + first[0]
    keep = jnp.where(odd, next_before, before)
    others = swap_bit(jnp.where(odd, before, next_before), 1, size)
    here = jnp.reshape(mine & 1, (1,))
    sides = [(here, keep), (1 - here, others)]
    prompt_y = ()
    hop = pair_size // 2
    while hop:
        step = functools.partial(spread_step, hop=hop, ctx_size=size, pair_size=pair_size)
        if sides:
            side, entering = sides.pop(0)
            (got, has), prompt_y = beside(
                step, total,
                lambda entering, y: (prompt_half(side, prompt_x, ready, entering, y),), entering, prompt_y)
        else:
            got, has = step(total)
        total = jnp.where(has, total, got)
        hop //= 2
    for side, entering in sides:
        prompt_y = (prompt_half(side, prompt_x, ready, entering, prompt_y),)
    start = total[0]
    for which in range(1, prompts):
        start = jnp.where(branch_prompt[0] == which, total[which], start)
    branch_y = finish(branch_len, *own, start)
    return prompt_y[0], branch_y


def solution(mesh):
    return jax.shard_map(
        body,
        mesh=mesh,
        in_specs=(
            P(None, "ctx", "pair"),
            P(None, None, None, "ctx"),
            P(None, "pair", "ctx"),
            P("pair", None, "ctx"),
            P(None, "pair", None, None),
            P("pair", "ctx", None),
            P("pair"),
            P("pair"),
        ),
        out_specs=(P(None, "ctx", "pair"), P("pair", None, "ctx")),
        check_vma=False,
    )
```

```python
import functools
import jax
import jax.numpy as jnp
from jax import lax
from jax.experimental import pallas as pl
from jax.experimental.pallas import tpu as pltpu
from jax.sharding import PartitionSpec as P

BLOCK = 256
CHUNK = 32
F32 = jnp.float32
BF16 = jnp.bfloat16
VMEM_LIMIT = 16 * 1024 * 1024


def iota(shape, dim):
    return lax.broadcasted_iota(jnp.int32, shape, dim)


def quotient(index, divisor):
    if divisor & (divisor - 1) == 0:
        return lax.shift_right_logical(index, divisor.bit_length() - 1)
    return lax.div(index, divisor)


def remainder(index, divisor):
    if divisor & (divisor - 1) == 0:
        return index & (divisor - 1)
    return lax.rem(index, divisor)


def exact_dot(a, b):
    return jnp.dot(a, b, preferred_element_type=F32, precision=lax.Precision.HIGHEST)


def gain_of(log_decay):
    z = 2.0 * log_decay
    series = 1.0 + z * (1.0 / 9.0)
    for k in (8, 7, 6, 5, 4, 3, 2):
        series = 1.0 + z * (1.0 / k) * series
    small = -z * series
    large = 1.0 - jnp.exp(z)
    return jnp.sqrt(jnp.maximum(jnp.where(z > -0.5, small, large), 0.0))


def hi_lo(value):
    high = value.astype(BF16).astype(F32)
    return jnp.concatenate([high, value - high], axis=0)


def in_hbm(array):
    return pltpu.with_memory_space_constraint(array, pltpu.HBM)


def split_dot(rows, one_hot):
    count = rows.shape[0]
    high = rows.astype(BF16).astype(F32)
    middle = (rows - high).astype(BF16).astype(F32)
    parts = jnp.concatenate([high, middle, rows - high - middle], axis=0).astype(BF16)
    out = jnp.dot(parts, one_hot, preferred_element_type=F32)
    return out[:count] + out[count:2 * count] + out[2 * count:]


def ends_kernel(
    x_ref, ld_in, bc_in, end_ref, log_ref, held_ref, ld_ref, b_ref, push_ref, sems, first_sems, *, width, lanes
):
    first_copies = [
        pltpu.make_async_copy(ld_in, ld_ref, first_sems.at[0]),
        pltpu.make_async_copy(bc_in.at[0], b_ref, first_sems.at[1]),
    ]
    for copy in first_copies:
        copy.start()
    count, heads, positions = ld_ref.shape
    state = end_ref.shape[1]
    channels = end_ref.shape[2]
    tiles = channels // lanes
    copies = {}
    for i in range(count):
        for j in range(tiles):
            cols = pl.ds(j * lanes, lanes)
            copies[i, j] = pltpu.make_async_copy(
                x_ref.at[i, :, cols], held_ref.at[i, :, cols], sems.at[i, j])
            copies[i, j].start()
    for copy in first_copies:
        copy.wait()
    logs = jnp.concatenate([ld_ref[i] for i in range(count)], axis=0)
    after = jnp.where(iota((positions, 1), 0) > iota((1, positions), 1), 1.0, 0.0)
    to_end = jnp.exp(exact_dot(logs, after)) * gain_of(logs)
    for i in range(count):
        b_rows = b_ref[i].astype(F32)
        push = b_rows[None, :, :] * to_end[i * heads:(i + 1) * heads][:, None, :]
        push_ref[i] = push.reshape(heads * state, positions).astype(BF16)
    group = 256 // width
    lane_head = quotient(iota((1, 256), 1), width)
    for i in range(count):
        totals = lax.dot_general(
            jnp.ones((16, positions), F32), ld_ref[i], (((1,), (1,)), ((), ())),
            preferred_element_type=F32, precision=lax.Precision.HIGHEST)
        for j in range(tiles):
            cols = pl.ds(j * lanes, lanes)
            pick = iota((heads, 1), 0) == quotient(iota((1, lanes), 1), width) + j * (lanes // width)
            log_ref[i, :, cols] = split_dot(totals, jnp.where(pick, 1.0, 0.0).astype(BF16))[:8]
    for i in range(count):
        for j in range(tiles):
            copies[i, j].wait()
            for g in range(lanes // 256):
                first = j * (lanes // width) + g * group
                cols = pl.ds(j * lanes + g * 256, 256)
                both = jnp.dot(
                    push_ref[i, pl.ds(first * state, group * state), :], held_ref[i, :, cols],
                    preferred_element_type=F32)
                end = jnp.where(lane_head == 0, both[:state], 0.0)
                for k in range(1, group):
                    end = jnp.where(lane_head == k, both[k * state:(k + 1) * state], end)
                end_ref[i, :, cols] = end


def local_ends(x, logdec, bc):
    count, positions, channels = x.shape
    heads, state = logdec.shape[1], bc.shape[2]
    width = channels // heads
    lanes = min(1024, channels)
    whole = pl.BlockSpec(memory_space=pltpu.VMEM)
    return pl.pallas_call(
        functools.partial(ends_kernel, width=width, lanes=lanes),
        in_specs=[pl.BlockSpec(memory_space=pltpu.HBM)] * 3,
        out_specs=[whole, whole],
        out_shape=[
            jax.ShapeDtypeStruct((count, state, channels), F32),
            jax.ShapeDtypeStruct((count, 8, channels), F32),
        ],
        scratch_shapes=[
            pltpu.VMEM(x.shape, BF16),
            pltpu.VMEM(logdec.shape, F32),
            pltpu.VMEM(bc.shape[1:], BF16),
            pltpu.VMEM((count, heads * state, positions), BF16),
            pltpu.SemaphoreType.DMA((count, channels // lanes)),
            pltpu.SemaphoreType.DMA((2,)),
        ],
        compiler_params=pltpu.CompilerParams(vmem_limit_bytes=VMEM_LIMIT),
        cost_estimate=pl.CostEstimate(
            flops=2 * 64 * x.size, bytes_accessed=2 * x.size, transcendentals=0),
        name="local_ends",
    )(in_hbm(x), in_hbm(logdec), in_hbm(bc))


def prepare(parts, logs, lv_ref, lc_ref, state, heads):
    size = logs.shape[1]
    chunks = size // CHUNK
    half = CHUNK // 2
    src, dst = iota((size, 1), 0), iota((1, size), 1)
    middle = quotient(dst, CHUNK) * CHUNK + half - 1
    plus = (src > middle) & (src <= dst)
    minus = (src > dst) & (src <= middle)
    offset = exact_dot(logs, jnp.where(plus, 1.0, jnp.where(minus, -1.0, 0.0)))
    row_scale = jnp.exp(offset)
    in_scale = jnp.exp(-offset) * gain_of(logs)
    span = iota((1, 128), 1) == quotient(src + half, CHUNK)
    steps = jnp.exp(exact_dot(logs, jnp.where(span, 1.0, 0.0)))
    rows = state * chunks
    mine = quotient(iota((rows, 1), 0), state) == quotient(dst, CHUNK)
    keep = (dst <= src) & (quotient(dst, CHUNK) == quotient(src, CHUNK))
    for i, (b_rows, c_rows) in enumerate(parts):
        b_all = jnp.concatenate([b_rows.astype(F32)] * chunks, axis=0)
        lv_ref[i, pl.ds(0, rows), :] = jnp.where(mine, b_all, 0.0).astype(BF16)
        scores = lax.dot_general(c_rows, b_rows, (((0,), (0,)), ((), ())), preferred_element_type=F32)
        lv_ref[i, pl.ds(rows, size), :] = jnp.where(keep, scores, 0.0).astype(BF16)
        c_all = jnp.concatenate([c_rows.astype(F32)] * chunks, axis=0)
        lc_ref[i] = jnp.where(mine, c_all, 0.0).T.astype(BF16)
    scales = []
    for first in range(0, logs.shape[0], heads):
        here = slice(first, first + heads)
        columns = [hi_lo(in_scale[here]).T, hi_lo(steps[here]).T[:16], hi_lo(row_scale[here]).T]
        scales.append(jnp.concatenate(columns, axis=0).astype(BF16))
    return scales


def cuts_of(ld_ref):
    count, _, positions = ld_ref.shape
    return [(i, pl.ds(b * BLOCK, BLOCK)) for i in range(count) for b in range(positions // BLOCK)]


def prepare_kernel(
    pld_ref, pbc_ref, bld_ref, bbc_ref,
    hot_ref, pw_ref, plv_ref, plc_ref, bw_ref, blv_ref, blc_ref, reach_ref, *, width
):
    state = pbc_ref.shape[2]

    def collect(ld_ref, bc_ref):
        cuts = cuts_of(ld_ref)
        logs = jnp.concatenate([ld_ref[i, :, cut] for i, cut in cuts], axis=0)
        return cuts, logs, [(bc_ref[0, i, :, cut], bc_ref[1, i, :, cut]) for i, cut in cuts]

    cuts, logs, parts = collect(bld_ref, bbc_ref)
    heads = bld_ref.shape[1]
    blocks = len(cuts) // bld_ref.shape[0]
    for k, w in enumerate(prepare(parts, logs, blv_ref, blc_ref, state, heads)):
        bw_ref[k] = w
    row_head = remainder(iota((2 * heads, 1), 0), heads)
    for g in range(hot_ref.shape[1] // 256):
        lane_head = quotient(iota((1, 256), 1), width) + g * (256 // width)
        hot_ref[:, pl.ds(g * 256, 256)] = jnp.where(row_head == lane_head, 1.0, 0.0).astype(BF16)
    upto = jnp.where(iota((BLOCK, 1), 0) <= iota((1, BLOCK), 1), 1.0, 0.0)
    runs = exact_dot(logs, upto)
    for k, (i, cut) in enumerate(cuts):
        run = runs[k * heads:(k + 1) * heads]
        if k % blocks:
            run = run + entered
        entered = run[:, BLOCK - 1:BLOCK]
        reach = parts[k][1].astype(F32)[None, :, :] * jnp.exp(run)[:, None, :]
        reach_ref[i, cut, :] = reach.reshape(heads * state, BLOCK).T.astype(BF16)

    cuts, logs, parts = collect(pld_ref, pbc_ref)
    heads = pld_ref.shape[1] // 2
    for k, w in enumerate(prepare(parts, logs, plv_ref, plc_ref, state, heads)):
        pw_ref[k // 2, k % 2] = w


def prepare_all(prompt_logdec, prompt_bc, branch_logdec, branch_bc, branch_channels):
    state = prompt_bc.shape[2]
    rows = BLOCK // CHUNK * state
    prompt_cuts = prompt_logdec.shape[0] * (prompt_logdec.shape[2] // BLOCK)
    branches, heads, positions = branch_logdec.shape
    branch_cuts = branches * (positions // BLOCK)
    half = prompt_logdec.shape[1] // 2
    shapes = [
        ((2 * heads, branch_channels), BF16),
        ((prompt_cuts, 2, 2 * BLOCK + 16, 2 * half), BF16),
        ((prompt_cuts, rows + BLOCK, BLOCK), BF16),
        ((prompt_cuts, BLOCK, rows), BF16),
        ((branch_cuts, 2 * BLOCK + 16, 2 * heads), BF16),
        ((branch_cuts, rows + BLOCK, BLOCK), BF16),
        ((branch_cuts, BLOCK, rows), BF16),
        ((branches, positions, heads * state), BF16),
    ]
    whole = pl.BlockSpec(memory_space=pltpu.VMEM)
    out = pl.pallas_call(
        functools.partial(prepare_kernel, width=branch_channels // heads),
        in_specs=[whole] * 4,
        out_specs=[pl.BlockSpec(shape, lambda rank=len(shape): (0,) * rank) for shape, _ in shapes],
        out_shape=[jax.ShapeDtypeStruct(*shape) for shape in shapes],
        compiler_params=pltpu.CompilerParams(vmem_limit_bytes=VMEM_LIMIT),
        cost_estimate=pl.CostEstimate(flops=10**8, bytes_accessed=10**6, transcendentals=0),
        name="prepare",
    )(prompt_logdec, prompt_bc, branch_logdec, branch_bc)
    return out[:4], (out[0], *out[4:7]), out[7]


def run_tiles(jobs):
    scaled, passed = {}, {}
    for g in range(len(jobs) + 2):
        if g < len(jobs):
            scaled[g] = jobs[g][0]()
        if 0 <= g - 1 < len(jobs):
            passed[g - 1] = jobs[g - 1][1](scaled.pop(g - 1))
        if 0 <= g - 2:
            jobs[g - 2][2](passed.pop(g - 2))


def tile_job(ready_refs, at, g, x_of, entering_of, leave, write):
    hot_ref, w_ref, lv_ref, lc_ref = ready_refs
    w_at, at = at
    rows = lc_ref.shape[2]
    chunks = BLOCK // CHUNK
    state = rows // chunks

    def scale():
        wide = jnp.dot(w_ref[w_at], hot_ref[:, pl.ds(g * 256, 256)], preferred_element_type=F32)
        scaled = (x_of().astype(F32) * wide[:BLOCK]).astype(BF16)
        return scaled, wide[BLOCK:BLOCK + 16], wide[BLOCK + 16:]

    def pass_on(given):
        scaled, steps, out_scale = given
        both = jnp.dot(lv_ref[at], scaled, preferred_element_type=F32)
        carries, carry = [], steps[0:1] * entering_of()
        for c in range(chunks):
            carries.append(carry.astype(BF16))
            carry = steps[c + 1:c + 2] * (carry + both[c * state:(c + 1) * state])
        leave(carry)
        return both[rows:], jnp.concatenate(carries, axis=0), out_scale

    def give(given):
        inner, carries, out_scale = given
        carried = jnp.dot(lc_ref[at], carries, preferred_element_type=F32)
        write((inner + carried) * out_scale)

    return scale, pass_on, give


class Copies:
    def __init__(self, sems):
        self.sems, self.started = sems, {}

    def start(self, key, source, target):
        copy = pltpu.make_async_copy(source, target, self.sems.at[key])
        copy.start()
        self.started[key] = copy

    def wait(self, key):
        self.started.pop(key).wait()

    def wait_all(self):
        for key in list(self.started):
            self.wait(key)


def branch_kernel(x_in, *refs, which):
    ready = refs[:4]
    own_ref, x_ref, s_ref, in_sems = refs[4:]
    positions, channels = x_ref.shape
    state = s_ref.shape[0]
    blocks = positions // BLOCK
    lanes = channels // in_sems.shape[1]
    came = Copies(in_sems)
    for b in range(blocks):
        for j in range(channels // lanes):
            spot = (pl.ds(b * BLOCK, BLOCK), pl.ds(j * lanes, lanes))
            came.start((b, j), x_in.at[(which, *spot)], x_ref.at[spot])

    def job(b, g):
        cols = pl.ds(g * 256, 256)
        here = (pl.ds(b * BLOCK, BLOCK), cols)

        def x_of():
            if g * 256 % lanes == 0:
                came.wait((b, g * 256 // lanes))
            return x_ref[here]

        def leave(carry):
            if b < blocks - 1:
                s_ref[:, cols] = carry

        def write(out):
            own_ref[here] = out

        def entering_of():
            return s_ref[:, cols] if b else jnp.zeros((state, 256), F32)

        at = which * blocks + b
        return tile_job(ready, (at, at), g, x_of, entering_of, leave, write)

    run_tiles([job(b, g) for b in range(blocks) for g in range(channels // 256)])


def branch_own(x, ready, which):
    _, positions, channels = x.shape
    state = ready[3].shape[2] * CHUNK // BLOCK
    whole = pl.BlockSpec(memory_space=pltpu.VMEM)
    work = positions * channels
    return pl.pallas_call(
        functools.partial(branch_kernel, which=which),
        in_specs=[pl.BlockSpec(memory_space=pltpu.HBM)] + [whole] * 4,
        out_specs=whole,
        out_shape=jax.ShapeDtypeStruct(x.shape[1:], F32),
        scratch_shapes=[
            pltpu.VMEM((positions, channels), BF16),
            pltpu.VMEM((state, channels), F32),
            pltpu.SemaphoreType.DMA((positions // BLOCK, channels // min(512, channels))),
        ],
        compiler_params=pltpu.CompilerParams(vmem_limit_bytes=VMEM_LIMIT),
        cost_estimate=pl.CostEstimate(
            flops=2 * 1152 * work, bytes_accessed=4 * work, transcendentals=0),
        name="branch_own",
    )(in_hbm(x), *ready)


def prompt_kernel(*refs, skip):
    half_ref, x_in, *ready, start_ref = refs[:7]
    y_out, x_ref, in_sems, out_sems = refs[7 + skip:]
    count, positions, channels = x_ref.shape
    blocks = positions // BLOCK
    lanes = channels // in_sems.shape[2]
    half = half_ref[0]
    came, left = Copies(in_sems), Copies(out_sems)
    entered = {}

    def spots(i, b, j):
        there = pl.ds(pl.multiple_of(half * channels + j * lanes, lanes), lanes)
        rows = pl.ds(b * BLOCK, BLOCK)
        return (i, rows, there), (i, rows, pl.ds(j * lanes, lanes))

    for i in range(count):
        for b in range(blocks):
            for j in range(channels // lanes):
                there, here = spots(i, b, j)
                came.start((i, b, j), x_in.at[there], x_ref.at[here])

    def job(i, b, g):
        here = (i, pl.ds(b * BLOCK, BLOCK), pl.ds(g * 256, 256))
        j = g * 256 // lanes

        def x_of():
            if g * 256 % lanes == 0:
                came.wait((i, b, j))
            return x_ref[here]

        def leave(carry):
            entered[i, g] = carry

        def entering_of():
            return entered[i, g] if b else start_ref[i, :, pl.ds(g * 256, 256)]

        def write(out):
            x_ref[here] = out.astype(BF16)
            if (g + 1) * 256 % lanes == 0:
                there, staged = spots(i, b, j)
                left.start((i, b, j), x_ref.at[staged], y_out.at[there])

        at = i * blocks + b
        return tile_job(ready, ((at, half), at), g, x_of, entering_of, leave, write)

    run_tiles([job(i, b, g) for i in range(count) for b in range(blocks) for g in range(channels // 256)])
    left.wait_all()


def prompt_half(half, x, ready, start, into):
    count, positions, channels = x.shape
    part = channels // 2
    whole = pl.BlockSpec(memory_space=pltpu.VMEM)
    hbm = pl.BlockSpec(memory_space=pltpu.HBM)
    parts = (count, positions // BLOCK, part // min(512, part))
    work = count * positions * part
    return pl.pallas_call(
        functools.partial(prompt_kernel, skip=len(into)),
        in_specs=[pl.BlockSpec(memory_space=pltpu.SMEM), hbm] + [whole] * 5 + [hbm] * len(into),
        out_specs=hbm,
        out_shape=jax.ShapeDtypeStruct(x.shape, BF16),
        scratch_shapes=[
            pltpu.VMEM((count, positions, part), BF16),
            pltpu.SemaphoreType.DMA(parts),
            pltpu.SemaphoreType.DMA(parts),
        ],
        input_output_aliases={7 + i: i for i in range(len(into))},
        compiler_params=pltpu.CompilerParams(vmem_limit_bytes=VMEM_LIMIT),
        cost_estimate=pl.CostEstimate(
            flops=2 * 1152 * work, bytes_accessed=4 * work, transcendentals=0),
        name="prompt_half",
    )(half, in_hbm(x), *ready, start, *into)


def finish_kernel(len_ref, reach_ref, start_ref, *refs, width):
    own_refs, (y_out, y_ref, sems) = refs[:-3], refs[-3:]
    count, positions, channels = y_ref.shape
    state = start_ref.shape[0]
    group = 128 // state
    span = group * width
    left = Copies(sems)
    own_head = quotient(iota((128, 1), 0), state) == quotient(iota((1, span), 1), width)
    starts = []
    for g in range(channels // span):
        start = jnp.concatenate([start_ref[:, pl.ds(g * span, span)]] * group, axis=0)
        starts.append(jnp.where(own_head, start, 0.0).astype(BF16))
    for i in range(count):
        for g in range(channels // span):
            for b in range(positions // BLOCK):
                rows, cols = pl.ds(b * BLOCK, BLOCK), pl.ds(g * span, span)
                term = jnp.dot(
                    reach_ref[i, rows, pl.ds(g * 128, 128)], starts[g], preferred_element_type=F32)
                live = iota((BLOCK, span), 0) < len_ref[i] - b * BLOCK
                y_ref[i, rows, cols] = jnp.where(live, own_refs[i][rows, cols] + term, 0.0).astype(BF16)
                left.start((i, b, g), y_ref.at[i, rows, cols], y_out.at[i, rows, cols])
    left.wait_all()


def finish(lengths, reach, start, own):
    count, (positions, channels) = len(own), own[0].shape
    state = start.shape[0]
    width = channels * state // reach.shape[2]
    whole = pl.BlockSpec(memory_space=pltpu.VMEM)
    return pl.pallas_call(
        functools.partial(finish_kernel, width=width),
        in_specs=[pl.BlockSpec(memory_space=pltpu.SMEM)] + [whole] * (2 + count),
        out_specs=pl.BlockSpec(memory_space=pltpu.HBM),
        out_shape=jax.ShapeDtypeStruct((count, positions, channels), BF16),
        scratch_shapes=[
            pltpu.VMEM((count, positions, channels), BF16),
            pltpu.SemaphoreType.DMA((count, positions // BLOCK, reach.shape[2] // 128)),
        ],
        compiler_params=pltpu.CompilerParams(vmem_limit_bytes=VMEM_LIMIT),
        cost_estimate=pl.CostEstimate(
            flops=2**28, bytes_accessed=2**23, transcendentals=0),
        name="branch_finish",
    )(lengths, reach, start, *own)


def swap_bit(value, bit, size):
    return lax.ppermute(value, "ctx", [(k, k ^ bit) for k in range(size)])


def pack(states, logs):
    lanes = states.shape[-1]
    return jnp.concatenate([states.reshape(-1, lanes), logs.reshape(-1, lanes)], axis=0)


def unpack(packed, count):
    lanes = packed.shape[-1]
    rows = packed.shape[0] - count
    return packed[:rows].reshape(count, rows // count, lanes), packed[rows:].reshape(count, 1, lanes)


def in_order(upper, mine, other):
    first = [jnp.where(upper, o, m) for m, o in zip(mine, other)]
    second = [jnp.where(upper, m, o) for m, o in zip(mine, other)]
    return first, second


def join(first, second):
    return jnp.exp(second[1]) * first[0] + second[0], first[1] + second[1]


def spread_step(value, hop, ctx_size, pair_size):
    known = [m for m in range(pair_size) if m & (2 * hop - 1) == 0]
    links = []
    for k in range(ctx_size):
        z = k * pair_size // ctx_size
        links += [(k * pair_size + (z ^ m), k * pair_size + (z ^ m ^ hop)) for m in known]
    return lax.ppermute(value, ("ctx", "pair"), links)


def halvings(size):
    return [size >> k for k in range(1, size.bit_length())]


def places(branch_prompt, prompts):
    size, pair_size = lax.axis_size("ctx"), lax.axis_size("pair")
    ctx, pair = lax.axis_index("ctx"), lax.axis_index("pair")
    away = pair ^ lax.div(ctx * pair_size, size)
    odd = ctx & 1
    return {
        "odd": odd == 1,
        "half": jnp.reshape(odd, (1,)),
        "other_half": jnp.reshape(1 - odd, (1,)),
        "upper": {bit: (ctx & bit) != 0 for bit in halvings(size)[:-1]},
        "has": {hop: (away & (2 * hop - 1)) == 0 for hop in halvings(pair_size)},
        "chosen": [branch_prompt[0] == which for which in range(1, prompts)],
    }


def body(
    prompt_x,
    prompt_bc,
    prompt_logdec,
    branch_x,
    branch_bc,
    branch_logdec,
    branch_prompt,
    branch_len,
):
    size, pair_size = lax.axis_size("ctx"), lax.axis_size("pair")
    prompts, branches = prompt_x.shape[0], branch_x.shape[0]
    assert size == 2 * pair_size and size & (size - 1) == 0 and branch_prompt.shape[0] == 1
    place, prompt_logdec = lax.optimization_barrier((places(branch_prompt, prompts), prompt_logdec))
    odd = place["odd"]

    def beside(exchange, value, work, *given):
        value, given = lax.optimization_barrier((value, given))
        got = exchange(value)
        return lax.optimization_barrier((got, work(*given)))

    end, log = local_ends(prompt_x, prompt_logdec, prompt_bc)
    half = end.shape[2] // 2
    low, high = (end[:, :, :half], log[:, :1, :half]), (end[:, :, half:], log[:, :1, half:])
    keep = [jnp.where(odd, h, l) for l, h in zip(low, high)]
    send = [jnp.where(odd, l, h) for l, h in zip(low, high)]
    got, (prompt_ready, branch_ready, reach) = beside(
        lambda v: swap_bit(v, 1, size),
        pack(*send),
        lambda ld: prepare_all(prompt_logdec, prompt_bc, ld, branch_bc, branch_x.shape[2]),
        branch_logdec,
    )
    got = unpack(got, prompts)
    first, second = in_order(odd, keep, got)
    total, total_log = join(first, second)
    before, before_log = jnp.zeros_like(total), jnp.zeros_like(total_log)

    own = ()
    works = iter(range(branches))
    bit = 2
    while bit < size:
        which = next(works, None)
        swap = functools.partial(swap_bit, bit=bit, size=size)
        if which is None:
            got = swap(pack(total, total_log))
        else:
            got, own = beside(
                swap, pack(total, total_log),
                lambda x, own: (*own, branch_own(x, branch_ready, which)), branch_x, own)
        other = unpack(got, prompts)
        upper = place["upper"][bit]
        before = jnp.where(upper, jnp.exp(before_log) * other[0] + before, before)
        before_log = jnp.where(upper, before_log + other[1], before_log)
        total, total_log = join(*in_order(upper, (total, total_log), other))
        bit *= 2
    for which in works:
        own = (*own, branch_own(branch_x, branch_ready, which))

    next_before = jnp.exp(first[1]) * before + first[0]
    keep = jnp.where(odd, next_before, before)
    others = swap_bit(jnp.where(odd, before, next_before), 1, size)
    sides = [(place["half"], keep), (place["other_half"], others)]
    prompt_y = ()
    for hop in halvings(pair_size):
        step = functools.partial(spread_step, hop=hop, ctx_size=size, pair_size=pair_size)
        if sides:
            side, entering = sides.pop(0)
            got, prompt_y = beside(
                step, total,
                lambda entering, y: (prompt_half(side, prompt_x, prompt_ready, entering, y),), entering, prompt_y)
        else:
            got = step(total)
        total = jnp.where(place["has"][hop], total, got)
    for side, entering in sides:
        prompt_y = (prompt_half(side, prompt_x, prompt_ready, entering, prompt_y),)
    start = total[0]
    for which in range(1, prompts):
        start = jnp.where(place["chosen"][which - 1], total[which], start)
    branch_y = finish(branch_len, reach, start, own)
    return prompt_y[0], branch_y


def solution(mesh):
    return jax.shard_map(
        body,
        mesh=mesh,
        in_specs=(
            P(None, "ctx", "pair"),
            P(None, None, None, "ctx"),
            P(None, "pair", "ctx"),
            P("pair", None, "ctx"),
            P(None, "pair", None, None),
            P("pair", "ctx", None),
            P("pair"),
            P("pair"),
        ),
        out_specs=(P(None, "ctx", "pair"), P("pair", None, "ctx")),
        check_vma=False,
    )
```

```python
import functools
import jax
import jax.numpy as jnp
from jax import lax
from jax.experimental import pallas as pl
from jax.experimental.pallas import tpu as pltpu
from jax.sharding import PartitionSpec as P

BLOCK = 256
CHUNK = 32
F32 = jnp.float32
BF16 = jnp.bfloat16
VMEM_LIMIT = 16 * 1024 * 1024


def iota(shape, dim):
    return lax.broadcasted_iota(jnp.int32, shape, dim)


def quotient(index, divisor):
    if divisor & (divisor - 1) == 0:
        return lax.shift_right_logical(index, divisor.bit_length() - 1)
    return lax.div(index, divisor)


def remainder(index, divisor):
    if divisor & (divisor - 1) == 0:
        return index & (divisor - 1)
    return lax.rem(index, divisor)


def exact_dot(a, b):
    return jnp.dot(a, b, preferred_element_type=F32, precision=lax.Precision.HIGHEST)


def gain_of(log_decay):
    z = 2.0 * log_decay
    series = 1.0 + z * (1.0 / 9.0)
    for k in (8, 7, 6, 5, 4, 3, 2):
        series = 1.0 + z * (1.0 / k) * series
    small = -z * series
    large = 1.0 - jnp.exp(z)
    return jnp.sqrt(jnp.maximum(jnp.where(z > -0.5, small, large), 0.0))


def hi_lo(value):
    high = value.astype(BF16).astype(F32)
    return jnp.concatenate([high, value - high], axis=0)


def in_hbm(array):
    return pltpu.with_memory_space_constraint(array, pltpu.HBM)


def split_dot(rows, one_hot):
    count = rows.shape[0]
    high = rows.astype(BF16).astype(F32)
    middle = (rows - high).astype(BF16).astype(F32)
    parts = jnp.concatenate([high, middle, rows - high - middle], axis=0).astype(BF16)
    out = jnp.dot(parts, one_hot, preferred_element_type=F32)
    return out[:count] + out[count:2 * count] + out[2 * count:]


def ends_kernel(
    x_ref, ld_in, bc_in, end_ref, log_ref, held_ref, ld_ref, b_ref, push_ref, sems, first_sems, *, width, lanes
):
    first_copies = [
        pltpu.make_async_copy(ld_in, ld_ref, first_sems.at[0]),
        pltpu.make_async_copy(bc_in.at[0], b_ref, first_sems.at[1]),
    ]
    for copy in first_copies:
        copy.start()
    count, heads, positions = ld_ref.shape
    state = end_ref.shape[1]
    channels = end_ref.shape[2]
    tiles = channels // lanes
    copies = {}
    for i in range(count):
        for j in range(tiles):
            cols = pl.ds(j * lanes, lanes)
            copies[i, j] = pltpu.make_async_copy(
                x_ref.at[i, :, cols], held_ref.at[i, :, cols], sems.at[i, j])
            copies[i, j].start()
    for copy in first_copies:
        copy.wait()
    logs = jnp.concatenate([ld_ref[i] for i in range(count)], axis=0)
    after = jnp.where(iota((positions, 1), 0) > iota((1, positions), 1), 1.0, 0.0)
    to_end = jnp.exp(exact_dot(logs, after)) * gain_of(logs)
    for i in range(count):
        b_rows = b_ref[i].astype(F32)
        push = b_rows[None, :, :] * to_end[i * heads:(i + 1) * heads][:, None, :]
        push_ref[i] = push.reshape(heads * state, positions).astype(BF16)
    group = 256 // width
    lane_head = quotient(iota((1, 256), 1), width)
    for i in range(count):
        totals = lax.dot_general(
            jnp.ones((16, positions), F32), ld_ref[i], (((1,), (1,)), ((), ())),
            preferred_element_type=F32, precision=lax.Precision.HIGHEST)
        for j in range(tiles):
            cols = pl.ds(j * lanes, lanes)
            pick = iota((heads, 1), 0) == quotient(iota((1, lanes), 1), width) + j * (lanes // width)
            log_ref[i, :, cols] = split_dot(totals, jnp.where(pick, 1.0, 0.0).astype(BF16))[:8]
    for i in range(count):
        for j in range(tiles):
            copies[i, j].wait()
            for g in range(lanes // 256):
                first = j * (lanes // width) + g * group
                cols = pl.ds(j * lanes + g * 256, 256)
                both = jnp.dot(
                    push_ref[i, pl.ds(first * state, group * state), :], held_ref[i, :, cols],
                    preferred_element_type=F32)
                end = jnp.where(lane_head == 0, both[:state], 0.0)
                for k in range(1, group):
                    end = jnp.where(lane_head == k, both[k * state:(k + 1) * state], end)
                end_ref[i, :, cols] = end


def local_ends(x, logdec, bc):
    count, positions, channels = x.shape
    heads, state = logdec.shape[1], bc.shape[2]
    width = channels // heads
    lanes = min(1024, channels)
    whole = pl.BlockSpec(memory_space=pltpu.VMEM)
    return pl.pallas_call(
        functools.partial(ends_kernel, width=width, lanes=lanes),
        in_specs=[pl.BlockSpec(memory_space=pltpu.HBM)] * 3,
        out_specs=[whole, whole, whole],
        out_shape=[
            jax.ShapeDtypeStruct((count, state, channels), F32),
            jax.ShapeDtypeStruct((count, 8, channels), F32),
            jax.ShapeDtypeStruct(x.shape, BF16),
        ],
        scratch_shapes=[
            pltpu.VMEM(logdec.shape, F32),
            pltpu.VMEM(bc.shape[1:], BF16),
            pltpu.VMEM((count, heads * state, positions), BF16),
            pltpu.SemaphoreType.DMA((count, channels // lanes)),
            pltpu.SemaphoreType.DMA((2,)),
        ],
        compiler_params=pltpu.CompilerParams(vmem_limit_bytes=VMEM_LIMIT),
        cost_estimate=pl.CostEstimate(
            flops=2 * 64 * x.size, bytes_accessed=2 * x.size, transcendentals=0),
        name="local_ends",
    )(in_hbm(x), in_hbm(logdec), in_hbm(bc))


def prepare(parts, logs, lv_ref, lc_ref, state, heads):
    size = logs.shape[1]
    chunks = size // CHUNK
    half = CHUNK // 2
    src, dst = iota((size, 1), 0), iota((1, size), 1)
    middle = quotient(dst, CHUNK) * CHUNK + half - 1
    plus = (src > middle) & (src <= dst)
    minus = (src > dst) & (src <= middle)
    offset = exact_dot(logs, jnp.where(plus, 1.0, jnp.where(minus, -1.0, 0.0)))
    row_scale = jnp.exp(offset)
    in_scale = jnp.exp(-offset) * gain_of(logs)
    span = iota((1, 128), 1) == quotient(src + half, CHUNK)
    steps = jnp.exp(exact_dot(logs, jnp.where(span, 1.0, 0.0)))
    rows = state * chunks
    mine = quotient(iota((rows, 1), 0), state) == quotient(dst, CHUNK)
    keep = (dst <= src) & (quotient(dst, CHUNK) == quotient(src, CHUNK))
    for i, (b_rows, c_rows) in enumerate(parts):
        b_all = jnp.concatenate([b_rows.astype(F32)] * chunks, axis=0)
        lv_ref[i, pl.ds(0, rows), :] = jnp.where(mine, b_all, 0.0).astype(BF16)
        scores = lax.dot_general(c_rows, b_rows, (((0,), (0,)), ((), ())), preferred_element_type=F32)
        lv_ref[i, pl.ds(rows, size), :] = jnp.where(keep, scores, 0.0).astype(BF16)
        c_all = jnp.concatenate([c_rows.astype(F32)] * chunks, axis=0)
        lc_ref[i] = jnp.where(mine, c_all, 0.0).T.astype(BF16)
    scales = []
    for first in range(0, logs.shape[0], heads):
        here = slice(first, first + heads)
        columns = [hi_lo(in_scale[here]).T, hi_lo(steps[here]).T[:16], hi_lo(row_scale[here]).T]
        scales.append(jnp.concatenate(columns, axis=0).astype(BF16))
    return scales


def cuts_of(ld_ref):
    count, _, positions = ld_ref.shape
    return [(i, pl.ds(b * BLOCK, BLOCK)) for i in range(count) for b in range(positions // BLOCK)]


def prepare_hot(hot_ref, heads, width):
    row_head = remainder(iota((2 * heads, 1), 0), heads)
    for g in range(hot_ref.shape[1] // 256):
        lane_head = quotient(iota((1, 256), 1), width) + g * (256 // width)
        hot_ref[:, pl.ds(g * 256, 256)] = jnp.where(row_head == lane_head, 1.0, 0.0).astype(BF16)


def blocks_of(ld_ref, bc_ref):
    cuts = cuts_of(ld_ref)
    logs = jnp.concatenate([ld_ref[i, :, cut] for i, cut in cuts], axis=0)
    return cuts, logs, [(bc_ref[0, i, :, cut], bc_ref[1, i, :, cut]) for i, cut in cuts]


def prompt_prepare_kernel(ld_ref, bc_ref, w_ref, lv_ref, lc_ref):
    _, logs, parts = blocks_of(ld_ref, bc_ref)
    for k, w in enumerate(prepare(parts, logs, lv_ref, lc_ref, bc_ref.shape[2], ld_ref.shape[1] // 2)):
        w_ref[k // 2, k % 2] = w


def branch_prepare_kernel(ld_ref, bc_ref, hot_ref, w_ref, lv_ref, lc_ref, reach_ref, *, width):
    heads, state = ld_ref.shape[1], bc_ref.shape[2]
    blocks = ld_ref.shape[2] // BLOCK
    cuts, logs, parts = blocks_of(ld_ref, bc_ref)
    for k, w in enumerate(prepare(parts, logs, lv_ref, lc_ref, state, heads)):
        w_ref[k] = w
    prepare_hot(hot_ref, heads, width)
    upto = jnp.where(iota((BLOCK, 1), 0) <= iota((1, BLOCK), 1), 1.0, 0.0)
    runs = exact_dot(logs, upto)
    for k, (i, cut) in enumerate(cuts):
        run = runs[k * heads:(k + 1) * heads]
        if k % blocks:
            run = run + entered
        entered = run[:, BLOCK - 1:BLOCK]
        reach = parts[k][1].astype(F32)[None, :, :] * jnp.exp(run)[:, None, :]
        reach_ref[i, cut, :] = reach.reshape(heads * state, BLOCK).T.astype(BF16)


def prepare_call(kernel, shapes, name, logdec, bc):
    whole = pl.BlockSpec(memory_space=pltpu.VMEM)
    return pl.pallas_call(
        kernel,
        in_specs=[whole] * 2,
        out_specs=[whole] * len(shapes),
        out_shape=[jax.ShapeDtypeStruct(shape, BF16) for shape in shapes],
        compiler_params=pltpu.CompilerParams(vmem_limit_bytes=VMEM_LIMIT),
        cost_estimate=pl.CostEstimate(flops=10**8, bytes_accessed=10**6, transcendentals=0),
        name=name,
    )(logdec, bc)


def prepare_prompts(logdec, bc):
    count, heads, positions = logdec.shape
    cuts, rows = count * (positions // BLOCK), BLOCK // CHUNK * bc.shape[2]
    shapes = [(cuts, 2, 2 * BLOCK + 16, heads), (cuts, rows + BLOCK, BLOCK), (cuts, BLOCK, rows)]
    return prepare_call(prompt_prepare_kernel, shapes, "prompt_prepare", logdec, bc)


def prepare_branches(logdec, bc, channels):
    count, heads, positions = logdec.shape
    state = bc.shape[2]
    cuts, rows = count * (positions // BLOCK), BLOCK // CHUNK * state
    shapes = [
        (2 * heads, channels),
        (cuts, 2 * BLOCK + 16, 2 * heads),
        (cuts, rows + BLOCK, BLOCK),
        (cuts, BLOCK, rows),
        (count, positions, heads * state),
    ]
    kernel = functools.partial(branch_prepare_kernel, width=channels // heads)
    out = prepare_call(kernel, shapes, "branch_prepare", logdec, bc)
    return out[:4], out[4]


def run_tiles(jobs):
    scaled, passed = {}, {}
    for g in range(len(jobs) + 2):
        if g < len(jobs):
            scaled[g] = jobs[g][0]()
        if 0 <= g - 1 < len(jobs):
            passed[g - 1] = jobs[g - 1][1](scaled.pop(g - 1))
        if 0 <= g - 2:
            jobs[g - 2][2](passed.pop(g - 2))


def tile_job(ready_refs, at, g, x_of, entering_of, leave, write):
    hot_ref, w_ref, lv_ref, lc_ref = ready_refs
    w_at, at = at
    rows = lc_ref.shape[2]
    chunks = BLOCK // CHUNK
    state = rows // chunks

    def scale():
        wide = jnp.dot(w_ref[w_at], hot_ref[:, pl.ds(g * 256, 256)], preferred_element_type=F32)
        scaled = (x_of().astype(F32) * wide[:BLOCK]).astype(BF16)
        return scaled, wide[BLOCK:BLOCK + 16], wide[BLOCK + 16:]

    def pass_on(given):
        scaled, steps, out_scale = given
        both = jnp.dot(lv_ref[at], scaled, preferred_element_type=F32)
        carries, carry = [], steps[0:1] * entering_of()
        for c in range(chunks):
            carries.append(carry.astype(BF16))
            carry = steps[c + 1:c + 2] * (carry + both[c * state:(c + 1) * state])
        leave(carry)
        return both[rows:], jnp.concatenate(carries, axis=0), out_scale

    def give(given):
        inner, carries, out_scale = given
        carried = jnp.dot(lc_ref[at], carries, preferred_element_type=F32)
        write((inner + carried) * out_scale)

    return scale, pass_on, give


class Copies:
    def __init__(self, sems):
        self.sems, self.started = sems, {}

    def start(self, key, source, target):
        copy = pltpu.make_async_copy(source, target, self.sems.at[key])
        copy.start()
        self.started[key] = copy

    def wait(self, key):
        self.started.pop(key).wait()

    def wait_all(self):
        for key in list(self.started):
            self.wait(key)


def branch_kernel(x_in, *refs, which):
    ready = refs[:4]
    own_ref, x_ref, s_ref, in_sems = refs[4:]
    positions, channels = x_ref.shape
    state = s_ref.shape[0]
    blocks = positions // BLOCK
    lanes = channels // in_sems.shape[1]
    came = Copies(in_sems)
    for b in range(blocks):
        for j in range(channels // lanes):
            spot = (pl.ds(b * BLOCK, BLOCK), pl.ds(j * lanes, lanes))
            came.start((b, j), x_in.at[(which, *spot)], x_ref.at[spot])

    def job(b, g):
        cols = pl.ds(g * 256, 256)
        here = (pl.ds(b * BLOCK, BLOCK), cols)

        def x_of():
            if g * 256 % lanes == 0:
                came.wait((b, g * 256 // lanes))
            return x_ref[here]

        def leave(carry):
            if b < blocks - 1:
                s_ref[:, cols] = carry

        def write(out):
            own_ref[here] = out

        def entering_of():
            return s_ref[:, cols] if b else jnp.zeros((state, 256), F32)

        at = which * blocks + b
        return tile_job(ready, (at, at), g, x_of, entering_of, leave, write)

    run_tiles([job(b, g) for b in range(blocks) for g in range(channels // 256)])


def branch_own(x, ready, which):
    _, positions, channels = x.shape
    state = ready[3].shape[2] * CHUNK // BLOCK
    whole = pl.BlockSpec(memory_space=pltpu.VMEM)
    work = positions * channels
    return pl.pallas_call(
        functools.partial(branch_kernel, which=which),
        in_specs=[pl.BlockSpec(memory_space=pltpu.HBM)] + [whole] * 4,
        out_specs=whole,
        out_shape=jax.ShapeDtypeStruct(x.shape[1:], F32),
        scratch_shapes=[
            pltpu.VMEM((positions, channels), BF16),
            pltpu.VMEM((state, channels), F32),
            pltpu.SemaphoreType.DMA((positions // BLOCK, channels // min(512, channels))),
        ],
        compiler_params=pltpu.CompilerParams(vmem_limit_bytes=VMEM_LIMIT),
        cost_estimate=pl.CostEstimate(
            flops=2 * 1152 * work, bytes_accessed=4 * work, transcendentals=0),
        name="branch_own",
    )(in_hbm(x), *ready)


def prompt_kernel(*refs, skip):
    half_ref, x_ref, *ready, start_ref = refs[:7]
    y_out, y_ref, sems = refs[7 + skip:]
    count, positions, channels = y_ref.shape
    blocks = positions // BLOCK
    half = half_ref[0]
    left = Copies(sems)
    entered = {}

    def job(i, b, g):
        rows = pl.ds(b * BLOCK, BLOCK)
        here = (i, rows, pl.ds(g * 256, 256))
        there = (i, rows, pl.ds(pl.multiple_of(half * channels + g * 256, 256), 256))

        def leave(carry):
            entered[i, g] = carry

        def entering_of():
            return entered[i, g] if b else start_ref[i, :, pl.ds(g * 256, 256)]

        def write(out):
            y_ref[here] = out.astype(BF16)
            left.start((i, b, g), y_ref.at[here], y_out.at[there])

        at = i * blocks + b
        return tile_job(ready, ((at, half), at), g, lambda: x_ref[there], entering_of, leave, write)

    run_tiles([job(i, b, g) for i in range(count) for b in range(blocks) for g in range(channels // 256)])
    left.wait_all()


def prompt_half(half, x, ready, start, into):
    count, positions, channels = x.shape
    part = channels // 2
    whole = pl.BlockSpec(memory_space=pltpu.VMEM)
    hbm = pl.BlockSpec(memory_space=pltpu.HBM)
    work = count * positions * part
    return pl.pallas_call(
        functools.partial(prompt_kernel, skip=len(into)),
        in_specs=[pl.BlockSpec(memory_space=pltpu.SMEM)] + [whole] * 6 + [hbm] * len(into),
        out_specs=hbm,
        out_shape=jax.ShapeDtypeStruct(x.shape, BF16),
        scratch_shapes=[
            pltpu.VMEM((count, positions, part), BF16),
            pltpu.SemaphoreType.DMA((count, positions // BLOCK, part // 256)),
        ],
        input_output_aliases={7 + i: i for i in range(len(into))},
        compiler_params=pltpu.CompilerParams(vmem_limit_bytes=VMEM_LIMIT),
        cost_estimate=pl.CostEstimate(
            flops=2 * 1152 * work, bytes_accessed=4 * work, transcendentals=0),
        name="prompt_half",
    )(half, x, *ready, start, *into)


def finish_kernel(len_ref, prompt_ref, reach_ref, total_ref, *refs, width):
    own_refs, (y_out, y_ref, sems) = refs[:-3], refs[-3:]
    count, positions, channels = y_ref.shape
    prompts, state, _ = total_ref.shape
    group = 128 // state
    span = group * width
    left = Copies(sems)
    own_head = quotient(iota((128, 1), 0), state) == quotient(iota((1, span), 1), width)
    starts = []
    for g in range(channels // span):
        start = total_ref[0, :, pl.ds(g * span, span)]
        for which in range(1, prompts):
            start = jnp.where(prompt_ref[0] == which, total_ref[which, :, pl.ds(g * span, span)], start)
        start = jnp.concatenate([start] * group, axis=0)
        starts.append(jnp.where(own_head, start, 0.0).astype(BF16))
    for i in range(count):
        for g in range(channels // span):
            for b in range(positions // BLOCK):
                rows, cols = pl.ds(b * BLOCK, BLOCK), pl.ds(g * span, span)
                term = jnp.dot(
                    reach_ref[i, rows, pl.ds(g * 128, 128)], starts[g], preferred_element_type=F32)
                live = iota((BLOCK, span), 0) < len_ref[i] - b * BLOCK
                y_ref[i, rows, cols] = jnp.where(live, own_refs[i][rows, cols] + term, 0.0).astype(BF16)
                left.start((i, b, g), y_ref.at[i, rows, cols], y_out.at[i, rows, cols])
    left.wait_all()


def finish(lengths, prompt, reach, total, own):
    count, (positions, channels) = len(own), own[0].shape
    state = total.shape[1]
    width = channels * state // reach.shape[2]
    whole = pl.BlockSpec(memory_space=pltpu.VMEM)
    return pl.pallas_call(
        functools.partial(finish_kernel, width=width),
        in_specs=[pl.BlockSpec(memory_space=pltpu.SMEM)] * 2 + [whole] * (2 + count),
        out_specs=pl.BlockSpec(memory_space=pltpu.HBM),
        out_shape=jax.ShapeDtypeStruct((count, positions, channels), BF16),
        scratch_shapes=[
            pltpu.VMEM((count, positions, channels), BF16),
            pltpu.SemaphoreType.DMA((count, positions // BLOCK, reach.shape[2] // 128)),
        ],
        compiler_params=pltpu.CompilerParams(vmem_limit_bytes=VMEM_LIMIT),
        cost_estimate=pl.CostEstimate(
            flops=2**28, bytes_accessed=2**23, transcendentals=0),
        name="branch_finish",
    )(lengths, prompt, reach, total, *own)


def swap_bit(value, bit, size):
    return lax.ppermute(value, "ctx", [(k, k ^ bit) for k in range(size)])


def pack(states, logs):
    states = states.reshape(-1, states.shape[-1])
    return jnp.concatenate([states, logs.reshape(states.shape[0], -1)], axis=1)


def unpack(packed, count):
    rows = packed.shape[0] // count
    lanes = packed.shape[1] * rows // (rows + 1)
    return packed[:, :lanes].reshape(count, rows, lanes), packed[:, lanes:].reshape(count, 1, lanes)


def in_order(upper, mine, other):
    first = [jnp.where(upper, o, m) for m, o in zip(mine, other)]
    second = [jnp.where(upper, m, o) for m, o in zip(mine, other)]
    return first, second


def join(first, second):
    return jnp.exp(second[1]) * first[0] + second[0], first[1] + second[1]


def spread_step(value, hop, ctx_size, pair_size):
    known = [m for m in range(pair_size) if m & (2 * hop - 1) == 0]
    links = []
    for k in range(ctx_size):
        z = k * pair_size // ctx_size
        links += [(k * pair_size + (z ^ m), k * pair_size + (z ^ m ^ hop)) for m in known]
    return lax.ppermute(value, ("ctx", "pair"), links)


def halvings(size):
    return [size >> k for k in range(1, size.bit_length())]


def places():
    size, pair_size = lax.axis_size("ctx"), lax.axis_size("pair")
    ctx, pair = lax.axis_index("ctx"), lax.axis_index("pair")
    away = pair ^ lax.div(ctx * pair_size, size)
    odd = ctx & 1
    return {
        "odd": odd == 1,
        "half": jnp.reshape(odd, (1,)),
        "other_half": jnp.reshape(1 - odd, (1,)),
        "upper": {bit: (ctx & bit) != 0 for bit in halvings(size)[:-1]},
        "has": {hop: (away & (2 * hop - 1)) == 0 for hop in halvings(pair_size)},
    }


def body(
    prompt_x,
    prompt_bc,
    prompt_logdec,
    branch_x,
    branch_bc,
    branch_logdec,
    branch_prompt,
    branch_len,
):
    size, pair_size = lax.axis_size("ctx"), lax.axis_size("pair")
    prompts, branches = prompt_x.shape[0], branch_x.shape[0]
    assert size == 2 * pair_size and size & (size - 1) == 0 and branch_prompt.shape[0] == 1
    place, prompt_logdec = lax.optimization_barrier((places(), prompt_logdec))
    odd = place["odd"]

    def beside(exchange, value, work, *given):
        value, given = lax.optimization_barrier((value, given))
        got = exchange(value)
        return lax.optimization_barrier((got, work(*given)))

    end, log, held = local_ends(prompt_x, prompt_logdec, prompt_bc)
    half = end.shape[2] // 2
    low, high = (end[:, :, :half], log[:, :1, :half]), (end[:, :, half:], log[:, :1, half:])
    keep = [jnp.where(odd, h, l) for l, h in zip(low, high)]
    send = [jnp.where(odd, l, h) for l, h in zip(low, high)]
    got, (ready, reach) = beside(
        lambda v: swap_bit(v, 1, size),
        pack(*send),
        lambda logdec: prepare_branches(logdec, branch_bc, branch_x.shape[2]),
        branch_logdec,
    )
    got = unpack(got, prompts)
    first, second = in_order(odd, keep, got)
    total, total_log = join(first, second)
    before, before_log = jnp.zeros_like(total), jnp.zeros_like(total_log)

    def part(which):
        def work(x, logdec):
            own = branch_own(x, ready, which)
            return own, prepare_prompts(logdec, prompt_bc) if which == branches - 1 else None

        return work

    done = []
    bit = 2
    while bit < size:
        swap = functools.partial(swap_bit, bit=bit, size=size)
        if len(done) < branches:
            got, out = beside(swap, pack(total, total_log), part(len(done)), branch_x, prompt_logdec)
            done.append(out)
        else:
            got = swap(pack(total, total_log))
        other = unpack(got, prompts)
        upper = place["upper"][bit]
        before = jnp.where(upper, jnp.exp(before_log) * other[0] + before, before)
        before_log = jnp.where(upper, before_log + other[1], before_log)
        total, total_log = join(*in_order(upper, (total, total_log), other))
        bit *= 2
    while len(done) < branches:
        done.append(part(len(done))(branch_x, prompt_logdec))
    own = [out[0] for out in done]
    prompt_ready = (ready[0], *done[-1][1])

    next_before = jnp.exp(first[1]) * before + first[0]
    keep = jnp.where(odd, next_before, before)
    others = swap_bit(jnp.where(odd, before, next_before), 1, size)
    sides = [(place["half"], keep), (place["other_half"], others)]
    prompt_y = ()
    for hop in halvings(pair_size):
        step = functools.partial(spread_step, hop=hop, ctx_size=size, pair_size=pair_size)
        if sides:
            side, entering = sides.pop(0)
            got, prompt_y = beside(
                step, total,
                lambda entering, y: (prompt_half(side, held, prompt_ready, entering, y),), entering, prompt_y)
        else:
            got = step(total)
        total = jnp.where(place["has"][hop], total, got)
    for side, entering in sides:
        prompt_y = (prompt_half(side, held, prompt_ready, entering, prompt_y),)
    branch_y = finish(branch_len, branch_prompt, reach, total, own)
    return prompt_y[0], branch_y


def solution(mesh):
    return jax.shard_map(
        body,
        mesh=mesh,
        in_specs=(
            P(None, "ctx", "pair"),
            P(None, None, None, "ctx"),
            P(None, "pair", "ctx"),
            P("pair", None, "ctx"),
            P(None, "pair", None, None),
            P("pair", "ctx", None),
            P("pair"),
            P("pair"),
        ),
        out_specs=(P(None, "ctx", "pair"), P("pair", None, "ctx")),
        check_vma=False,
    )
```

```python
import functools
import jax
import jax.numpy as jnp
from jax import lax
from jax.experimental import pallas as pl
from jax.experimental.pallas import tpu as pltpu
from jax.sharding import PartitionSpec as P

BLOCK = 256
CHUNK = 32
F32 = jnp.float32
BF16 = jnp.bfloat16
VMEM_LIMIT = 16 * 1024 * 1024


def iota(shape, dim):
    return lax.broadcasted_iota(jnp.int32, shape, dim)


def quotient(index, divisor):
    if divisor & (divisor - 1) == 0:
        return lax.shift_right_logical(index, divisor.bit_length() - 1)
    return lax.div(index, divisor)


def remainder(index, divisor):
    if divisor & (divisor - 1) == 0:
        return index & (divisor - 1)
    return lax.rem(index, divisor)


def exact_dot(a, b):
    return jnp.dot(a, b, preferred_element_type=F32, precision=lax.Precision.HIGHEST)


def gain_of(log_decay):
    z = 2.0 * log_decay
    series = 1.0 + z * (1.0 / 9.0)
    for k in (8, 7, 6, 5, 4, 3, 2):
        series = 1.0 + z * (1.0 / k) * series
    small = -z * series
    large = 1.0 - jnp.exp(z)
    return jnp.sqrt(jnp.maximum(jnp.where(z > -0.5, small, large), 0.0))


def hi_lo(value):
    high = value.astype(BF16).astype(F32)
    return jnp.concatenate([high, value - high], axis=0)


def in_hbm(array):
    return pltpu.with_memory_space_constraint(array, pltpu.HBM)


def split_dot(rows, one_hot):
    count = rows.shape[0]
    high = rows.astype(BF16).astype(F32)
    middle = (rows - high).astype(BF16).astype(F32)
    parts = jnp.concatenate([high, middle, rows - high - middle], axis=0).astype(BF16)
    out = jnp.dot(parts, one_hot, preferred_element_type=F32)
    return out[:count] + out[count:2 * count] + out[2 * count:]


def ends_kernel(
    x_ref, ld_in, bc_in, end_ref, log_ref, held_ref, ld_ref, b_ref, push_ref, sems, first_sems, *, width, lanes
):
    first_copies = [
        pltpu.make_async_copy(ld_in, ld_ref, first_sems.at[0]),
        pltpu.make_async_copy(bc_in.at[0], b_ref, first_sems.at[1]),
    ]
    for copy in first_copies:
        copy.start()
    count, heads, positions = ld_ref.shape
    state = end_ref.shape[1]
    channels = end_ref.shape[2]
    tiles = channels // lanes
    copies = {}
    for i in range(count):
        for j in range(tiles):
            cols = pl.ds(j * lanes, lanes)
            copies[i, j] = pltpu.make_async_copy(
                x_ref.at[i, :, cols], held_ref.at[i, :, cols], sems.at[i, j])
            copies[i, j].start()
    for copy in first_copies:
        copy.wait()
    logs = jnp.concatenate([ld_ref[i] for i in range(count)], axis=0)
    after = jnp.where(iota((positions, 1), 0) > iota((1, positions), 1), 1.0, 0.0)
    to_end = jnp.exp(exact_dot(logs, after)) * gain_of(logs)
    for i in range(count):
        b_rows = b_ref[i].astype(F32)
        push = b_rows[None, :, :] * to_end[i * heads:(i + 1) * heads][:, None, :]
        push_ref[i] = push.reshape(heads * state, positions).astype(BF16)
    group = 256 // width
    lane_head = quotient(iota((1, 256), 1), width)
    for i in range(count):
        totals = lax.dot_general(
            jnp.ones((16, positions), F32), ld_ref[i], (((1,), (1,)), ((), ())),
            preferred_element_type=F32, precision=lax.Precision.HIGHEST)
        for j in range(tiles):
            cols = pl.ds(j * lanes, lanes)
            pick = iota((heads, 1), 0) == quotient(iota((1, lanes), 1), width) + j * (lanes // width)
            log_ref[i, :, cols] = split_dot(totals, jnp.where(pick, 1.0, 0.0).astype(BF16))[:8]
    for i in range(count):
        for j in range(tiles):
            copies[i, j].wait()
            for g in range(lanes // 256):
                first = j * (lanes // width) + g * group
                cols = pl.ds(j * lanes + g * 256, 256)
                both = jnp.dot(
                    push_ref[i, pl.ds(first * state, group * state), :], held_ref[i, :, cols],
                    preferred_element_type=F32)
                end = jnp.where(lane_head == 0, both[:state], 0.0)
                for k in range(1, group):
                    end = jnp.where(lane_head == k, both[k * state:(k + 1) * state], end)
                end_ref[i, :, cols] = end


def local_ends(x, logdec, bc):
    count, positions, channels = x.shape
    heads, state = logdec.shape[1], bc.shape[2]
    width = channels // heads
    lanes = min(1024, channels)
    whole = pl.BlockSpec(memory_space=pltpu.VMEM)
    return pl.pallas_call(
        functools.partial(ends_kernel, width=width, lanes=lanes),
        in_specs=[pl.BlockSpec(memory_space=pltpu.HBM)] * 3,
        out_specs=[whole, whole, whole],
        out_shape=[
            jax.ShapeDtypeStruct((count, state, channels), F32),
            jax.ShapeDtypeStruct((count, 8, channels), F32),
            jax.ShapeDtypeStruct(x.shape, BF16),
        ],
        scratch_shapes=[
            pltpu.VMEM(logdec.shape, F32),
            pltpu.VMEM(bc.shape[1:], BF16),
            pltpu.VMEM((count, heads * state, positions), BF16),
            pltpu.SemaphoreType.DMA((count, channels // lanes)),
            pltpu.SemaphoreType.DMA((2,)),
        ],
        compiler_params=pltpu.CompilerParams(vmem_limit_bytes=VMEM_LIMIT),
        cost_estimate=pl.CostEstimate(
            flops=2 * 64 * x.size, bytes_accessed=2 * x.size, transcendentals=0),
        name="local_ends",
    )(in_hbm(x), in_hbm(logdec), in_hbm(bc))


def prepare(parts, logs, lv_ref, lc_ref, state, heads):
    size = logs.shape[1]
    chunks = size // CHUNK
    half = CHUNK // 2
    src, dst = iota((size, 1), 0), iota((1, size), 1)
    middle = quotient(dst, CHUNK) * CHUNK + half - 1
    plus = (src > middle) & (src <= dst)
    minus = (src > dst) & (src <= middle)
    offset = exact_dot(logs, jnp.where(plus, 1.0, jnp.where(minus, -1.0, 0.0)))
    row_scale = jnp.exp(offset)
    in_scale = jnp.exp(-offset) * gain_of(logs)
    span = iota((1, 128), 1) == quotient(src + half, CHUNK)
    steps = jnp.exp(exact_dot(logs, jnp.where(span, 1.0, 0.0)))
    rows = state * chunks
    mine = quotient(iota((rows, 1), 0), state) == quotient(dst, CHUNK)
    keep = (dst <= src) & (quotient(dst, CHUNK) == quotient(src, CHUNK))
    for i, (b_rows, c_rows) in enumerate(parts):
        b_all = jnp.concatenate([b_rows.astype(F32)] * chunks, axis=0)
        lv_ref[i, pl.ds(0, rows), :] = jnp.where(mine, b_all, 0.0).astype(BF16)
        scores = lax.dot_general(c_rows, b_rows, (((0,), (0,)), ((), ())), preferred_element_type=F32)
        lv_ref[i, pl.ds(rows, size), :] = jnp.where(keep, scores, 0.0).astype(BF16)
        c_all = jnp.concatenate([c_rows.astype(F32)] * chunks, axis=0)
        lc_ref[i] = jnp.where(mine, c_all, 0.0).T.astype(BF16)
    scales = []
    for first in range(0, logs.shape[0], heads):
        here = slice(first, first + heads)
        columns = [hi_lo(in_scale[here]).T, hi_lo(steps[here]).T[:16], hi_lo(row_scale[here]).T]
        scales.append(jnp.concatenate(columns, axis=0).astype(BF16))
    return scales


def cuts_of(ld_ref):
    count, _, positions = ld_ref.shape
    return [(i, pl.ds(b * BLOCK, BLOCK)) for i in range(count) for b in range(positions // BLOCK)]


def prepare_hot(hot_ref, heads, width):
    row_head = remainder(iota((2 * heads, 1), 0), heads)
    for g in range(hot_ref.shape[1] // 256):
        lane_head = quotient(iota((1, 256), 1), width) + g * (256 // width)
        hot_ref[:, pl.ds(g * 256, 256)] = jnp.where(row_head == lane_head, 1.0, 0.0).astype(BF16)


def blocks_of(ld_ref, bc_ref):
    cuts = cuts_of(ld_ref)
    logs = jnp.concatenate([ld_ref[i, :, cut] for i, cut in cuts], axis=0)
    return cuts, logs, [(bc_ref[0, i, :, cut], bc_ref[1, i, :, cut]) for i, cut in cuts]


def prompt_prepare_kernel(ld_ref, bc_ref, w_ref, lv_ref, lc_ref):
    _, logs, parts = blocks_of(ld_ref, bc_ref)
    for k, w in enumerate(prepare(parts, logs, lv_ref, lc_ref, bc_ref.shape[2], ld_ref.shape[1] // 2)):
        w_ref[k // 2, k % 2] = w


def branch_prepare_kernel(ld_ref, bc_ref, hot_ref, w_ref, lv_ref, lc_ref, reach_ref, *, width):
    heads, state = ld_ref.shape[1], bc_ref.shape[2]
    blocks = ld_ref.shape[2] // BLOCK
    cuts, logs, parts = blocks_of(ld_ref, bc_ref)
    for k, w in enumerate(prepare(parts, logs, lv_ref, lc_ref, state, heads)):
        w_ref[k] = w
    prepare_hot(hot_ref, heads, width)
    upto = jnp.where(iota((BLOCK, 1), 0) <= iota((1, BLOCK), 1), 1.0, 0.0)
    runs = exact_dot(logs, upto)
    for k, (i, cut) in enumerate(cuts):
        run = runs[k * heads:(k + 1) * heads]
        if k % blocks:
            run = run + entered
        entered = run[:, BLOCK - 1:BLOCK]
        reach = parts[k][1].astype(F32)[None, :, :] * jnp.exp(run)[:, None, :]
        reach_ref[i, cut, :] = reach.reshape(heads * state, BLOCK).T.astype(BF16)


def prepare_call(kernel, shapes, name, logdec, bc):
    whole = pl.BlockSpec(memory_space=pltpu.VMEM)
    return pl.pallas_call(
        kernel,
        in_specs=[whole] * 2,
        out_specs=[whole] * len(shapes),
        out_shape=[jax.ShapeDtypeStruct(shape, BF16) for shape in shapes],
        compiler_params=pltpu.CompilerParams(vmem_limit_bytes=VMEM_LIMIT),
        cost_estimate=pl.CostEstimate(flops=10**8, bytes_accessed=10**6, transcendentals=0),
        name=name,
    )(logdec, bc)


def prepare_prompts(logdec, bc):
    count, heads, positions = logdec.shape
    cuts, rows = count * (positions // BLOCK), BLOCK // CHUNK * bc.shape[2]
    shapes = [(cuts, 2, 2 * BLOCK + 16, heads), (cuts, rows + BLOCK, BLOCK), (cuts, BLOCK, rows)]
    return prepare_call(prompt_prepare_kernel, shapes, "prompt_prepare", logdec, bc)


def prepare_branches(logdec, bc, channels):
    count, heads, positions = logdec.shape
    state = bc.shape[2]
    cuts, rows = count * (positions // BLOCK), BLOCK // CHUNK * state
    shapes = [
        (2 * heads, channels),
        (cuts, 2 * BLOCK + 16, 2 * heads),
        (cuts, rows + BLOCK, BLOCK),
        (cuts, BLOCK, rows),
        (count, positions, heads * state),
    ]
    kernel = functools.partial(branch_prepare_kernel, width=channels // heads)
    out = prepare_call(kernel, shapes, "branch_prepare", logdec, bc)
    return out[:4], out[4]


def run_tiles(jobs):
    scaled, passed = {}, {}
    for g in range(len(jobs) + 2):
        if g < len(jobs):
            scaled[g] = jobs[g][0]()
        if 0 <= g - 1 < len(jobs):
            passed[g - 1] = jobs[g - 1][1](scaled.pop(g - 1))
        if 0 <= g - 2:
            jobs[g - 2][2](passed.pop(g - 2))


def tile_job(ready_refs, at, g, x_of, entering_of, leave, write):
    hot_ref, w_ref, lv_ref, lc_ref = ready_refs
    w_at, at = at
    rows = lc_ref.shape[2]
    chunks = BLOCK // CHUNK
    state = rows // chunks

    def scale():
        wide = jnp.dot(w_ref[w_at], hot_ref[:, pl.ds(g * 256, 256)], preferred_element_type=F32)
        scaled = (x_of().astype(F32) * wide[:BLOCK]).astype(BF16)
        return scaled, wide[BLOCK:BLOCK + 16], wide[BLOCK + 16:]

    def pass_on(given):
        scaled, steps, out_scale = given
        both = jnp.dot(lv_ref[at], scaled, preferred_element_type=F32)
        carries, carry = [], steps[0:1] * entering_of()
        for c in range(chunks):
            carries.append(carry.astype(BF16))
            carry = steps[c + 1:c + 2] * (carry + both[c * state:(c + 1) * state])
        leave(carry)
        return both[rows:], jnp.concatenate(carries, axis=0), out_scale

    def give(given):
        inner, carries, out_scale = given
        carried = jnp.dot(lc_ref[at], carries, preferred_element_type=F32)
        write((inner + carried) * out_scale)

    return scale, pass_on, give


class Copies:
    def __init__(self, sems):
        self.sems, self.started = sems, {}

    def start(self, key, source, target):
        copy = pltpu.make_async_copy(source, target, self.sems.at[key])
        copy.start()
        self.started[key] = copy

    def wait(self, key):
        self.started.pop(key).wait()

    def wait_all(self):
        for key in list(self.started):
            self.wait(key)


def branch_kernel(x_in, *refs, which):
    ready = refs[:4]
    own_ref, x_ref, s_ref, in_sems = refs[4:]
    positions, channels = x_ref.shape
    state = s_ref.shape[0]
    blocks = positions // BLOCK
    lanes = channels // in_sems.shape[1]
    came = Copies(in_sems)
    for b in range(blocks):
        for j in range(channels // lanes):
            spot = (pl.ds(b * BLOCK, BLOCK), pl.ds(j * lanes, lanes))
            came.start((b, j), x_in.at[(which, *spot)], x_ref.at[spot])

    def job(b, g):
        cols = pl.ds(g * 256, 256)
        here = (pl.ds(b * BLOCK, BLOCK), cols)

        def x_of():
            if g * 256 % lanes == 0:
                came.wait((b, g * 256 // lanes))
            return x_ref[here]

        def leave(carry):
            if b < blocks - 1:
                s_ref[:, cols] = carry

        def write(out):
            own_ref[here] = out

        def entering_of():
            return s_ref[:, cols] if b else jnp.zeros((state, 256), F32)

        at = which * blocks + b
        return tile_job(ready, (at, at), g, x_of, entering_of, leave, write)

    run_tiles([job(b, g) for b in range(blocks) for g in range(channels // 256)])


def branch_own(x, ready, which):
    _, positions, channels = x.shape
    state = ready[3].shape[2] * CHUNK // BLOCK
    whole = pl.BlockSpec(memory_space=pltpu.VMEM)
    work = positions * channels
    return pl.pallas_call(
        functools.partial(branch_kernel, which=which),
        in_specs=[pl.BlockSpec(memory_space=pltpu.HBM)] + [whole] * 4,
        out_specs=whole,
        out_shape=jax.ShapeDtypeStruct(x.shape[1:], F32),
        scratch_shapes=[
            pltpu.VMEM((positions, channels), BF16),
            pltpu.VMEM((state, channels), F32),
            pltpu.SemaphoreType.DMA((positions // BLOCK, channels // min(512, channels))),
        ],
        compiler_params=pltpu.CompilerParams(vmem_limit_bytes=VMEM_LIMIT),
        cost_estimate=pl.CostEstimate(
            flops=2 * 1152 * work, bytes_accessed=4 * work, transcendentals=0),
        name="branch_own",
    )(in_hbm(x), *ready)


def prompt_kernel(*refs, skip):
    half_ref, x_ref, *ready, start_ref = refs[:7]
    y_out, y_ref, sems = refs[7 + skip:]
    count, positions, channels = y_ref.shape
    blocks = positions // BLOCK
    half = half_ref[0]
    left = Copies(sems)
    entered = {}

    def job(i, b, g):
        rows = pl.ds(b * BLOCK, BLOCK)
        here = (i, rows, pl.ds(g * 256, 256))
        there = (i, rows, pl.ds(pl.multiple_of(half * channels + g * 256, 256), 256))

        def leave(carry):
            entered[i, g] = carry

        def entering_of():
            return entered[i, g] if b else start_ref[i, :, pl.ds(g * 256, 256)]

        def write(out):
            y_ref[here] = out.astype(BF16)
            left.start((i, b, g), y_ref.at[here], y_out.at[there])

        at = i * blocks + b
        return tile_job(ready, ((at, half), at), g, lambda: x_ref[there], entering_of, leave, write)

    run_tiles([job(i, b, g) for i in range(count) for b in range(blocks) for g in range(channels // 256)])
    left.wait_all()


def prompt_half(half, x, ready, start, into):
    count, positions, channels = x.shape
    part = channels // 2
    whole = pl.BlockSpec(memory_space=pltpu.VMEM)
    hbm = pl.BlockSpec(memory_space=pltpu.HBM)
    work = count * positions * part
    return pl.pallas_call(
        functools.partial(prompt_kernel, skip=len(into)),
        in_specs=[pl.BlockSpec(memory_space=pltpu.SMEM)] + [whole] * 6 + [hbm] * len(into),
        out_specs=hbm,
        out_shape=jax.ShapeDtypeStruct(x.shape, BF16),
        scratch_shapes=[
            pltpu.VMEM((count, positions, part), BF16),
            pltpu.SemaphoreType.DMA((count, positions // BLOCK, part // 256)),
        ],
        input_output_aliases={7 + i: i for i in range(len(into))},
        compiler_params=pltpu.CompilerParams(vmem_limit_bytes=VMEM_LIMIT),
        cost_estimate=pl.CostEstimate(
            flops=2 * 1152 * work, bytes_accessed=4 * work, transcendentals=0),
        name="prompt_half",
    )(half, x, *ready, start, *into)


def finish_kernel(len_ref, prompt_ref, reach_ref, total_ref, *refs, width):
    own_refs, (y_out, y_ref, sems) = refs[:-3], refs[-3:]
    count, positions, channels = y_ref.shape
    prompts, state, _ = total_ref.shape
    group = 128 // state
    span = group * width
    left = Copies(sems)
    own_head = quotient(iota((128, 1), 0), state) == quotient(iota((1, span), 1), width)
    starts = []
    for g in range(channels // span):
        start = total_ref[0, :, pl.ds(g * span, span)]
        for which in range(1, prompts):
            start = jnp.where(prompt_ref[0] == which, total_ref[which, :, pl.ds(g * span, span)], start)
        start = jnp.concatenate([start] * group, axis=0)
        starts.append(jnp.where(own_head, start, 0.0).astype(BF16))
    for i in range(count):
        for g in range(channels // span):
            for b in range(positions // BLOCK):
                rows, cols = pl.ds(b * BLOCK, BLOCK), pl.ds(g * span, span)
                term = jnp.dot(
                    reach_ref[i, rows, pl.ds(g * 128, 128)], starts[g], preferred_element_type=F32)
                live = iota((BLOCK, span), 0) < len_ref[i] - b * BLOCK
                y_ref[i, rows, cols] = jnp.where(live, own_refs[i][rows, cols] + term, 0.0).astype(BF16)
                left.start((i, b, g), y_ref.at[i, rows, cols], y_out.at[i, rows, cols])
    left.wait_all()


def finish(lengths, prompt, reach, total, own):
    count, (positions, channels) = len(own), own[0].shape
    state = total.shape[1]
    width = channels * state // reach.shape[2]
    whole = pl.BlockSpec(memory_space=pltpu.VMEM)
    return pl.pallas_call(
        functools.partial(finish_kernel, width=width),
        in_specs=[pl.BlockSpec(memory_space=pltpu.SMEM)] * 2 + [whole] * (2 + count),
        out_specs=pl.BlockSpec(memory_space=pltpu.HBM),
        out_shape=jax.ShapeDtypeStruct((count, positions, channels), BF16),
        scratch_shapes=[
            pltpu.VMEM((count, positions, channels), BF16),
            pltpu.SemaphoreType.DMA((count, positions // BLOCK, reach.shape[2] // 128)),
        ],
        compiler_params=pltpu.CompilerParams(vmem_limit_bytes=VMEM_LIMIT),
        cost_estimate=pl.CostEstimate(
            flops=2**28, bytes_accessed=2**23, transcendentals=0),
        name="branch_finish",
    )(lengths, prompt, reach, total, *own)


def swap_bit(values, bit, size):
    links = [(k, k ^ bit) for k in range(size)]
    return jax.tree.map(lambda value: lax.ppermute(value, "ctx", links), values)


def in_order(upper, mine, other):
    first = [jnp.where(upper, o, m) for m, o in zip(mine, other)]
    second = [jnp.where(upper, m, o) for m, o in zip(mine, other)]
    return first, second


def join(first, second):
    return jnp.exp(second[1]) * first[0] + second[0], first[1] + second[1]


def spread_step(value, hop, ctx_size, pair_size):
    known = [m for m in range(pair_size) if m & (2 * hop - 1) == 0]
    links = []
    for k in range(ctx_size):
        z = k * pair_size // ctx_size
        links += [(k * pair_size + (z ^ m), k * pair_size + (z ^ m ^ hop)) for m in known]
    return lax.ppermute(value, ("ctx", "pair"), links)


def halvings(size):
    return [size >> k for k in range(1, size.bit_length())]


def places():
    size, pair_size = lax.axis_size("ctx"), lax.axis_size("pair")
    ctx, pair = lax.axis_index("ctx"), lax.axis_index("pair")
    away = pair ^ lax.div(ctx * pair_size, size)
    odd = ctx & 1
    return {
        "odd": odd == 1,
        "half": jnp.reshape(odd, (1,)),
        "other_half": jnp.reshape(1 - odd, (1,)),
        "upper": {bit: (ctx & bit) != 0 for bit in halvings(size)[:-1]},
        "has": {hop: (away & (2 * hop - 1)) == 0 for hop in halvings(pair_size)},
    }


def body(
    prompt_x,
    prompt_bc,
    prompt_logdec,
    branch_x,
    branch_bc,
    branch_logdec,
    branch_prompt,
    branch_len,
):
    size, pair_size = lax.axis_size("ctx"), lax.axis_size("pair")
    branches = branch_x.shape[0]
    assert size == 2 * pair_size and size & (size - 1) == 0 and branch_prompt.shape[0] == 1
    place, prompt_logdec = lax.optimization_barrier((places(), prompt_logdec))
    odd = place["odd"]

    def beside(exchange, value, work, *given):
        value, given = lax.optimization_barrier((value, given))
        got = exchange(value)
        return lax.optimization_barrier((got, work(*given)))

    end, log, held = local_ends(prompt_x, prompt_logdec, prompt_bc)
    half = end.shape[2] // 2
    low, high = (end[:, :, :half], log[:, :1, :half]), (end[:, :, half:], log[:, :1, half:])
    keep = [jnp.where(odd, h, l) for l, h in zip(low, high)]
    send = [jnp.where(odd, l, h) for l, h in zip(low, high)]
    got, (ready, reach) = beside(
        lambda v: swap_bit(v, 1, size),
        send,
        lambda logdec: prepare_branches(logdec, branch_bc, branch_x.shape[2]),
        branch_logdec,
    )
    first, second = in_order(odd, keep, got)
    total, total_log = join(first, second)
    before, before_log = jnp.zeros_like(total), jnp.zeros_like(total_log)

    def part(which):
        def work(x, logdec):
            own = branch_own(x, ready, which)
            return own, prepare_prompts(logdec, prompt_bc) if which == branches - 1 else None

        return work

    done = []
    bit = 2
    while bit < size:
        swap = functools.partial(swap_bit, bit=bit, size=size)
        if len(done) < branches:
            other, out = beside(swap, (total, total_log), part(len(done)), branch_x, prompt_logdec)
            done.append(out)
        else:
            other = swap((total, total_log))
        upper = place["upper"][bit]
        before = jnp.where(upper, jnp.exp(before_log) * other[0] + before, before)
        before_log = jnp.where(upper, before_log + other[1], before_log)
        total, total_log = join(*in_order(upper, (total, total_log), other))
        bit *= 2
    while len(done) < branches:
        done.append(part(len(done))(branch_x, prompt_logdec))
    own = [out[0] for out in done]
    prompt_ready = (ready[0], *done[-1][1])

    next_before = jnp.exp(first[1]) * before + first[0]
    keep = jnp.where(odd, next_before, before)
    others = swap_bit(jnp.where(odd, before, next_before), 1, size)
    sides = [(place["half"], keep), (place["other_half"], others)]
    prompt_y = ()
    for hop in halvings(pair_size):
        step = functools.partial(spread_step, hop=hop, ctx_size=size, pair_size=pair_size)
        if sides:
            side, entering = sides.pop(0)
            got, prompt_y = beside(
                step, total,
                lambda entering, y: (prompt_half(side, held, prompt_ready, entering, y),), entering, prompt_y)
        else:
            got = step(total)
        total = jnp.where(place["has"][hop], total, got)
    for side, entering in sides:
        prompt_y = (prompt_half(side, held, prompt_ready, entering, prompt_y),)
    branch_y = finish(branch_len, branch_prompt, reach, total, own)
    return prompt_y[0], branch_y


def solution(mesh):
    return jax.shard_map(
        body,
        mesh=mesh,
        in_specs=(
            P(None, "ctx", "pair"),
            P(None, None, None, "ctx"),
            P(None, "pair", "ctx"),
            P("pair", None, "ctx"),
            P(None, "pair", None, None),
            P("pair", "ctx", None),
            P("pair"),
            P("pair"),
        ),
        out_specs=(P(None, "ctx", "pair"), P("pair", None, "ctx")),
        check_vma=False,
    )
```

```python
import functools
import jax
import jax.numpy as jnp
from jax import lax
from jax.experimental import pallas as pl
from jax.experimental.pallas import tpu as pltpu
from jax.sharding import PartitionSpec as P

BLOCK = 256
CHUNK = 32
F32 = jnp.float32
BF16 = jnp.bfloat16
VMEM_LIMIT = 16 * 1024 * 1024


def iota(shape, dim):
    return lax.broadcasted_iota(jnp.int32, shape, dim)


def quotient(index, divisor):
    if divisor & (divisor - 1) == 0:
        return lax.shift_right_logical(index, divisor.bit_length() - 1)
    return lax.div(index, divisor)


def remainder(index, divisor):
    if divisor & (divisor - 1) == 0:
        return index & (divisor - 1)
    return lax.rem(index, divisor)


def exact_dot(a, b):
    return jnp.dot(a, b, preferred_element_type=F32, precision=lax.Precision.HIGHEST)


def gain_of(log_decay):
    z = 2.0 * log_decay
    series = 1.0 + z * (1.0 / 9.0)
    for k in (8, 7, 6, 5, 4, 3, 2):
        series = 1.0 + z * (1.0 / k) * series
    small = -z * series
    large = 1.0 - jnp.exp(z)
    return jnp.sqrt(jnp.maximum(jnp.where(z > -0.5, small, large), 0.0))


def hi_lo(value):
    high = value.astype(BF16).astype(F32)
    return jnp.concatenate([high, value - high], axis=0)


def in_hbm(array):
    return pltpu.with_memory_space_constraint(array, pltpu.HBM)


def split_dot(rows, one_hot):
    count = rows.shape[0]
    high = rows.astype(BF16).astype(F32)
    middle = (rows - high).astype(BF16).astype(F32)
    parts = jnp.concatenate([high, middle, rows - high - middle], axis=0).astype(BF16)
    out = jnp.dot(parts, one_hot, preferred_element_type=F32)
    return out[:count] + out[count:2 * count] + out[2 * count:]


def ends_kernel(
    x_ref, ld_in, bc_in, end_ref, log_ref, held_ref, ld_ref, b_ref, push_ref, sems, first_sems, *, width, lanes
):
    first_copies = [
        pltpu.make_async_copy(ld_in, ld_ref, first_sems.at[0]),
        pltpu.make_async_copy(bc_in.at[0], b_ref, first_sems.at[1]),
    ]
    for copy in first_copies:
        copy.start()
    count, heads, positions = ld_ref.shape
    state = end_ref.shape[1]
    channels = end_ref.shape[2]
    tiles = channels // lanes
    copies = {}
    for i in range(count):
        for j in range(tiles):
            cols = pl.ds(j * lanes, lanes)
            copies[i, j] = pltpu.make_async_copy(
                x_ref.at[i, :, cols], held_ref.at[i, :, cols], sems.at[i, j])
            copies[i, j].start()
    for copy in first_copies:
        copy.wait()
    logs = jnp.concatenate([ld_ref[i] for i in range(count)], axis=0)
    after = jnp.where(iota((positions, 1), 0) > iota((1, positions), 1), 1.0, 0.0)
    to_end = jnp.exp(exact_dot(logs, after)) * gain_of(logs)
    for i in range(count):
        b_rows = b_ref[i].astype(F32)
        push = b_rows[None, :, :] * to_end[i * heads:(i + 1) * heads][:, None, :]
        push_ref[i] = push.reshape(heads * state, positions).astype(BF16)
    group = 256 // width
    lane_head = quotient(iota((1, 256), 1), width)
    high = logs.astype(BF16)
    middle = (logs - high.astype(F32)).astype(BF16)
    low = (logs - high.astype(F32) - middle.astype(F32)).astype(BF16)
    totals = sum(
        lax.dot_general(
            jnp.ones((16, positions), BF16), part, (((1,), (1,)), ((), ())), preferred_element_type=F32)
        for part in (high, middle, low))
    totals = jnp.concatenate([totals[:8, i * heads:(i + 1) * heads] for i in range(count)], axis=0)
    for j in range(tiles):
        pick = iota((heads, 1), 0) == quotient(iota((1, lanes), 1), width) + j * (lanes // width)
        wide = split_dot(totals, jnp.where(pick, 1.0, 0.0).astype(BF16))
        for i in range(count):
            log_ref[i, :, pl.ds(j * lanes, lanes)] = wide[8 * i:8 * i + 8]
    for i in range(count):
        for j in range(tiles):
            copies[i, j].wait()
            for g in range(lanes // 256):
                first = j * (lanes // width) + g * group
                cols = pl.ds(j * lanes + g * 256, 256)
                both = jnp.dot(
                    push_ref[i, pl.ds(first * state, group * state), :], held_ref[i, :, cols],
                    preferred_element_type=F32)
                end = jnp.where(lane_head == 0, both[:state], 0.0)
                for k in range(1, group):
                    end = jnp.where(lane_head == k, both[k * state:(k + 1) * state], end)
                end_ref[i, :, cols] = end


def local_ends(x, logdec, bc):
    count, positions, channels = x.shape
    heads, state = logdec.shape[1], bc.shape[2]
    width = channels // heads
    lanes = min(1024, channels)
    whole = pl.BlockSpec(memory_space=pltpu.VMEM)
    return pl.pallas_call(
        functools.partial(ends_kernel, width=width, lanes=lanes),
        in_specs=[pl.BlockSpec(memory_space=pltpu.HBM)] * 3,
        out_specs=[whole, whole, whole],
        out_shape=[
            jax.ShapeDtypeStruct((count, state, channels), F32),
            jax.ShapeDtypeStruct((count, 8, channels), F32),
            jax.ShapeDtypeStruct(x.shape, BF16),
        ],
        scratch_shapes=[
            pltpu.VMEM(logdec.shape, F32),
            pltpu.VMEM(bc.shape[1:], BF16),
            pltpu.VMEM((count, heads * state, positions), BF16),
            pltpu.SemaphoreType.DMA((count, channels // lanes)),
            pltpu.SemaphoreType.DMA((2,)),
        ],
        compiler_params=pltpu.CompilerParams(vmem_limit_bytes=VMEM_LIMIT),
        cost_estimate=pl.CostEstimate(
            flops=2 * 64 * x.size, bytes_accessed=2 * x.size, transcendentals=0),
        name="local_ends",
    )(in_hbm(x), in_hbm(logdec), in_hbm(bc))


def prepare(parts, logs, lv_ref, lc_ref, state, heads):
    size = logs.shape[1]
    chunks = size // CHUNK
    half = CHUNK // 2
    src, dst = iota((size, 1), 0), iota((1, size), 1)
    middle = quotient(dst, CHUNK) * CHUNK + half - 1
    plus = (src > middle) & (src <= dst)
    minus = (src > dst) & (src <= middle)
    offset = exact_dot(logs, jnp.where(plus, 1.0, jnp.where(minus, -1.0, 0.0)))
    row_scale = jnp.exp(offset)
    in_scale = jnp.exp(-offset) * gain_of(logs)
    span = iota((1, 128), 1) == quotient(src + half, CHUNK)
    steps = jnp.exp(exact_dot(logs, jnp.where(span, 1.0, 0.0)))
    rows = state * chunks
    mine = quotient(iota((rows, 1), 0), state) == quotient(dst, CHUNK)
    keep = (dst <= src) & (quotient(dst, CHUNK) == quotient(src, CHUNK))
    for i, (b_rows, c_rows) in enumerate(parts):
        b_all = jnp.concatenate([b_rows.astype(F32)] * chunks, axis=0)
        lv_ref[i, pl.ds(0, rows), :] = jnp.where(mine, b_all, 0.0).astype(BF16)
        scores = lax.dot_general(c_rows, b_rows, (((0,), (0,)), ((), ())), preferred_element_type=F32)
        lv_ref[i, pl.ds(rows, size), :] = jnp.where(keep, scores, 0.0).astype(BF16)
        c_all = jnp.concatenate([c_rows.astype(F32)] * chunks, axis=0)
        lc_ref[i] = jnp.where(mine, c_all, 0.0).T.astype(BF16)
    scales = []
    for first in range(0, logs.shape[0], heads):
        here = slice(first, first + heads)
        columns = [hi_lo(in_scale[here]).T, hi_lo(steps[here]).T[:16], hi_lo(row_scale[here]).T]
        scales.append(jnp.concatenate(columns, axis=0).astype(BF16))
    return scales


def cuts_of(ld_ref):
    count, _, positions = ld_ref.shape
    return [(i, pl.ds(b * BLOCK, BLOCK)) for i in range(count) for b in range(positions // BLOCK)]


def prepare_hot(hot_ref, heads, width):
    row_head = remainder(iota((2 * heads, 1), 0), heads)
    for g in range(hot_ref.shape[1] // 256):
        lane_head = quotient(iota((1, 256), 1), width) + g * (256 // width)
        hot_ref[:, pl.ds(g * 256, 256)] = jnp.where(row_head == lane_head, 1.0, 0.0).astype(BF16)


def blocks_of(ld_ref, bc_ref):
    cuts = cuts_of(ld_ref)
    logs = jnp.concatenate([ld_ref[i, :, cut] for i, cut in cuts], axis=0)
    return cuts, logs, [(bc_ref[0, i, :, cut], bc_ref[1, i, :, cut]) for i, cut in cuts]


def prompt_prepare_kernel(ld_ref, bc_ref, w_ref, lv_ref, lc_ref):
    _, logs, parts = blocks_of(ld_ref, bc_ref)
    for k, w in enumerate(prepare(parts, logs, lv_ref, lc_ref, bc_ref.shape[2], ld_ref.shape[1] // 2)):
        w_ref[k // 2, k % 2] = w


def branch_prepare_kernel(prompt_ref, ld_ref, bc_ref, hot_ref, w_ref, lv_ref, lc_ref, reach_ref, row_ref, *, width):
    row_ref[...] = jnp.full(row_ref.shape, prompt_ref[0], jnp.int32).astype(F32)
    heads, state = ld_ref.shape[1], bc_ref.shape[2]
    blocks = ld_ref.shape[2] // BLOCK
    cuts, logs, parts = blocks_of(ld_ref, bc_ref)
    for k, w in enumerate(prepare(parts, logs, lv_ref, lc_ref, state, heads)):
        w_ref[k] = w
    prepare_hot(hot_ref, heads, width)
    upto = jnp.where(iota((BLOCK, 1), 0) <= iota((1, BLOCK), 1), 1.0, 0.0)
    runs = exact_dot(logs, upto)
    for k, (i, cut) in enumerate(cuts):
        run = runs[k * heads:(k + 1) * heads]
        if k % blocks:
            run = run + entered
        entered = run[:, BLOCK - 1:BLOCK]
        reach = parts[k][1].astype(F32)[None, :, :] * jnp.exp(run)[:, None, :]
        reach_ref[i, cut, :] = reach.reshape(heads * state, BLOCK).T.astype(BF16)


def prepare_call(kernel, shapes, name, *args):
    whole = pl.BlockSpec(memory_space=pltpu.VMEM)
    scalars = [pl.BlockSpec(memory_space=pltpu.SMEM)] * (len(args) - 2)
    return pl.pallas_call(
        kernel,
        in_specs=scalars + [whole] * 2,
        out_specs=[whole] * len(shapes),
        out_shape=[jax.ShapeDtypeStruct(*shape) for shape in shapes],
        compiler_params=pltpu.CompilerParams(vmem_limit_bytes=VMEM_LIMIT),
        cost_estimate=pl.CostEstimate(flops=10**8, bytes_accessed=10**6, transcendentals=0),
        name=name,
    )(*args)


def prepare_prompts(logdec, bc):
    count, heads, positions = logdec.shape
    cuts, rows = count * (positions // BLOCK), BLOCK // CHUNK * bc.shape[2]
    shapes = [(cuts, 2, 2 * BLOCK + 16, heads), (cuts, rows + BLOCK, BLOCK), (cuts, BLOCK, rows)]
    shapes = [(shape, BF16) for shape in shapes]
    return prepare_call(prompt_prepare_kernel, shapes, "prompt_prepare", logdec, bc)


def prepare_branches(prompt, logdec, bc, channels):
    count, heads, positions = logdec.shape
    state = bc.shape[2]
    cuts, rows = count * (positions // BLOCK), BLOCK // CHUNK * state
    shapes = [
        ((2 * heads, channels), BF16),
        ((cuts, 2 * BLOCK + 16, 2 * heads), BF16),
        ((cuts, rows + BLOCK, BLOCK), BF16),
        ((cuts, BLOCK, rows), BF16),
        ((count, positions, heads * state), BF16),
        ((1, channels), F32),
    ]
    kernel = functools.partial(branch_prepare_kernel, width=channels // heads)
    out = prepare_call(kernel, shapes, "branch_prepare", prompt, logdec, bc)
    return out[:4], out[4], out[5]


def run_tiles(jobs):
    scaled, passed = {}, {}
    for g in range(len(jobs) + 2):
        if g < len(jobs):
            scaled[g] = jobs[g][0]()
        if 0 <= g - 1 < len(jobs):
            passed[g - 1] = jobs[g - 1][1](scaled.pop(g - 1))
        if 0 <= g - 2:
            jobs[g - 2][2](passed.pop(g - 2))


def tile_job(ready_refs, at, g, x_of, entering_of, leave, write):
    hot_ref, w_ref, lv_ref, lc_ref = ready_refs
    w_at, at = at
    rows = lc_ref.shape[2]
    chunks = BLOCK // CHUNK
    state = rows // chunks

    def scale():
        wide = jnp.dot(w_ref[w_at], hot_ref[:, pl.ds(g * 256, 256)], preferred_element_type=F32)
        scaled = (x_of().astype(F32) * wide[:BLOCK]).astype(BF16)
        return scaled, wide[BLOCK:BLOCK + 16], wide[BLOCK + 16:]

    def pass_on(given):
        scaled, steps, out_scale = given
        both = jnp.dot(lv_ref[at], scaled, preferred_element_type=F32)
        carries, carry = [], steps[0:1] * entering_of()
        for c in range(chunks):
            carries.append(carry.astype(BF16))
            carry = steps[c + 1:c + 2] * (carry + both[c * state:(c + 1) * state])
        leave(carry)
        return both[rows:], jnp.concatenate(carries, axis=0), out_scale

    def give(given):
        inner, carries, out_scale = given
        carried = jnp.dot(lc_ref[at], carries, preferred_element_type=F32)
        write((inner + carried) * out_scale)

    return scale, pass_on, give


class Copies:
    def __init__(self, sems):
        self.sems, self.started = sems, {}

    def start(self, key, source, target):
        copy = pltpu.make_async_copy(source, target, self.sems.at[key])
        copy.start()
        self.started[key] = copy

    def wait(self, key):
        self.started.pop(key).wait()

    def wait_all(self):
        for key in list(self.started):
            self.wait(key)


def branch_kernel(x_in, *refs, which):
    ready = refs[:4]
    own_ref, x_ref, s_ref, in_sems = refs[4:]
    positions, channels = x_ref.shape
    state = s_ref.shape[0]
    blocks = positions // BLOCK
    lanes = channels // in_sems.shape[1]
    came = Copies(in_sems)
    for b in range(blocks):
        for j in range(channels // lanes):
            spot = (pl.ds(b * BLOCK, BLOCK), pl.ds(j * lanes, lanes))
            came.start((b, j), x_in.at[(which, *spot)], x_ref.at[spot])

    def job(b, g):
        cols = pl.ds(g * 256, 256)
        here = (pl.ds(b * BLOCK, BLOCK), cols)

        def x_of():
            if g * 256 % lanes == 0:
                came.wait((b, g * 256 // lanes))
            return x_ref[here]

        def leave(carry):
            if b < blocks - 1:
                s_ref[:, cols] = carry

        def write(out):
            own_ref[here] = out

        def entering_of():
            return s_ref[:, cols] if b else jnp.zeros((state, 256), F32)

        at = which * blocks + b
        return tile_job(ready, (at, at), g, x_of, entering_of, leave, write)

    run_tiles([job(b, g) for b in range(blocks) for g in range(channels // 256)])


def branch_own(x, ready, which):
    _, positions, channels = x.shape
    state = ready[3].shape[2] * CHUNK // BLOCK
    whole = pl.BlockSpec(memory_space=pltpu.VMEM)
    work = positions * channels
    return pl.pallas_call(
        functools.partial(branch_kernel, which=which),
        in_specs=[pl.BlockSpec(memory_space=pltpu.HBM)] + [whole] * 4,
        out_specs=whole,
        out_shape=jax.ShapeDtypeStruct(x.shape[1:], F32),
        scratch_shapes=[
            pltpu.VMEM((positions, channels), BF16),
            pltpu.VMEM((state, channels), F32),
            pltpu.SemaphoreType.DMA((positions // BLOCK, channels // min(512, channels))),
        ],
        compiler_params=pltpu.CompilerParams(vmem_limit_bytes=VMEM_LIMIT),
        cost_estimate=pl.CostEstimate(
            flops=2 * 1152 * work, bytes_accessed=4 * work, transcendentals=0),
        name="branch_own",
    )(in_hbm(x), *ready)


def prompt_kernel(*refs, skip):
    half_ref, x_ref, *ready, start_ref = refs[:7]
    y_out, y_ref, sems = refs[7 + skip:]
    count, positions, channels = y_ref.shape
    blocks = positions // BLOCK
    half = half_ref[0]
    left = Copies(sems)
    entered = {}

    def job(i, b, g):
        rows = pl.ds(b * BLOCK, BLOCK)
        here = (i, rows, pl.ds(g * 256, 256))
        there = (i, rows, pl.ds(pl.multiple_of(half * channels + g * 256, 256), 256))

        def leave(carry):
            entered[i, g] = carry

        def entering_of():
            return entered[i, g] if b else start_ref[i, :, pl.ds(g * 256, 256)]

        def write(out):
            y_ref[here] = out.astype(BF16)
            left.start((i, b, g), y_ref.at[here], y_out.at[there])

        at = i * blocks + b
        return tile_job(ready, ((at, half), at), g, lambda: x_ref[there], entering_of, leave, write)

    run_tiles([job(i, b, g) for i in range(count) for b in range(blocks) for g in range(channels // 256)])
    left.wait_all()


def prompt_half(half, x, ready, start, into):
    count, positions, channels = x.shape
    part = channels // 2
    whole = pl.BlockSpec(memory_space=pltpu.VMEM)
    hbm = pl.BlockSpec(memory_space=pltpu.HBM)
    work = count * positions * part
    return pl.pallas_call(
        functools.partial(prompt_kernel, skip=len(into)),
        in_specs=[pl.BlockSpec(memory_space=pltpu.SMEM)] + [whole] * 6 + [hbm] * len(into),
        out_specs=hbm,
        out_shape=jax.ShapeDtypeStruct(x.shape, BF16),
        scratch_shapes=[
            pltpu.VMEM((count, positions, part), BF16),
            pltpu.SemaphoreType.DMA((count, positions // BLOCK, part // 256)),
        ],
        input_output_aliases={7 + i: i for i in range(len(into))},
        compiler_params=pltpu.CompilerParams(vmem_limit_bytes=VMEM_LIMIT),
        cost_estimate=pl.CostEstimate(
            flops=2 * 1152 * work, bytes_accessed=4 * work, transcendentals=0),
        name="prompt_half",
    )(half, x, *ready, start, *into)


def finish_kernel(len_ref, reach_ref, start_ref, *refs, width):
    own_refs, (y_out, y_ref, sems) = refs[:-3], refs[-3:]
    count, positions, channels = y_ref.shape
    state = start_ref.shape[0]
    group = 128 // state
    span = group * width
    left = Copies(sems)
    own_head = quotient(iota((128, 1), 0), state) == quotient(iota((1, span), 1), width)
    for g in range(channels // span):
        cols = pl.ds(g * span, span)
        start = jnp.concatenate([start_ref[:, cols]] * group, axis=0)
        start = jnp.where(own_head, start, 0.0).astype(BF16)
        for i in range(count):
            for b in range(positions // BLOCK):
                rows = pl.ds(b * BLOCK, BLOCK)
                term = jnp.dot(
                    reach_ref[i, rows, pl.ds(g * 128, 128)], start, preferred_element_type=F32)
                live = iota((BLOCK, span), 0) < len_ref[i] - b * BLOCK
                y_ref[i, rows, cols] = jnp.where(live, own_refs[i][rows, cols] + term, 0.0).astype(BF16)
                left.start((i, b, g), y_ref.at[i, rows, cols], y_out.at[i, rows, cols])
    left.wait_all()


def finish(lengths, reach, start, own):
    count, (positions, channels) = len(own), own[0].shape
    state = start.shape[0]
    width = channels * state // reach.shape[2]
    whole = pl.BlockSpec(memory_space=pltpu.VMEM)
    return pl.pallas_call(
        functools.partial(finish_kernel, width=width),
        in_specs=[pl.BlockSpec(memory_space=pltpu.SMEM)] + [whole] * (2 + count),
        out_specs=pl.BlockSpec(memory_space=pltpu.HBM),
        out_shape=jax.ShapeDtypeStruct((count, positions, channels), BF16),
        scratch_shapes=[
            pltpu.VMEM((count, positions, channels), BF16),
            pltpu.SemaphoreType.DMA((count, positions // BLOCK, reach.shape[2] // 128)),
        ],
        compiler_params=pltpu.CompilerParams(vmem_limit_bytes=VMEM_LIMIT),
        cost_estimate=pl.CostEstimate(
            flops=2**28, bytes_accessed=2**23, transcendentals=0),
        name="branch_finish",
    )(lengths, reach, start, *own)


def swap_bit(values, bit, size):
    links = [(k, k ^ bit) for k in range(size)]
    return jax.tree.map(lambda value: lax.ppermute(value, "ctx", links), values)


def in_order(upper, mine, other):
    first = [jnp.where(upper, o, m) for m, o in zip(mine, other)]
    second = [jnp.where(upper, m, o) for m, o in zip(mine, other)]
    return first, second


def join(first, second):
    return jnp.exp(second[1]) * first[0] + second[0], first[1] + second[1]


def spread_step(value, hop, ctx_size, pair_size):
    known = [m for m in range(pair_size) if m & (2 * hop - 1) == 0]
    links = []
    for k in range(ctx_size):
        z = k * pair_size // ctx_size
        links += [(k * pair_size + (z ^ m), k * pair_size + (z ^ m ^ hop)) for m in known]
    return lax.ppermute(value, ("ctx", "pair"), links)


def halvings(size):
    return [size >> k for k in range(1, size.bit_length())]


def places():
    size, pair_size = lax.axis_size("ctx"), lax.axis_size("pair")
    ctx, pair = lax.axis_index("ctx"), lax.axis_index("pair")
    away = pair ^ lax.div(ctx * pair_size, size)
    odd = ctx & 1
    return {
        "odd": odd == 1,
        "half": jnp.reshape(odd, (1,)),
        "other_half": jnp.reshape(1 - odd, (1,)),
        "upper": {bit: (ctx & bit) != 0 for bit in halvings(size)[:-1]},
        "has": {hop: (away & (2 * hop - 1)) == 0 for hop in halvings(pair_size)},
    }


def body(
    prompt_x,
    prompt_bc,
    prompt_logdec,
    branch_x,
    branch_bc,
    branch_logdec,
    branch_prompt,
    branch_len,
):
    size, pair_size = lax.axis_size("ctx"), lax.axis_size("pair")
    branches = branch_x.shape[0]
    assert size == 2 * pair_size and size & (size - 1) == 0 and branch_prompt.shape[0] == 1
    place, prompt_logdec = lax.optimization_barrier((places(), prompt_logdec))
    odd = place["odd"]

    def beside(exchange, value, work, *given):
        value, given = lax.optimization_barrier((value, given))
        got = exchange(value)
        return lax.optimization_barrier((got, work(*given)))

    end, log, held = local_ends(prompt_x, prompt_logdec, prompt_bc)
    half = end.shape[2] // 2
    low, high = (end[:, :, :half], log[:, :1, :half]), (end[:, :, half:], log[:, :1, half:])
    keep = [jnp.where(odd, h, l) for l, h in zip(low, high)]
    send = [jnp.where(odd, l, h) for l, h in zip(low, high)]
    got, (ready, reach, row) = beside(
        lambda v: swap_bit(v, 1, size),
        send,
        lambda logdec: prepare_branches(branch_prompt, logdec, branch_bc, branch_x.shape[2]),
        branch_logdec,
    )
    first, second = in_order(odd, keep, got)
    total, total_log = join(first, second)
    before, before_log = jnp.zeros_like(total), jnp.zeros_like(total_log)

    def chosen(total, row):
        out = total[0]
        for which in range(1, total.shape[0]):
            out = jnp.where(row == which, total[which], out)
        return out

    def part(which):
        def work(x, logdec):
            own = branch_own(x, ready, which)
            return own, prepare_prompts(logdec, prompt_bc) if which == branches - 1 else None

        return work

    done = []
    bit = 2
    while bit < size:
        swap = functools.partial(swap_bit, bit=bit, size=size)
        if not done:
            def with_row(values):
                return swap(values[:2]), lax.ppermute(values[2], "pair", [(z, z ^ 1) for z in range(pair_size)])

            (other, next_row), out = beside(
                with_row, (total, total_log, row), part(0), branch_x, prompt_logdec)
            done.append(out)
        elif len(done) < branches:
            other, out = beside(swap, (total, total_log), part(len(done)), branch_x, prompt_logdec)
            done.append(out)
        else:
            other = swap((total, total_log))
        upper = place["upper"][bit]
        before = jnp.where(upper, jnp.exp(before_log) * other[0] + before, before)
        before_log = jnp.where(upper, before_log + other[1], before_log)
        total, total_log = join(*in_order(upper, (total, total_log), other))
        bit *= 2
    while len(done) < branches:
        done.append(part(len(done))(branch_x, prompt_logdec))
    own = [out[0] for out in done]
    prompt_ready = (ready[0], *done[-1][1])

    next_before = jnp.exp(first[1]) * before + first[0]
    keep = jnp.where(odd, next_before, before)
    others = swap_bit(jnp.where(odd, before, next_before), 1, size)
    sides = [(place["half"], keep), (place["other_half"], others)]
    prompt_y = ()
    for hop in halvings(pair_size):
        step = functools.partial(spread_step, hop=hop, ctx_size=size, pair_size=pair_size)
        value = total if hop > 1 else chosen(total, next_row)
        if sides:
            side, entering = sides.pop(0)
            got, prompt_y = beside(
                step, value,
                lambda entering, y: (prompt_half(side, held, prompt_ready, entering, y),), entering, prompt_y)
        else:
            got = step(value)
        if hop > 1:
            total = jnp.where(place["has"][hop], total, got)
    for side, entering in sides:
        prompt_y = (prompt_half(side, held, prompt_ready, entering, prompt_y),)
    start = jnp.where(place["has"][1], chosen(total, row), got)
    branch_y = finish(branch_len, reach, start, own)
    return prompt_y[0], branch_y


def solution(mesh):
    return jax.shard_map(
        body,
        mesh=mesh,
        in_specs=(
            P(None, "ctx", "pair"),
            P(None, None, None, "ctx"),
            P(None, "pair", "ctx"),
            P("pair", None, "ctx"),
            P(None, "pair", None, None),
            P("pair", "ctx", None),
            P("pair"),
            P("pair"),
        ),
        out_specs=(P(None, "ctx", "pair"), P("pair", None, "ctx")),
        check_vma=False,
    )
```

```python
import functools
import jax
import jax.numpy as jnp
from jax import lax
from jax.experimental import pallas as pl
from jax.experimental.pallas import tpu as pltpu
from jax.sharding import PartitionSpec as P

BLOCK = 256
CHUNK = 32
F32 = jnp.float32
BF16 = jnp.bfloat16
VMEM_LIMIT = 16 * 1024 * 1024


def iota(shape, dim):
    return lax.broadcasted_iota(jnp.int32, shape, dim)


def quotient(index, divisor):
    if divisor & (divisor - 1) == 0:
        return lax.shift_right_logical(index, divisor.bit_length() - 1)
    return lax.div(index, divisor)


def remainder(index, divisor):
    if divisor & (divisor - 1) == 0:
        return index & (divisor - 1)
    return lax.rem(index, divisor)


def exact_dot(a, b):
    return jnp.dot(a, b, preferred_element_type=F32, precision=lax.Precision.HIGHEST)


def gain_of(log_decay):
    z = 2.0 * log_decay
    series = 1.0 + z * (1.0 / 9.0)
    for k in (8, 7, 6, 5, 4, 3, 2):
        series = 1.0 + z * (1.0 / k) * series
    small = -z * series
    large = 1.0 - jnp.exp(z)
    return jnp.sqrt(jnp.maximum(jnp.where(z > -0.5, small, large), 0.0))


def hi_lo(value):
    high = value.astype(BF16).astype(F32)
    return jnp.concatenate([high, value - high], axis=0)


def in_hbm(array):
    return pltpu.with_memory_space_constraint(array, pltpu.HBM)


def split_dot(rows, one_hot):
    count = rows.shape[0]
    high = rows.astype(BF16).astype(F32)
    middle = (rows - high).astype(BF16).astype(F32)
    parts = jnp.concatenate([high, middle, rows - high - middle], axis=0).astype(BF16)
    out = jnp.dot(parts, one_hot, preferred_element_type=F32)
    return out[:count] + out[count:2 * count] + out[2 * count:]


def ends_kernel(
    x_ref, ld_in, bc_in, end_ref, log_ref, held_ref, ld_ref, b_ref, push_ref, sems, first_sems, *, width, lanes
):
    first_copies = [
        pltpu.make_async_copy(ld_in, ld_ref, first_sems.at[0]),
        pltpu.make_async_copy(bc_in.at[0], b_ref, first_sems.at[1]),
    ]
    for copy in first_copies:
        copy.start()
    count, heads, positions = ld_ref.shape
    state = end_ref.shape[1]
    channels = end_ref.shape[2]
    tiles = channels // lanes
    copies = {}
    for i in range(count):
        for j in range(tiles):
            cols = pl.ds(j * lanes, lanes)
            copies[i, j] = pltpu.make_async_copy(
                x_ref.at[i, :, cols], held_ref.at[i, :, cols], sems.at[i, j])
            copies[i, j].start()
    for copy in first_copies:
        copy.wait()
    logs = jnp.concatenate([ld_ref[i] for i in range(count)], axis=0)
    after = jnp.where(iota((positions, 1), 0) > iota((1, positions), 1), 1.0, 0.0)
    to_end = jnp.exp(exact_dot(logs, after)) * gain_of(logs)
    group = 256 // width
    lane_head = quotient(iota((1, 256), 1), width)
    high = logs.astype(BF16)
    middle = (logs - high.astype(F32)).astype(BF16)
    low = (logs - high.astype(F32) - middle.astype(F32)).astype(BF16)
    totals = sum(
        lax.dot_general(
            jnp.ones((16, positions), BF16), part, (((1,), (1,)), ((), ())), preferred_element_type=F32)
        for part in (high, middle, low))
    totals = jnp.concatenate([totals[:8, i * heads:(i + 1) * heads] for i in range(count)], axis=0)
    for j in range(tiles):
        pick = iota((heads, 1), 0) == quotient(iota((1, lanes), 1), width) + j * (lanes // width)
        wide = split_dot(totals, jnp.where(pick, 1.0, 0.0).astype(BF16))
        for i in range(count):
            log_ref[i, :, pl.ds(j * lanes, lanes)] = wide[8 * i:8 * i + 8]
    for i in range(count):
        b_rows = b_ref[i].astype(F32)
        push = b_rows[None, :, :] * to_end[i * heads:(i + 1) * heads][:, None, :]
        push_ref[i] = push.reshape(heads * state, positions).astype(BF16)
        for j in range(tiles):
            copies[i, j].wait()
            for g in range(lanes // 256):
                first = j * (lanes // width) + g * group
                cols = pl.ds(j * lanes + g * 256, 256)
                both = jnp.dot(
                    push_ref[i, pl.ds(first * state, group * state), :], held_ref[i, :, cols],
                    preferred_element_type=F32)
                end = jnp.where(lane_head == 0, both[:state], 0.0)
                for k in range(1, group):
                    end = jnp.where(lane_head == k, both[k * state:(k + 1) * state], end)
                end_ref[i, :, cols] = end


def local_ends(x, logdec, bc):
    count, positions, channels = x.shape
    heads, state = logdec.shape[1], bc.shape[2]
    width = channels // heads
    lanes = min(1024, channels)
    whole = pl.BlockSpec(memory_space=pltpu.VMEM)
    return pl.pallas_call(
        functools.partial(ends_kernel, width=width, lanes=lanes),
        in_specs=[pl.BlockSpec(memory_space=pltpu.HBM)] * 3,
        out_specs=[whole] * 3,
        out_shape=[
            jax.ShapeDtypeStruct((count, state, channels), F32),
            jax.ShapeDtypeStruct((count, 8, channels), F32),
            jax.ShapeDtypeStruct(x.shape, BF16),
        ],
        scratch_shapes=[
            pltpu.VMEM(logdec.shape, F32),
            pltpu.VMEM(bc.shape[1:], BF16),
            pltpu.VMEM((count, heads * state, positions), BF16),
            pltpu.SemaphoreType.DMA((count, channels // lanes)),
            pltpu.SemaphoreType.DMA((2,)),
        ],
        compiler_params=pltpu.CompilerParams(vmem_limit_bytes=VMEM_LIMIT),
        cost_estimate=pl.CostEstimate(
            flops=2 * 64 * x.size, bytes_accessed=2 * x.size, transcendentals=0),
        name="local_ends",
    )(in_hbm(x), in_hbm(logdec), in_hbm(bc))


def prepare(parts, logs, lv_ref, lc_ref, state, heads):
    size = logs.shape[1]
    chunks = size // CHUNK
    half = CHUNK // 2
    src, dst = iota((size, 1), 0), iota((1, size), 1)
    middle = quotient(dst, CHUNK) * CHUNK + half - 1
    plus = (src > middle) & (src <= dst)
    minus = (src > dst) & (src <= middle)
    offset = exact_dot(logs, jnp.where(plus, 1.0, jnp.where(minus, -1.0, 0.0)))
    row_scale = jnp.exp(offset)
    in_scale = jnp.exp(-offset) * gain_of(logs)
    span = iota((1, 128), 1) == quotient(src + half, CHUNK)
    steps = jnp.exp(exact_dot(logs, jnp.where(span, 1.0, 0.0)))
    rows = state * chunks
    mine = quotient(iota((rows, 1), 0), state) == quotient(dst, CHUNK)
    keep = (dst <= src) & (quotient(dst, CHUNK) == quotient(src, CHUNK))
    for i, (b_rows, c_rows) in enumerate(parts):
        b_all = jnp.concatenate([b_rows.astype(F32)] * chunks, axis=0)
        lv_ref[i, pl.ds(0, rows), :] = jnp.where(mine, b_all, 0.0).astype(BF16)
        scores = lax.dot_general(c_rows, b_rows, (((0,), (0,)), ((), ())), preferred_element_type=F32)
        lv_ref[i, pl.ds(rows, size), :] = jnp.where(keep, scores, 0.0).astype(BF16)
        c_all = jnp.concatenate([c_rows.astype(F32)] * chunks, axis=0)
        lc_ref[i] = jnp.where(mine, c_all, 0.0).T.astype(BF16)
    scales = []
    for first in range(0, logs.shape[0], heads):
        here = slice(first, first + heads)
        columns = [hi_lo(in_scale[here]).T, hi_lo(steps[here]).T[:16], hi_lo(row_scale[here]).T]
        scales.append(jnp.concatenate(columns, axis=0).astype(BF16))
    return scales


def cuts_of(ld_ref):
    count, _, positions = ld_ref.shape
    return [(i, pl.ds(b * BLOCK, BLOCK)) for i in range(count) for b in range(positions // BLOCK)]


def prepare_hot(hot_ref, heads, width):
    row_head = remainder(iota((2 * heads, 1), 0), heads)
    for g in range(hot_ref.shape[1] // 256):
        lane_head = quotient(iota((1, 256), 1), width) + g * (256 // width)
        hot_ref[:, pl.ds(g * 256, 256)] = jnp.where(row_head == lane_head, 1.0, 0.0).astype(BF16)


def blocks_of(ld_ref, bc_ref):
    cuts = cuts_of(ld_ref)
    logs = jnp.concatenate([ld_ref[i, :, cut] for i, cut in cuts], axis=0)
    return cuts, logs, [(bc_ref[0, i, :, cut], bc_ref[1, i, :, cut]) for i, cut in cuts]


def prompt_prepare_kernel(ld_ref, bc_ref, w_ref, lv_ref, lc_ref):
    _, logs, parts = blocks_of(ld_ref, bc_ref)
    for k, w in enumerate(prepare(parts, logs, lv_ref, lc_ref, bc_ref.shape[2], ld_ref.shape[1] // 2)):
        w_ref[k // 2, k % 2] = w


def branch_prepare_kernel(prompt_ref, ld_ref, bc_ref, hot_ref, w_ref, lv_ref, lc_ref, row_ref, *, width):
    row_ref[...] = jnp.full(row_ref.shape, prompt_ref[0], jnp.int32).astype(F32)
    heads, state = ld_ref.shape[1], bc_ref.shape[2]
    _, logs, parts = blocks_of(ld_ref, bc_ref)
    for k, w in enumerate(prepare(parts, logs, lv_ref, lc_ref, state, heads)):
        w_ref[k] = w
    prepare_hot(hot_ref, heads, width)


def branch_reach_kernel(ld_ref, bc_ref, reach_ref):
    heads, state = ld_ref.shape[1], bc_ref.shape[2]
    blocks = ld_ref.shape[2] // BLOCK
    cuts, logs, parts = blocks_of(ld_ref, bc_ref)
    upto = jnp.where(iota((BLOCK, 1), 0) <= iota((1, BLOCK), 1), 1.0, 0.0)
    runs = exact_dot(logs, upto)
    for k, (i, cut) in enumerate(cuts):
        run = runs[k * heads:(k + 1) * heads]
        if k % blocks:
            run = run + entered
        entered = run[:, BLOCK - 1:BLOCK]
        reach = parts[k][1].astype(F32)[None, :, :] * jnp.exp(run)[:, None, :]
        reach_ref[i, cut, :] = reach.reshape(heads * state, BLOCK).T.astype(BF16)


def prepare_call(kernel, shapes, name, *args):
    whole = pl.BlockSpec(memory_space=pltpu.VMEM)
    scalars = [pl.BlockSpec(memory_space=pltpu.SMEM)] * (len(args) - 2)
    return pl.pallas_call(
        kernel,
        in_specs=scalars + [whole] * 2,
        out_specs=[whole] * len(shapes),
        out_shape=[jax.ShapeDtypeStruct(*shape) for shape in shapes],
        compiler_params=pltpu.CompilerParams(vmem_limit_bytes=VMEM_LIMIT),
        cost_estimate=pl.CostEstimate(flops=10**8, bytes_accessed=10**6, transcendentals=0),
        name=name,
    )(*args)


def prepare_prompts(logdec, bc):
    count, heads, positions = logdec.shape
    cuts, rows = count * (positions // BLOCK), BLOCK // CHUNK * bc.shape[2]
    shapes = [(cuts, 2, 2 * BLOCK + 16, heads), (cuts, rows + BLOCK, BLOCK), (cuts, BLOCK, rows)]
    shapes = [(shape, BF16) for shape in shapes]
    return prepare_call(prompt_prepare_kernel, shapes, "prompt_prepare", logdec, bc)


def prepare_branches(prompt, logdec, bc, channels):
    count, heads, positions = logdec.shape
    cuts, rows = count * (positions // BLOCK), BLOCK // CHUNK * bc.shape[2]
    shapes = [
        ((2 * heads, channels), BF16),
        ((cuts, 2 * BLOCK + 16, 2 * heads), BF16),
        ((cuts, rows + BLOCK, BLOCK), BF16),
        ((cuts, BLOCK, rows), BF16),
        ((1, channels), F32),
    ]
    kernel = functools.partial(branch_prepare_kernel, width=channels // heads)
    out = prepare_call(kernel, shapes, "branch_prepare", prompt, logdec, bc)
    return out[:4], out[4]


def branch_reach(logdec, bc):
    count, heads, positions = logdec.shape
    shapes = [((count, positions, heads * bc.shape[2]), BF16)]
    return prepare_call(branch_reach_kernel, shapes, "branch_reach", logdec, bc)[0]


def run_tiles(jobs):
    scaled, passed = {}, {}
    for g in range(len(jobs) + 2):
        if g < len(jobs):
            scaled[g] = jobs[g][0]()
        if 0 <= g - 1 < len(jobs):
            passed[g - 1] = jobs[g - 1][1](scaled.pop(g - 1))
        if 0 <= g - 2:
            jobs[g - 2][2](passed.pop(g - 2))


def tile_job(ready_refs, at, g, x_of, entering_of, leave, write):
    hot_ref, w_ref, lv_ref, lc_ref = ready_refs
    w_at, at = at
    rows = lc_ref.shape[2]
    chunks = BLOCK // CHUNK
    state = rows // chunks

    def scale():
        wide = jnp.dot(w_ref[w_at], hot_ref[:, pl.ds(g * 256, 256)], preferred_element_type=F32)
        scaled = (x_of().astype(F32) * wide[:BLOCK]).astype(BF16)
        return scaled, wide[BLOCK:BLOCK + 16], wide[BLOCK + 16:]

    def pass_on(given):
        scaled, steps, out_scale = given
        both = jnp.dot(lv_ref[at], scaled, preferred_element_type=F32)
        carries, carry = [], steps[0:1] * entering_of()
        for c in range(chunks):
            carries.append(carry.astype(BF16))
            carry = steps[c + 1:c + 2] * (carry + both[c * state:(c + 1) * state])
        leave(carry)
        return both[rows:], jnp.concatenate(carries, axis=0), out_scale

    def give(given):
        inner, carries, out_scale = given
        carried = jnp.dot(lc_ref[at], carries, preferred_element_type=F32)
        write((inner + carried) * out_scale)

    return scale, pass_on, give


class Copies:
    def __init__(self, sems):
        self.sems, self.started = sems, {}

    def start(self, key, source, target):
        copy = pltpu.make_async_copy(source, target, self.sems.at[key])
        copy.start()
        self.started[key] = copy

    def wait(self, key):
        self.started.pop(key).wait()

    def wait_all(self):
        for key in list(self.started):
            self.wait(key)


def branch_kernel(x_in, *refs, which):
    ready = refs[:4]
    own_ref, x_ref, s_ref, in_sems = refs[4:]
    positions, channels = x_ref.shape
    state = s_ref.shape[0]
    blocks = positions // BLOCK
    lanes = channels // in_sems.shape[1]
    came = Copies(in_sems)
    for b in range(blocks):
        for j in range(channels // lanes):
            spot = (pl.ds(b * BLOCK, BLOCK), pl.ds(j * lanes, lanes))
            came.start((b, j), x_in.at[(which, *spot)], x_ref.at[spot])

    def job(b, g):
        cols = pl.ds(g * 256, 256)
        here = (pl.ds(b * BLOCK, BLOCK), cols)

        def x_of():
            if g * 256 % lanes == 0:
                came.wait((b, g * 256 // lanes))
            return x_ref[here]

        def leave(carry):
            if b < blocks - 1:
                s_ref[:, cols] = carry

        def write(out):
            own_ref[here] = out

        def entering_of():
            return s_ref[:, cols] if b else jnp.zeros((state, 256), F32)

        at = which * blocks + b
        return tile_job(ready, (at, at), g, x_of, entering_of, leave, write)

    run_tiles([job(b, g) for b in range(blocks) for g in range(channels // 256)])


def branch_own(x, ready, which):
    _, positions, channels = x.shape
    state = ready[3].shape[2] * CHUNK // BLOCK
    whole = pl.BlockSpec(memory_space=pltpu.VMEM)
    work = positions * channels
    return pl.pallas_call(
        functools.partial(branch_kernel, which=which),
        in_specs=[pl.BlockSpec(memory_space=pltpu.HBM)] + [whole] * 4,
        out_specs=whole,
        out_shape=jax.ShapeDtypeStruct(x.shape[1:], F32),
        scratch_shapes=[
            pltpu.VMEM((positions, channels), BF16),
            pltpu.VMEM((state, channels), F32),
            pltpu.SemaphoreType.DMA((positions // BLOCK, channels // min(512, channels))),
        ],
        compiler_params=pltpu.CompilerParams(vmem_limit_bytes=VMEM_LIMIT),
        cost_estimate=pl.CostEstimate(
            flops=2 * 1152 * work, bytes_accessed=4 * work, transcendentals=0),
        name="branch_own",
    )(in_hbm(x), *ready)


def prompt_kernel(*refs, skip):
    half_ref, x_ref, *ready, start_ref = refs[:7]
    y_out, y_ref, sems = refs[7 + skip:]
    count, positions, channels = y_ref.shape
    blocks = positions // BLOCK
    half = half_ref[0]
    left = Copies(sems)
    entered = {}

    def job(i, b, g):
        rows = pl.ds(b * BLOCK, BLOCK)
        here = (i, rows, pl.ds(g * 256, 256))
        there = (i, rows, pl.ds(pl.multiple_of(half * channels + g * 256, 256), 256))

        def leave(carry):
            entered[i, g] = carry

        def entering_of():
            return entered[i, g] if b else start_ref[i, :, pl.ds(g * 256, 256)]

        def write(out):
            y_ref[here] = out.astype(BF16)
            left.start((i, b, g), y_ref.at[here], y_out.at[there])

        at = i * blocks + b
        return tile_job(ready, ((at, half), at), g, lambda: x_ref[there], entering_of, leave, write)

    run_tiles([job(i, b, g) for i in range(count) for b in range(blocks) for g in range(channels // 256)])
    left.wait_all()


def prompt_half(half, x, ready, start, into):
    count, positions, channels = x.shape
    part = channels // 2
    whole = pl.BlockSpec(memory_space=pltpu.VMEM)
    hbm = pl.BlockSpec(memory_space=pltpu.HBM)
    work = count * positions * part
    return pl.pallas_call(
        functools.partial(prompt_kernel, skip=len(into)),
        in_specs=[pl.BlockSpec(memory_space=pltpu.SMEM)] + [whole] * 6 + [hbm] * len(into),
        out_specs=hbm,
        out_shape=jax.ShapeDtypeStruct(x.shape, BF16),
        scratch_shapes=[
            pltpu.VMEM((count, positions, part), BF16),
            pltpu.SemaphoreType.DMA((count, positions // BLOCK, part // 256)),
        ],
        input_output_aliases={7 + i: i for i in range(len(into))},
        compiler_params=pltpu.CompilerParams(vmem_limit_bytes=VMEM_LIMIT),
        cost_estimate=pl.CostEstimate(
            flops=2 * 1152 * work, bytes_accessed=4 * work, transcendentals=0),
        name="prompt_half",
    )(half, x, *ready, start, *into)


def finish_kernel(len_ref, reach_ref, start_ref, *refs, width):
    own_refs, (y_out, y_ref, sems) = refs[:-3], refs[-3:]
    count, positions, channels = y_ref.shape
    state = start_ref.shape[0]
    group = 128 // state
    span = group * width
    left = Copies(sems)
    own_head = quotient(iota((128, 1), 0), state) == quotient(iota((1, span), 1), width)
    for g in range(channels // span):
        cols = pl.ds(g * span, span)
        start = jnp.concatenate([start_ref[:, cols]] * group, axis=0)
        start = jnp.where(own_head, start, 0.0).astype(BF16)
        for i in range(count):
            for b in range(positions // BLOCK):
                rows = pl.ds(b * BLOCK, BLOCK)
                term = jnp.dot(
                    reach_ref[i, rows, pl.ds(g * 128, 128)], start, preferred_element_type=F32)
                live = iota((BLOCK, span), 0) < len_ref[i] - b * BLOCK
                y_ref[i, rows, cols] = jnp.where(live, own_refs[i][rows, cols] + term, 0.0).astype(BF16)
                left.start((i, b, g), y_ref.at[i, rows, cols], y_out.at[i, rows, cols])
    left.wait_all()


def finish(lengths, reach, start, own):
    count, (positions, channels) = len(own), own[0].shape
    state = start.shape[0]
    width = channels * state // reach.shape[2]
    whole = pl.BlockSpec(memory_space=pltpu.VMEM)
    return pl.pallas_call(
        functools.partial(finish_kernel, width=width),
        in_specs=[pl.BlockSpec(memory_space=pltpu.SMEM)] + [whole] * (2 + count),
        out_specs=pl.BlockSpec(memory_space=pltpu.HBM),
        out_shape=jax.ShapeDtypeStruct((count, positions, channels), BF16),
        scratch_shapes=[
            pltpu.VMEM((count, positions, channels), BF16),
            pltpu.SemaphoreType.DMA((count, positions // BLOCK, reach.shape[2] // 128)),
        ],
        compiler_params=pltpu.CompilerParams(vmem_limit_bytes=VMEM_LIMIT),
        cost_estimate=pl.CostEstimate(
            flops=2**28, bytes_accessed=2**23, transcendentals=0),
        name="branch_finish",
    )(lengths, reach, start, *own)


def swap_bit(values, bit, size):
    links = [(k, k ^ bit) for k in range(size)]
    return jax.tree.map(lambda value: lax.ppermute(value, "ctx", links), values)


def in_order(upper, mine, other):
    first = [jnp.where(upper, o, m) for m, o in zip(mine, other)]
    second = [jnp.where(upper, m, o) for m, o in zip(mine, other)]
    return first, second


def join(first, second):
    return jnp.exp(second[1]) * first[0] + second[0], first[1] + second[1]


def spread_step(value, hop, ctx_size, pair_size):
    known = [m for m in range(pair_size) if m & (2 * hop - 1) == 0]
    links = []
    for k in range(ctx_size):
        z = k * pair_size // ctx_size
        links += [(k * pair_size + (z ^ m), k * pair_size + (z ^ m ^ hop)) for m in known]
    return lax.ppermute(value, ("ctx", "pair"), links)


def halvings(size):
    return [size >> k for k in range(1, size.bit_length())]


def places():
    size, pair_size = lax.axis_size("ctx"), lax.axis_size("pair")
    ctx, pair = lax.axis_index("ctx"), lax.axis_index("pair")
    away = pair ^ lax.div(ctx * pair_size, size)
    odd = ctx & 1
    return {
        "odd": odd == 1,
        "half": jnp.reshape(odd, (1,)),
        "other_half": jnp.reshape(1 - odd, (1,)),
        "upper": {bit: (ctx & bit) != 0 for bit in halvings(size)[:-1]},
        "has": {hop: (away & (2 * hop - 1)) == 0 for hop in halvings(pair_size)},
    }


def body(
    prompt_x,
    prompt_bc,
    prompt_logdec,
    branch_x,
    branch_bc,
    branch_logdec,
    branch_prompt,
    branch_len,
):
    size, pair_size = lax.axis_size("ctx"), lax.axis_size("pair")
    branches = branch_x.shape[0]
    assert size == 2 * pair_size and size & (size - 1) == 0 and branch_prompt.shape[0] == 1
    place, prompt_logdec = lax.optimization_barrier((places(), prompt_logdec))
    odd = place["odd"]

    def beside(exchange, value, work, *given):
        value, given = lax.optimization_barrier((value, given))
        got = exchange(value)
        return lax.optimization_barrier((got, work(*given)))

    end, log, held = local_ends(prompt_x, prompt_logdec, prompt_bc)
    half = end.shape[2] // 2
    low, high = (end[:, :, :half], log[:, :1, :half]), (end[:, :, half:], log[:, :1, half:])
    keep = [jnp.where(odd, h, l) for l, h in zip(low, high)]
    send = [jnp.where(odd, l, h) for l, h in zip(low, high)]
    got, (ready, row) = beside(
        lambda v: swap_bit(v, 1, size),
        send,
        lambda logdec: prepare_branches(branch_prompt, logdec, branch_bc, branch_x.shape[2]),
        branch_logdec,
    )
    first, second = in_order(odd, keep, got)
    total, total_log = join(first, second)
    before, before_log = jnp.zeros_like(total), jnp.zeros_like(total_log)

    def chosen(total, row):
        out = total[0]
        for which in range(1, total.shape[0]):
            out = jnp.where(row == which, total[which], out)
        return out

    def part(which):
        def work(x, prompt_logdec, branch_logdec):
            own = branch_own(x, ready, which)
            return (
                own,
                branch_reach(branch_logdec, branch_bc) if which == 0 else None,
                prepare_prompts(prompt_logdec, prompt_bc) if which == branches - 1 else None,
            )

        return work

    done = []
    bit = 2
    while bit < size:
        swap = functools.partial(swap_bit, bit=bit, size=size)
        if not done:
            def with_row(values):
                return swap(values[:2]), lax.ppermute(values[2], "pair", [(z, z ^ 1) for z in range(pair_size)])

            (other, next_row), out = beside(
                with_row, (total, total_log, row), part(0), branch_x, prompt_logdec, branch_logdec)
            done.append(out)
        elif len(done) < branches:
            other, out = beside(
                swap, (total, total_log), part(len(done)), branch_x, prompt_logdec, branch_logdec)
            done.append(out)
        else:
            other = swap((total, total_log))
        upper = place["upper"][bit]
        before = jnp.where(upper, jnp.exp(before_log) * other[0] + before, before)
        before_log = jnp.where(upper, before_log + other[1], before_log)
        total, total_log = join(*in_order(upper, (total, total_log), other))
        bit *= 2
    while len(done) < branches:
        done.append(part(len(done))(branch_x, prompt_logdec, branch_logdec))
    own = [out[0] for out in done]
    reach, prompt_ready = done[0][1], (ready[0], *done[-1][2])

    next_before = jnp.exp(first[1]) * before + first[0]
    keep = jnp.where(odd, next_before, before)
    others = swap_bit(jnp.where(odd, before, next_before), 1, size)
    sides = [(place["half"], keep), (place["other_half"], others)]
    prompt_y = ()
    for hop in halvings(pair_size):
        step = functools.partial(spread_step, hop=hop, ctx_size=size, pair_size=pair_size)
        value = total if hop > 1 else chosen(total, next_row)
        if sides:
            side, entering = sides.pop(0)
            got, prompt_y = beside(
                step, value,
                lambda entering, y: (prompt_half(side, held, prompt_ready, entering, y),), entering, prompt_y)
        else:
            got = step(value)
        if hop > 1:
            total = jnp.where(place["has"][hop], total, got)
    for side, entering in sides:
        prompt_y = (prompt_half(side, held, prompt_ready, entering, prompt_y),)
    start = jnp.where(place["has"][1], chosen(total, row), got)
    branch_y = finish(branch_len, reach, start, own)
    return prompt_y[0], branch_y


def solution(mesh):
    return jax.shard_map(
        body,
        mesh=mesh,
        in_specs=(
            P(None, "ctx", "pair"),
            P(None, None, None, "ctx"),
            P(None, "pair", "ctx"),
            P("pair", None, "ctx"),
            P(None, "pair", None, None),
            P("pair", "ctx", None),
            P("pair"),
            P("pair"),
        ),
        out_specs=(P(None, "ctx", "pair"), P("pair", None, "ctx")),
        check_vma=False,
    )
```
